256 devices in a mesh: dp: 32 (over z, x), row: 2 (over core), col: 4 (over y).
Axes of the slice: x: 4, y: 4, z: 8, core: 2. Of those that a mesh axis runs over, the one named last changes fastest.
Arguments:
- tokens: bfloat16 [5120, 3584], P('dp'), may hold values from -6 to 6
- routes: int32 [5120, 8], P(('dp', 'col')), may hold values from 0 to 127, all different within a row; in each aligned block of 40 rows (0 to 39, 40 to 79, ...) at most 3 rows name the same one
- route_weights: float32 [5120, 8], P(('dp', 'col')), may hold values from 0.05 to 0.6
- teacher_in: bfloat16 [128, 2, 3584, 1024], P(('dp', 'col'), None, None, 'row'), may hold values from -0.09375 to 0.09375
- teacher_out: bfloat16 [128, 1024, 3584], P(('dp', 'col'), 'row'), may hold values from -0.1875 to 0.1875
- student_in: bfloat16 [2, 3584, 9216], P(None, 'dp', ('row', 'col')), may hold values from -0.09375 to 0.09375
- student_out: bfloat16 [9216, 3584], P(('row', 'col'), 'dp'), may hold values from -0.0625 to 0.0625
Outputs:
- token_loss: float32 [5120], P('dp')
- grad_down: float32 [9216, 3584], P(('row', 'col'), 'dp')
The draws below stay inside these ranges and needn't reach their ends.
Inputs may be any that keep to these rules, and one draw needn't show every extreme that they name: `routes`: each token names 8 different experts; in each block of 40 consecutive tokens (the tokens of one index of dp and col) no expert is named more than 3 times, a bound that some block reaches.
All inputs are finite; a program needn't handle non-finite values.
Results may differ from the reference program's by a relative error of at most 0.02.
Values may be sent and summed in bfloat16 or wider, within the bound.
A program may use at most 128 MiB of HBM per device.

```python
import math
import jax
import jax.numpy as jnp
import numpy as np
from jax import lax

D = 3584
H = 1024
FF = 9216
TOP = 8
TOK_DEV = 160
TOKENS = 5120
EXPERTS = 128
CAP = 3
N_DP = 32
N_ROW = 2
N_COL = 4


def shard_levels(rng, extent, split, least, high):
    def one(axis_at, shards_of):
        draws = jax.random.uniform(jax.random.fold_in(jax.random.fold_in(rng, 6), axis_at), (shards_of,), jnp.float32, least / len(split), high / len(split))
        return jnp.repeat(jnp.exp(draws), extent[axis_at] // shards_of).reshape((-1,) + (1,) * (len(extent) - axis_at - 1))

    factor_of = one(*split[0])
    for cut in split[1:]:
        factor_of = factor_of * one(*cut)
    return factor_of


def shared_out(stream_key, own, number, rows, number_of, top, most, slope):
    ranking = jax.random.permutation(stream_key, number_of)
    heavy_load, ordinary = load_shares(number_of, rows * top, most, slope, True), load_shares(number_of, rows * top, most, slope, False)
    places = jnp.arange(number_of)

    def named(sizes, offset_by):
        used = int((sizes > 0).sum())
        fixed = max(1, used // 4)
        passed = fixed + (places - fixed + offset_by * (used - fixed)) % max(1, number_of - fixed)
        return jnp.zeros((number_of,), jnp.int32).at[ranking[jnp.where(places < fixed, places, passed)]].set(jnp.asarray(sizes, jnp.int32))

    sizes = jnp.where(number % 4 == 0, named(heavy_load, number // 4), named(ordinary, number - number // 4 - 1))
    mixed = jax.random.permutation(jax.random.fold_in(own, 3), number_of)
    source_of, sink = mixed[0:number_of // 2 * 2:2], mixed[1:number_of // 2 * 2:2]
    margin = jnp.minimum(sizes[source_of] - 1, most - sizes[sink]) // 2
    margin = jnp.where((source_of == ranking[0]) | (sink == ranking[0]) | (sizes[sink] == 0), 0, jnp.maximum(margin, 0))
    passed = jax.random.randint(jax.random.fold_in(own, 4), (number_of // 2,), 0, 1 << 20) % (margin + 1)
    sizes = sizes.at[source_of].add(-passed).at[sink].add(passed)
    labels = jnp.searchsorted(jnp.cumsum(sizes), jnp.arange(rows * top), side="right").astype(jnp.int32)
    grid = labels.reshape(top, rows).T
    grid = grid[jax.random.permutation(jax.random.fold_in(own, 1), rows)]
    offset_by = jax.random.randint(jax.random.fold_in(own, 2), (rows, 1), 0, top)
    return jnp.take_along_axis(grid, (jnp.arange(top)[None, :] + offset_by) % top, axis=1)


def load_shares(number_of, total, reach, skew, full):
    portions = [(1 << 20) // math.isqrt(grade ** skew) + 1 for grade in range(1, number_of + 1)]
    largest = reach if full else min(reach, max(-(-total // number_of), total * portions[0] // sum(portions)))
    least = 1 if total - largest >= number_of - 1 else 0
    holding, spare = [largest] + [least] * (number_of - 1), total - largest - least * (number_of - 1)
    while spare > 0:
        movable = [i for i in range(1, number_of) if holding[i] < largest] or [i for i in range(1, number_of) if holding[i] < reach]
        pool, left = sum([portions[i] for i in movable]), spare
        for i in movable:
            more = min(reach - holding[i], max(1, left * portions[i] // pool), spare)
            holding[i] = holding[i] + more
            spare = spare - more
    return np.array(holding)


def centred(own_key, dims, width, most, shards=(), kind=jnp.bfloat16):
    array = jax.random.normal(own_key, dims, jnp.float32) * width
    if len(shards) > 0:
        array = shard_levels(own_key, dims, shards, -0.22, 0.18) * array
    return jnp.clip(array, min=-most, max=most).astype(kind)


def setup_inputs(seed: int = 0) -> dict:
    keys = jax.random.split(jax.random.key(seed), 8)
    tokens = centred(keys[0], (TOKENS, D), 1.0, 6.0, ((0, 32),))
    routes_keys = jax.random.split(jax.random.fold_in(keys[1], 1), TOKENS // (TOK_DEV // N_COL))
    routes_turns = jax.random.permutation(jax.random.fold_in(keys[1], 3), TOKENS // (TOK_DEV // N_COL))
    routes = jax.vmap(lambda own, number: shared_out(jax.random.fold_in(keys[1], 2), own, number, TOK_DEV // N_COL, EXPERTS, TOP, CAP, 2))(routes_keys, routes_turns).reshape((TOKENS, TOP))
    route_weights = jnp.clip(jnp.exp(math.log(0.6) - 2.4849067 * jax.random.uniform(keys[2], (TOKENS, TOP), jnp.float32) ** shard_levels(keys[2], (TOKENS, TOP), ((0, 128),), -0.2, 0.2)), 0.05, 0.6)
    teacher_in = centred(keys[3], (EXPERTS, 2, D, H), D ** -0.5, 0.09375, ((0, 128), (3, 2)))
    teacher_out = centred(keys[4], (EXPERTS, H, D), H ** -0.5, 0.1875, ((0, 128), (1, 2)))
    student_in = centred(keys[5], (2, D, FF), D ** -0.5, 0.09375, ((1, 32), (2, 8)))
    student_out = centred(keys[6], (FF, D), FF ** -0.5, 0.0625, ((0, 8), (1, 32)))
    return dict(tokens=tokens, routes=routes, route_weights=route_weights, teacher_in=teacher_in, teacher_out=teacher_out, student_in=student_in, student_out=student_out)


def expert_parts(inputs):
    expert_rows, inner_weight, outer_weight = inputs
    group_width = H // N_ROW
    outputs = []
    for group_index in range(N_ROW):
        offset = group_index * group_width
        gate_part = jnp.dot(expert_rows, inner_weight[0, :, offset:offset + group_width], preferred_element_type=jnp.float32)
        up_part = jnp.dot(expert_rows, inner_weight[1, :, offset:offset + group_width], preferred_element_type=jnp.float32)
        activation = (jax.nn.silu(gate_part) * up_part).astype(jnp.bfloat16)
        outputs.append(jnp.dot(activation, outer_weight[offset:offset + group_width], preferred_element_type=jnp.float32).astype(jnp.bfloat16))
    return jnp.stack(outputs)


def reference(tokens, routes, route_weights, teacher_in, teacher_out, student_in, student_out):
    slot_count = N_DP * N_COL * CAP
    flat_routes = routes.reshape(-1).astype(jnp.int32)
    one_hot = (flat_routes[:, None] == jnp.arange(EXPERTS, dtype=jnp.int32)[None, :]).astype(jnp.int32)
    earlier = jnp.cumsum(one_hot, axis=0) - one_hot
    slot_index = jnp.sum(earlier * one_hot, axis=1)
    position = (flat_routes * slot_count + slot_index).astype(jnp.int32)
    owner_row = jnp.repeat(jnp.arange(TOKENS, dtype=jnp.int32), TOP)
    buffer = jnp.zeros((EXPERTS * slot_count, D), jnp.bfloat16).at[position].set(tokens[owner_row])
    expert_out = lax.map(expert_parts, (buffer.reshape(EXPERTS, slot_count, D), teacher_in, teacher_out))
    expert_out = jnp.transpose(expert_out, (1, 0, 2, 3)).reshape(N_ROW, EXPERTS * slot_count, D)

    def teacher_block(inputs):
        block_position, block_weights = inputs
        teacher_sum = jnp.zeros((TOK_DEV, D), jnp.float32)
        for group_index in range(N_ROW):
            picked = jnp.take(expert_out[group_index], block_position, axis=0).astype(jnp.float32).reshape(TOK_DEV, TOP, D)
            teacher_sum = teacher_sum + jnp.sum(block_weights[:, :, None] * picked, axis=1)
        return teacher_sum

    teacher_y = lax.map(teacher_block, (position.reshape(N_DP, TOK_DEV * TOP), route_weights.reshape(N_DP, TOK_DEV, TOP))).reshape(TOKENS, D)
    gate_full = jnp.dot(tokens, student_in[0], preferred_element_type=jnp.float32)
    up_full = jnp.dot(tokens, student_in[1], preferred_element_type=jnp.float32)
    hidden = (jax.nn.silu(gate_full) * up_full).astype(jnp.bfloat16)
    student_y = jnp.dot(hidden, student_out, preferred_element_type=jnp.float32)
    gap_full = student_y - teacher_y
    token_loss = jnp.mean(gap_full * gap_full, axis=1)
    gap_round = gap_full.astype(jnp.bfloat16)

    def add_group(running, inputs):
        group_hidden, group_gap = inputs
        group_term = lax.dot_general(group_hidden, group_gap, (((0,), (0,)), ((), ())), preferred_element_type=jnp.float32) / TOK_DEV
        group_term = lax.optimization_barrier(group_term.astype(jnp.bfloat16)).astype(jnp.float32)
        return running + group_term, None

    grad_down, _ = lax.scan(add_group, jnp.zeros((FF, D), jnp.float32), (hidden.reshape(N_DP, TOK_DEV, FF), gap_round.reshape(N_DP, TOK_DEV, D)))
    return token_loss, grad_down
```

```python
import jax
import jax.numpy as jnp
from jax import lax
from jax.sharding import Mesh, PartitionSpec as P

NX = 4
F32 = jnp.float32
BF = jnp.bfloat16


def split_mesh(mesh):
    dp, row, col = mesh.devices.shape
    return Mesh(mesh.devices.reshape(dp // NX, NX, row, col), ("z", "x", "row", "col"))


def dot(a, b, dims):
    return lax.dot_general(a, b, (dims, ((), ())), preferred_element_type=F32)


def pad_lanes(a):
    lanes = a.shape[-1]
    wide = -(-lanes // 128) * 128
    return jnp.pad(a, [(0, 0)] * (a.ndim - 1) + [(0, wide - lanes)])


def routing(routes, weights, plane, ny, cap):
    nz, block, _ = routes.shape
    experts = NX * ny
    local = routes - plane * experts
    ids = jnp.arange(experts, dtype=jnp.int32)
    hit = local[..., None] == ids
    named = jnp.any(hit, axis=2)
    weight = jnp.sum(jnp.where(hit, weights[..., None], 0.0), axis=2)
    count = named.astype(jnp.int32)
    slot = jnp.cumsum(count, axis=1) - count
    place = named[..., None] & (slot[..., None] == jnp.arange(cap, dtype=jnp.int32))
    same = jnp.eye(nz, dtype=bool)
    full = place[:, :, :, None, :] & same[:, None, None, :, None]
    combine = jnp.where(full, weight[:, :, :, None, None], 0.0)
    rows = experts * nz * cap
    return full.reshape(nz * block, rows).astype(BF), combine.reshape(nz * block, rows)


def on_device(tokens, routes, route_weights, teacher_in, teacher_out, student_in, student_out):
    nz, nr, ny = lax.axis_size("z"), lax.axis_size("row"), lax.axis_size("col")
    z, x, r, y = (lax.axis_index(a) for a in ("z", "x", "row", "col"))
    tok, width = tokens.shape
    block, top = routes.shape
    blk = student_in.shape[1]
    ff = student_in.shape[2]
    sub = ff // NX
    half = width // nr
    plane_experts = NX * ny
    cap = max(2, 3 * block * top // (2 * nz * plane_experts))
    blocks = nz * NX

    parts = jnp.concatenate([jnp.swapaxes(student_in, 1, 2), student_out[None]], axis=0)
    parts = pad_lanes(parts)
    lanes = parts.shape[-1]
    wide = blocks * lanes
    parts = lax.all_to_all(parts.reshape(3, NX, sub, lanes), "x", split_axis=1, concat_axis=1, tiled=True)
    parts = jnp.swapaxes(parts, 1, 2).reshape(3, sub, NX * lanes)
    inner = lax.all_gather(parts[:2], "z", axis=2, tiled=True)
    outer = lax.all_gather(parts[2], "z", axis=1, tiled=True)

    padded = pad_lanes(tokens.reshape(tok, blocks, blk)).reshape(tok, wide)
    plane_tokens = lax.all_gather(padded, "x", axis=0, tiled=True)

    mine = lax.dynamic_slice(tokens, (y * block, r * half), (block, half))
    column = lax.all_gather(mine, "z", axis=0, tiled=True)
    routes_z = lax.all_gather(routes, "z")
    weights_z = lax.all_gather(route_weights, "z")
    place, combine = routing(routes_z, weights_z, z, ny, cap)
    slots = nz * cap
    outgoing = dot(place, column, ((0,), (0,))).astype(BF).reshape(plane_experts, slots, half)
    arrived = lax.all_to_all(outgoing, ("x", "col"), split_axis=0, concat_axis=0, tiled=True)
    arrived = lax.all_gather(arrived.reshape(plane_experts * slots, half), "row", axis=1, tiled=True)
    gate = dot(arrived, teacher_in[0, 0], ((1,), (0,)))
    up = dot(arrived, teacher_in[0, 1], ((1,), (0,)))
    act = (jax.nn.silu(gate) * up).astype(BF)
    part = dot(act, teacher_out[0], ((1,), (0,))).astype(BF)
    both = lax.all_to_all(part.reshape(-1, nr, half), "row", split_axis=1, concat_axis=1, tiled=True)
    summed = jnp.sum(both.astype(F32), axis=1).astype(BF).reshape(plane_experts, slots, half)
    back = lax.all_to_all(summed, ("x", "col"), split_axis=0, concat_axis=0, tiled=True)
    back = back.reshape(plane_experts * slots, half)
    high = combine.astype(BF)
    low = (combine - high.astype(F32)).astype(BF)
    teacher = dot(high, back, ((1,), (0,))) + dot(low, back, ((1,), (0,)))
    teacher = lax.psum_scatter(teacher.astype(BF).reshape(nz, block, half), "z", scatter_dimension=0, tiled=False)
    teacher = pad_lanes(teacher.reshape(block, blocks // nr, blk)).reshape(block, wide // nr)

    gate = dot(plane_tokens, inner[0], ((1,), (1,)))
    up = dot(plane_tokens, inner[1], ((1,), (1,)))
    hidden = (jax.nn.silu(gate) * up).astype(BF)
    hidden_both = lax.all_gather(hidden, "row", axis=1, tiled=True)
    outer_both = lax.all_to_all(outer.reshape(sub, nr, wide // nr), "row", split_axis=1, concat_axis=0, tiled=True)
    outer_both = outer_both.reshape(nr * sub, wide // nr)
    y_part = dot(hidden_both, outer_both, ((1,), (0,))).astype(BF)
    student = lax.all_to_all(y_part.reshape(plane_experts, block, -1), ("x", "col"), split_axis=0, concat_axis=0, tiled=True)
    student = jnp.sum(student.astype(F32), axis=0)
    gap = student - teacher.astype(F32)
    loss = lax.psum(jnp.sum(gap * gap, axis=1), "row") / width
    token_loss = lax.all_gather(loss, "col", axis=0, tiled=True)
    gap_round = lax.all_gather(gap.astype(BF), ("x", "col"), axis=0, tiled=True)
    term = (dot(hidden_both, gap_round, ((0,), (0,))) / tok).astype(BF)
    term = lax.all_to_all(term.reshape(nr, sub, wide // nr), "row", split_axis=0, concat_axis=2, tiled=True)
    term = term.reshape(sub, nz, NX * lanes).swapaxes(0, 1)
    grad = lax.psum_scatter(term, "z", scatter_dimension=0, tiled=False)
    grad = grad.reshape(sub, NX, lanes)
    grad = lax.all_to_all(grad, "x", split_axis=1, concat_axis=0, tiled=True)
    grad = grad.reshape(ff, lanes)[:, :blk].astype(F32)
    return token_loss, grad


def solution(mesh):
    dp = ("z", "x")
    in_specs = (
        P(dp, None),
        P(dp + ("col",), None),
        P(dp + ("col",), None),
        P(dp + ("col",), None, None, "row"),
        P(dp + ("col",), "row", None),
        P(None, dp, ("row", "col")),
        P(("row", "col"), dp),
    )
    out_specs = (P(dp), P(("row", "col"), dp))
    return jax.shard_map(
        on_device, mesh=split_mesh(mesh), in_specs=in_specs, out_specs=out_specs, check_vma=False
    )
```

```python
import functools

import jax
import jax.numpy as jnp
from jax import lax
from jax.experimental import pallas as pl
from jax.experimental.pallas import tpu as pltpu
from jax.sharding import Mesh, PartitionSpec as P

NX = 4
MESH = pl.DeviceIdType.MESH
F32 = jnp.float32
BF = jnp.bfloat16


def split_mesh(mesh):
    dp, row, col = mesh.devices.shape
    return Mesh(mesh.devices.reshape(dp // NX, NX, row, col), ("z", "x", "row", "col"))


def dot(a, b, dims):
    return lax.dot_general(a, b, (dims, ((), ())), preferred_element_type=F32)


def pad_lanes(a):
    lanes = a.shape[-1]
    wide = -(-lanes // 128) * 128
    return jnp.pad(a, [(0, 0)] * (a.ndim - 1) + [(0, wide - lanes)])


def here():
    return tuple(lax.axis_index(a) for a in ("z", "x", "row", "col"))


def remote(src, dst, send, recv, device):
    return pltpu.make_async_remote_copy(
        src_ref=src, dst_ref=dst, send_sem=send, recv_sem=recv, device_id=device, device_id_type=MESH
    )


def greet(devices):
    barrier = pltpu.get_barrier_semaphore()
    for device in devices:
        pl.semaphore_signal(barrier, inc=1, device_id=device, device_id_type=MESH)
    pl.semaphore_wait(barrier, len(devices))


def lanes_at(start, size):
    return pl.ds(pl.multiple_of(start * size, size), size)


def kernel_call(body, number, outs, scratch, *args):
    whole = pl.BlockSpec(memory_space=pltpu.VMEM)
    return pl.pallas_call(
        body,
        out_shape=outs,
        in_specs=[whole] * len(args),
        out_specs=[whole] * len(outs),
        scratch_shapes=scratch,
        compiler_params=pltpu.CompilerParams(
            collective_id=number, has_side_effects=True, vmem_limit_bytes=48 * 1024 * 1024
        ),
    )(*args)


def dma(*shape):
    return pltpu.SemaphoreType.DMA(shape)


def plane_steps(ny):
    steps = [(dx, dy) for dx in range(NX) for dy in range(ny) if dx or dy]
    far = lambda s: min(s[0], NX - s[0]) + min(s[1], ny - s[1])
    return sorted(steps, key=far, reverse=True)


def weights_kernel(parts, inner, outer, send, recv, own):
    z, x, r, y = here()
    greet([(z, (x + d) % NX, r, y) for d in (1, 2, 3)])
    copies = []
    for d in (2, 1, 3):
        to = (x + d) % NX
        device = (z, to, r, y)
        for kind in (0, 1, 2):
            dst = outer.at[:, lanes_at(x, 128)] if kind == 2 else inner.at[kind, :, lanes_at(x, 128)]
            copies.append(remote(parts.at[kind, to], dst, send.at[d - 1, kind], recv.at[d - 1, kind], device))
            copies[-1].start()
    local = []
    for kind in (0, 1, 2):
        dst = outer.at[:, lanes_at(x, 128)] if kind == 2 else inner.at[kind, :, lanes_at(x, 128)]
        local.append(pltpu.make_async_copy(parts.at[kind, x], dst, own.at[kind]))
        local[-1].start()
    for copy in copies + local:
        copy.wait()


def tokens_kernel(nz, padded, mine, meta, plane, column, metas, xs, xr, ys, yr, cs, cr, zs, zr, ms, mr, own):
    z, x, r, y = here()
    up, down = (z + 1) % nz, (z + nz - 1) % nz
    ny = lax.axis_size("col")
    north, south = (y + 1) % ny, (y + ny - 1) % ny
    sibling = (z, x, 1 - r, y)
    greet(
        [(z, (x + d) % NX, r, y) for d in (1, 2, 3)]
        + [(z, x, r, north), (z, x, r, south), (up, x, r, y), (down, x, r, y), sibling]
    )
    rows, wide = padded.shape
    high, span = rows // 2, wide // 2
    quarter = span // 2
    mine_rows = pl.ds(pl.multiple_of(r * high, high), high)
    parity = y % 2
    held = lanes_at(parity, span)
    started = []

    def go(copy):
        copy.start()
        started.append(copy)
        return copy

    local = [
        pltpu.make_async_copy(padded, plane.at[x], own.at[0]),
        pltpu.make_async_copy(mine, column.at[z], own.at[1]),
        pltpu.make_async_copy(meta, metas.at[z], own.at[2]),
    ]
    for copy in local:
        copy.start()

    def z_step(s):
        half = mine.shape[1] // 2
        a, b = (z + nz - s + 1) % nz, (z + s - 1) % nz
        if s == 1:
            one, two, three, four = mine, mine, meta, meta
        else:
            one, two, three, four = column.at[a], column.at[b], metas.at[a], metas.at[b]
        to_a, to_b = column.at[a], column.at[b]
        if s == nz // 2:
            low, top = pl.ds(0, half), pl.ds(half, half)
            one, to_a, two, to_b = column.at[a, :, low], column.at[a, :, low], column.at[b, :, top], column.at[b, :, top]
        out = [
            go(remote(one, to_a, zs.at[0, s - 1], zr.at[0, s - 1], (up, x, r, y))),
            go(remote(two, to_b, zs.at[1, s - 1], zr.at[1, s - 1], (down, x, r, y))),
            go(remote(three, metas.at[a], ms.at[0, s - 1], mr.at[0, s - 1], (up, x, r, y))),
        ]
        if s < nz // 2:
            out.append(go(remote(four, metas.at[b], ms.at[1, s - 1], mr.at[1, s - 1], (down, x, r, y))))
        return out

    def arrived(copies):
        for copy in copies:
            copy.wait_recv()

    ring = z_step(1)
    from_x = {}
    for d in (2, 1, 3):
        device = (z, (x + d) % NX, r, y)
        from_x[d] = go(remote(padded.at[mine_rows, held], plane.at[x, mine_rows, held], xs.at[d - 1], xr.at[d - 1], device))
    turn = 0
    from_sib, from_y = [], []
    for d in (1, 3, 2):
        arrived(ring)
        turn += 1
        ring = z_step(turn + 1)
        from_x[d].wait_recv()
        source = (x + NX - d) % NX
        for side, device in ((0, (z, x, r, north)), (1, (z, x, r, south))):
            piece = plane.at[source, mine_rows, lanes_at(parity * 2 + side, quarter)]
            from_y.append((d, side, go(remote(piece, piece, ys.at[side, d - 1], yr.at[side, d - 1], device))))
        piece = plane.at[source, mine_rows, held]
        from_sib.append(go(remote(piece, piece, cs.at[0, d - 1], cr.at[0, d - 1], sibling)))
    arrived(ring)
    for d, side, copy in from_y:
        copy.wait_recv()
        source = (x + NX - d) % NX
        piece = plane.at[source, mine_rows, lanes_at((1 - parity) * 2 + side, quarter)]
        from_sib.append(go(remote(piece, piece, cs.at[1 + side, d - 1], cr.at[1 + side, d - 1], sibling)))
    arrived(from_sib)
    for copy in started:
        copy.wait_send()
    for copy in local:
        copy.wait()


def dispatch_kernel(outgoing, got, send, recv, fsend, frecv, own):
    z, x, r, y = here()
    ny = lax.axis_size("col")
    steps = plane_steps(ny)
    sibling = (z, x, 1 - r, y)
    greet([(z, (x + dx) % NX, r, (y + dy) % ny) for dx, dy in steps] + [sibling])
    me = x * ny + y
    mine = lanes_at(r, outgoing.shape[2])
    local = pltpu.make_async_copy(outgoing.at[me], got.at[me, :, mine], own.at[0])
    local.start()
    sends, forwards = [], []
    for k, (dx, dy) in enumerate(steps):
        tx, ty = (x + dx) % NX, (y + dy) % ny
        sends.append(remote(outgoing.at[tx * ny + ty], got.at[me, :, mine], send.at[k], recv.at[k], (z, tx, r, ty)))
        sends[-1].start()
    forwards.append(remote(outgoing.at[me], got.at[me, :, mine], fsend.at[len(steps)], frecv.at[len(steps)], sibling))
    forwards[-1].start()
    for k, (dx, dy) in reversed(list(enumerate(steps))):
        sends[k].wait_recv()
        source = (x + NX - dx) % NX * ny + (y + ny - dy) % ny
        piece = got.at[source, :, mine]
        forwards.append(remote(piece, piece, fsend.at[k], frecv.at[k], sibling))
        forwards[-1].start()
    for copy in forwards:
        copy.wait()
    for copy in sends:
        copy.wait_send()
    local.wait()


def return_kernel(part, back, other, total, send, recv, csend, crecv):
    z, x, r, y = here()
    ny = lax.axis_size("col")
    steps = plane_steps(ny)
    sibling = (z, x, 1 - r, y)
    greet([(z, (x + dx) % NX, r, (y + dy) % ny) for dx, dy in steps] + [sibling])
    me = x * ny + y
    half = back.shape[2]
    keep, give = lanes_at(r, half), lanes_at(1 - r, half)
    steps = steps + [(0, 0)]
    swaps, sends = [], []
    for k, (dx, dy) in enumerate(steps):
        to = (x + dx) % NX * ny + (y + dy) % ny
        swaps.append(remote(part.at[to, :, give], other.at[to], csend.at[k], crecv.at[k], sibling))
        swaps[-1].start()
    for k, (dx, dy) in enumerate(steps):
        tx, ty = (x + dx) % NX, (y + dy) % ny
        to = tx * ny + ty
        swaps[k].wait_recv()
        value = (part[to, :, keep].astype(F32) + other[to].astype(F32)).astype(BF)
        if dx or dy:
            total[to] = value
            sends.append(remote(total.at[to], back.at[me], send.at[k], recv.at[k], (z, tx, r, ty)))
            sends[-1].start()
        else:
            back[me] = value
    for copy in sends:
        copy.wait()
    for copy in swaps:
        copy.wait_send()


def ring_sum(nz, z, up, down, chunks, slabs, low, top, came, leave, send, recv):
    half = nz // 2
    far = (z + half) % nz
    copies = [
        remote(chunks.at[(far,) + low], came.at[(0, 0) + low], send.at[0, 0], recv.at[0, 0], up),
        remote(chunks.at[(far,) + top], came.at[(1, 0) + top], send.at[1, 0], recv.at[1, 0], down),
    ]
    for copy in copies:
        copy.start()
    for s in range(1, half):
        for way, device in ((0, up), (1, down)):
            d = (z + half - s) % nz if way == 0 else (z + half + s) % nz
            copies[2 * (s - 1) + way].wait_recv()
            for slab in slabs:
                if s == 1 and slab[0] != way:
                    leave[(way, s - 1) + slab[1]] = chunks[(d,) + slab[1]]
                else:
                    value = chunks[(d,) + slab[1]].astype(F32) + came[(way, s - 1) + slab[1]].astype(F32)
                    leave[(way, s - 1) + slab[1]] = value.astype(BF)
            copies.append(remote(leave.at[way, s - 1], came.at[way, s], send.at[way, s], recv.at[way, s], device))
            copies[-1].start()
    return copies


def gap_kernel(nz, parts, teacher, gaps, loss, arrived, came, leave, total, send, recv, zsend, zrecv, gsend, grecv):
    z, x, r, y = here()
    ny = lax.axis_size("col")
    steps = plane_steps(ny)
    up, down = ((z + 1) % nz, x, r, y), ((z + nz - 1) % nz, x, r, y)
    greet([(z, (x + dx) % NX, r, (y + dy) % ny) for dx, dy in steps] + [up, down])
    me = x * ny + y
    half = teacher.shape[2] // 2
    low, top = (slice(None), pl.ds(0, half)), (slice(None), pl.ds(half, half))
    sends = []
    for k, (dx, dy) in enumerate(steps):
        tx, ty = (x + dx) % NX, (y + dy) % ny
        sends.append(remote(parts.at[tx * ny + ty], arrived.at[k], send.at[k], recv.at[k], (z, tx, r, ty)))
        sends[-1].start()
    ring = ring_sum(nz, z, up, down, teacher, [(0, low), (1, top)], low, top, came, leave, zsend, zrecv)
    total[...] = parts[me].astype(F32) - teacher[z].astype(F32)
    for k in reversed(range(len(steps))):
        sends[k].wait_recv()
        total[...] += arrived[k].astype(F32)
    for way in (0, 1):
        ring[-2 + way].wait_recv()
        total[...] -= came[way, nz // 2 - 1].astype(F32)
    gaps[me] = total[...].astype(BF)
    outs = []
    for k, (dx, dy) in enumerate(steps):
        tx, ty = (x + dx) % NX, (y + dy) % ny
        outs.append(remote(gaps.at[me], gaps.at[me], gsend.at[k], grecv.at[k], (z, tx, r, ty)))
        outs[-1].start()
    squares = jnp.zeros(loss.shape, F32)
    for tile in range(total.shape[1] // 128):
        value = total[:, pl.ds(tile * 128, 128)]
        squares += value * value
    loss[...] = squares
    for copy in outs:
        copy.wait()
    for copy in sends + ring:
        copy.wait_send()


def grad_kernel(nz, term, loss, grad, losses, chunks, came, leave, total, send, recv, csend, crecv, xsend, xrecv, lsend, lrecv, own):
    z, x, r, y = here()
    ny = lax.axis_size("col")
    up, down = ((z + 1) % nz, x, r, y), ((z + nz - 1) % nz, x, r, y)
    sibling = (z, x, 1 - r, y)
    mates = [(d, (z, x, r, (y + d) % ny)) for d in range(1, ny)]
    mates += [(ny + d, (z, x, 1 - r, (y + d) % ny)) for d in range(ny)]
    across = [(d, (x + d) % NX) for d in (2, 1, 3)]
    greet([up, down] + [m for _, m in mates] + [(z, tx, r, y) for _, tx in across])
    rows, span = chunks.shape[1], chunks.shape[2]
    keep = pl.ds(pl.multiple_of(r * rows, rows), rows)
    give = pl.ds(pl.multiple_of((1 - r) * rows, rows), rows)
    per = nz // 2
    local, swaps = [], []
    for q in range(per):
        columns = pl.ds(q * span, span)
        swaps.append(remote(term.at[give, columns], chunks.at[r * per + q], csend.at[q], crecv.at[q], sibling))
        swaps[-1].start()
        local.append(pltpu.make_async_copy(term.at[keep, columns], chunks.at[r * per + q], own.at[q]))
        local[-1].start()
    slot = r * ny + y
    local.append(pltpu.make_async_copy(loss, losses.at[slot], own.at[per]))
    local[-1].start()
    tells = []
    for k, (_, device) in enumerate(mates):
        tells.append(remote(loss, losses.at[slot], lsend.at[k], lrecv.at[k], device))
        tells[-1].start()
    for copy in local:
        copy.wait()
    for copy in swaps:
        copy.wait_recv()
    half = rows // 2
    low, top = (pl.ds(0, half), slice(None)), (pl.ds(half, half), slice(None))
    ring = ring_sum(nz, z, up, down, chunks, [(0, low), (1, top)], low, top, came, leave, send, recv)
    for way in (0, 1):
        ring[-2 + way].wait_recv()
    value = chunks[z].astype(F32) + came[0, per - 1].astype(F32) + came[1, per - 1].astype(F32)
    total[...] = value.astype(BF)
    lanes = span // NX
    outs = []
    for d, tx in across:
        outs.append(remote(total.at[:, lanes_at(tx, lanes)], grad.at[x], xsend.at[d - 1], xrecv.at[d - 1], (z, tx, r, y)))
        outs[-1].start()
    last = pltpu.make_async_copy(total.at[:, lanes_at(x, lanes)], grad.at[x], own.at[per + 1])
    last.start()
    last.wait()
    for copy in outs + tells:
        copy.wait()
    for copy in swaps + ring:
        copy.wait_send()


def routing(routes, weights, plane, ny, cap):
    nz, block, _ = routes.shape
    experts = NX * ny
    local = routes - plane * experts
    ids = jnp.arange(experts, dtype=jnp.int32)
    hit = local[..., None] == ids
    named = jnp.any(hit, axis=2)
    weight = jnp.sum(jnp.where(hit, weights[..., None], 0.0), axis=2)
    count = named.astype(jnp.int32)
    slot = jnp.cumsum(count, axis=1) - count
    place = named[..., None] & (slot[..., None] == jnp.arange(cap, dtype=jnp.int32))
    same = jnp.eye(nz, dtype=bool)
    full = place[:, :, :, None, :] & same[:, None, None, :, None]
    combine = jnp.where(full, weight[:, :, :, None, None], 0.0)
    rows = experts * nz * cap
    return full.reshape(nz * block, rows).astype(BF), combine.reshape(nz * block, rows)


def on_device(tokens, routes, route_weights, teacher_in, teacher_out, student_in, student_out):
    nz, nr, ny = lax.axis_size("z"), lax.axis_size("row"), lax.axis_size("col")
    z, x, r, y = here()
    tok, width = tokens.shape
    block, top = routes.shape
    blk = student_in.shape[1]
    ff = student_in.shape[2]
    sub = ff // NX
    half = width // nr
    experts = NX * ny
    cap = max(2, 3 * block * top // (2 * nz * experts))
    blocks = nz * NX
    shape = jax.ShapeDtypeStruct

    parts = jnp.concatenate([jnp.swapaxes(student_in, 1, 2), student_out[None]], axis=0)
    parts = pad_lanes(parts)
    lanes = parts.shape[-1]
    wide = blocks * lanes
    inner, outer = kernel_call(
        weights_kernel, 0,
        [shape((2, sub, NX * lanes), BF), shape((sub, NX * lanes), BF)],
        [dma(3, 3), dma(3, 3), dma(3)],
        parts.reshape(3, NX, sub, lanes),
    )
    padded = pad_lanes(tokens.reshape(tok, blocks, blk)).reshape(tok, wide)
    mine = lax.dynamic_slice(tokens, (y * block, r * half), (block, half))
    meta = jnp.concatenate([routes.astype(F32), route_weights], axis=1)
    meta = jnp.pad(meta, ((0, 0), (0, 128 - 2 * top)))
    inner, outer, padded, mine, meta = lax.optimization_barrier((inner, outer, padded, mine, meta))
    inner = lax.all_gather(inner, "z", axis=2, tiled=True)
    outer = lax.all_gather(outer, "z", axis=1, tiled=True)

    steps = nz // 2
    plane_tokens, column, metas = kernel_call(
        functools.partial(tokens_kernel, nz), 1,
        [shape((NX, tok, wide), BF), shape((nz, block, half), BF), shape((nz, block, 128), F32)],
        [dma(3), dma(3), dma(2, 3), dma(2, 3), dma(3, 3), dma(3, 3)] + [dma(2, steps)] * 4 + [dma(3)],
        padded, mine, meta,
    )
    routes_z = metas[:, :, :top].astype(jnp.int32)
    place, combine = routing(routes_z, metas[:, :, top:2 * top], z, ny, cap)
    slots = nz * cap
    outgoing = dot(place, column.reshape(nz * block, half), ((0,), (0,))).astype(BF)
    (arrived,) = kernel_call(
        dispatch_kernel, 2,
        [shape((experts, slots, width), BF)],
        [dma(experts)] * 4 + [dma(1)],
        outgoing.reshape(experts, slots, half),
    )
    arrived = arrived.reshape(experts * slots, width)
    gate = dot(arrived, teacher_in[0, 0], ((1,), (0,)))
    up = dot(arrived, teacher_in[0, 1], ((1,), (0,)))
    act = (jax.nn.silu(gate) * up).astype(BF)
    part = dot(act, teacher_out[0], ((1,), (0,))).astype(BF)
    (back,) = kernel_call(
        return_kernel, 3,
        [shape((experts, slots, half), BF)],
        [pltpu.VMEM((experts, slots, half), BF)] * 2 + [dma(experts)] * 4,
        part.reshape(experts, slots, width),
    )
    back = back.reshape(experts * slots, half)
    high = combine.astype(BF)
    low = (combine - high.astype(F32)).astype(BF)
    teacher = dot(jnp.concatenate([high, low], axis=1), jnp.concatenate([back, back], axis=0), ((1,), (0,))).astype(BF)
    teacher = pad_lanes(teacher.reshape(nz, block, blocks // nr, blk)).reshape(nz, block, wide // nr)

    plane_tokens = plane_tokens.reshape(NX * tok, wide)
    gate = dot(plane_tokens, inner[0], ((1,), (1,)))
    up = dot(plane_tokens, inner[1], ((1,), (1,)))
    hidden = (jax.nn.silu(gate) * up).astype(BF)
    hidden_both = lax.all_gather(hidden, "row", axis=1, tiled=True)
    outer_both = lax.all_to_all(outer.reshape(sub, nr, wide // nr), "row", split_axis=1, concat_axis=0, tiled=True)
    outer_both = outer_both.reshape(nr * sub, wide // nr)
    y_part = dot(hidden_both, outer_both, ((1,), (0,))).astype(BF)
    span = wide // nr
    gap_round, loss = kernel_call(
        functools.partial(gap_kernel, nz), 4,
        [shape((experts, block, span), BF), shape((block, 128), F32)],
        [pltpu.VMEM((experts - 1, block, span), BF)]
        + [pltpu.VMEM((2, steps, block, span), BF), pltpu.VMEM((2, steps - 1, block, span), BF)]
        + [pltpu.VMEM((block, span), F32)]
        + [dma(experts - 1)] * 2 + [dma(2, steps)] * 2 + [dma(experts - 1)] * 2,
        y_part.reshape(experts, block, span), teacher,
    )
    term = (dot(hidden_both, gap_round.reshape(experts * block, span), ((0,), (0,))) / tok).astype(BF)
    chunk = NX * lanes
    grad, losses = kernel_call(
        functools.partial(grad_kernel, nz), 5,
        [shape((NX, sub, lanes), BF), shape((nr * ny, block, 128), F32)],
        [pltpu.VMEM((nz, sub, chunk), BF), pltpu.VMEM((2, steps, sub, chunk), BF)]
        + [pltpu.VMEM((2, steps - 1, sub, chunk), BF), pltpu.VMEM((sub, chunk), BF)]
        + [dma(2, steps)] * 2 + [dma(steps)] * 2 + [dma(3)] * 2 + [dma(2 * ny - 1)] * 2 + [dma(steps + 2)],
        term, loss,
    )
    token_loss = jnp.sum(losses.reshape(nr, ny * block, 128), axis=(0, 2)) / width
    grad = grad.reshape(ff, lanes)[:, :blk].astype(F32)
    return token_loss, grad


def solution(mesh):
    dp = ("z", "x")
    in_specs = (
        P(dp, None),
        P(dp + ("col",), None),
        P(dp + ("col",), None),
        P(dp + ("col",), None, None, "row"),
        P(dp + ("col",), "row", None),
        P(None, dp, ("row", "col")),
        P(("row", "col"), dp),
    )
    out_specs = (P(dp), P(("row", "col"), dp))
    return jax.shard_map(
        on_device, mesh=split_mesh(mesh), in_specs=in_specs, out_specs=out_specs, check_vma=False
    )
```

```python
import functools

import jax
import jax.numpy as jnp
from jax import lax
from jax.experimental import pallas as pl
from jax.experimental.pallas import tpu as pltpu
from jax.sharding import Mesh, PartitionSpec as P

NX = 4
MESH = pl.DeviceIdType.MESH
F32 = jnp.float32
BF = jnp.bfloat16


def split_mesh(mesh):
    dp, row, col = mesh.devices.shape
    return Mesh(mesh.devices.reshape(dp // NX, NX, row, col), ("z", "x", "row", "col"))


def dot(a, b, dims):
    return lax.dot_general(a, b, (dims, ((), ())), preferred_element_type=F32)


def pad_lanes(a):
    lanes = a.shape[-1]
    wide = -(-lanes // 128) * 128
    return jnp.pad(a, [(0, 0)] * (a.ndim - 1) + [(0, wide - lanes)])


def here():
    return tuple(lax.axis_index(a) for a in ("z", "x", "row", "col"))


def remote(src, dst, send, recv, device):
    return pltpu.make_async_remote_copy(
        src_ref=src, dst_ref=dst, send_sem=send, recv_sem=recv, device_id=device, device_id_type=MESH
    )


def greet(devices):
    barrier = pltpu.get_barrier_semaphore()
    for device in devices:
        pl.semaphore_signal(barrier, inc=1, device_id=device, device_id_type=MESH)
    pl.semaphore_wait(barrier, len(devices))


def lanes_at(start, size):
    return pl.ds(pl.multiple_of(start * size, size), size)


def kernel_call(body, number, outs, scratch, *args):
    whole = pl.BlockSpec(memory_space=pltpu.VMEM)
    return pl.pallas_call(
        body,
        out_shape=outs,
        in_specs=[whole] * len(args),
        out_specs=[whole] * len(outs),
        scratch_shapes=scratch,
        compiler_params=pltpu.CompilerParams(
            collective_id=number, has_side_effects=True, vmem_limit_bytes=48 * 1024 * 1024
        ),
    )(*args)


def dma(*shape):
    return pltpu.SemaphoreType.DMA(shape)


def plane_steps(ny):
    steps = [(dx, dy) for dx in range(NX) for dy in range(ny) if dx or dy]
    far = lambda s: min(s[0], NX - s[0]) + min(s[1], ny - s[1])
    return sorted(steps, key=far, reverse=True)


def tokens_kernel(nz, padded, mine, meta, parts, plane, column, metas, shard, xs, xr, ys, yr, cs, cr, zs, zr, ms, mr, ws, wr, own):
    z, x, r, y = here()
    up, down = (z + 1) % nz, (z + nz - 1) % nz
    ny = lax.axis_size("col")
    north, south = (y + 1) % ny, (y + ny - 1) % ny
    sibling = (z, x, 1 - r, y)
    per = nz // 2
    core = z // per
    plane_z = per * r + z % per
    moves = core != r
    others = [(z, (x + d) % NX, r, y) for d in (1, 2, 3)]
    others += [(plane_z, (x + d) % NX, core, y) for d in (1, 2, 3)]
    others += [(z, x, r, north), (z, x, r, south), (up, x, r, y), (down, x, r, y), sibling]

    @pl.when(moves)
    def _():
        greet(others + [(plane_z, x, core, y)])

    @pl.when(jnp.logical_not(moves))
    def _():
        greet(others)

    rows, wide = padded.shape
    high, span = rows // 2, wide // 2
    quarter = span // 2
    mine_rows = pl.ds(pl.multiple_of(r * high, high), high)
    parity = y % 2
    held = lanes_at(parity, span)
    slot = lanes_at(x, 128)
    started = []

    def go(copy):
        copy.start()
        started.append(copy)
        return copy

    local = [
        pltpu.make_async_copy(padded, plane.at[x], own.at[0]),
        pltpu.make_async_copy(mine, column.at[z], own.at[1]),
        pltpu.make_async_copy(meta, metas.at[z], own.at[2]),
        pltpu.make_async_copy(parts.at[0, x], shard.at[0, :, slot], own.at[3]),
        pltpu.make_async_copy(parts.at[1, x], shard.at[1, :, slot], own.at[4]),
    ]
    for copy in local:
        copy.start()

    def z_step(s):
        half = mine.shape[1] // 2
        a, b = (z + nz - s + 1) % nz, (z + s - 1) % nz
        if s == 1:
            one, two, three, four = mine, mine, meta, meta
        else:
            one, two, three, four = column.at[a], column.at[b], metas.at[a], metas.at[b]
        to_a, to_b = column.at[a], column.at[b]
        if s == nz // 2:
            low, top = pl.ds(0, half), pl.ds(half, half)
            one, to_a, two, to_b = column.at[a, :, low], column.at[a, :, low], column.at[b, :, top], column.at[b, :, top]
        out = [
            go(remote(one, to_a, zs.at[0, s - 1], zr.at[0, s - 1], (up, x, r, y))),
            go(remote(two, to_b, zs.at[1, s - 1], zr.at[1, s - 1], (down, x, r, y))),
            go(remote(three, metas.at[a], ms.at[0, s - 1], mr.at[0, s - 1], (up, x, r, y))),
        ]
        if s < nz // 2:
            out.append(go(remote(four, metas.at[b], ms.at[1, s - 1], mr.at[1, s - 1], (down, x, r, y))))
        return out

    def arrived(copies):
        for copy in copies:
            copy.wait_recv()

    ring = z_step(1)
    from_x = {}
    for d in (2, 1, 3):
        device = (z, (x + d) % NX, r, y)
        from_x[d] = go(remote(padded.at[mine_rows, held], plane.at[x, mine_rows, held], xs.at[d - 1], xr.at[d - 1], device))
    weights = []
    for d in (2, 1, 3):
        to = (x + d) % NX
        for kind in (0, 1):
            weights.append(go(remote(parts.at[kind, to], shard.at[kind, :, slot], ws.at[d, kind], wr.at[d, kind], (z, to, r, y))))
        weights.append(go(remote(parts.at[2, to], shard.at[2, :, slot], ws.at[d, 2], wr.at[d, 2], (plane_z, to, core, y))))
    down_own = remote(parts.at[2, x], shard.at[2, :, slot], ws.at[0, 2], wr.at[0, 2], (plane_z, x, core, y))
    down_here = pltpu.make_async_copy(parts.at[2, x], shard.at[2, :, slot], own.at[5])

    @pl.when(moves)
    def _():
        down_own.start()

    @pl.when(jnp.logical_not(moves))
    def _():
        down_here.start()

    turn = 0
    from_sib, from_y = [], []
    for d in (1, 3, 2):
        arrived(ring)
        turn += 1
        ring = z_step(turn + 1)
        from_x[d].wait_recv()
        source = (x + NX - d) % NX
        for side, device in ((0, (z, x, r, north)), (1, (z, x, r, south))):
            piece = plane.at[source, mine_rows, lanes_at(parity * 2 + side, quarter)]
            from_y.append((d, side, go(remote(piece, piece, ys.at[side, d - 1], yr.at[side, d - 1], device))))
        piece = plane.at[source, mine_rows, held]
        from_sib.append(go(remote(piece, piece, cs.at[0, d - 1], cr.at[0, d - 1], sibling)))
    arrived(ring)
    for d, side, copy in from_y:
        copy.wait_recv()
        source = (x + NX - d) % NX
        piece = plane.at[source, mine_rows, lanes_at((1 - parity) * 2 + side, quarter)]
        from_sib.append(go(remote(piece, piece, cs.at[1 + side, d - 1], cr.at[1 + side, d - 1], sibling)))
    arrived(weights)
    arrived(from_sib)
    for copy in started:
        copy.wait_send()
    for copy in local:
        copy.wait()

    @pl.when(moves)
    def _():
        down_own.wait()

    @pl.when(jnp.logical_not(moves))
    def _():
        down_here.wait()


def dispatch_kernel(outgoing, got, send, recv, fsend, frecv, own):
    z, x, r, y = here()
    ny = lax.axis_size("col")
    steps = plane_steps(ny)
    sibling = (z, x, 1 - r, y)
    greet([(z, (x + dx) % NX, r, (y + dy) % ny) for dx, dy in steps] + [sibling])
    me = x * ny + y
    mine = lanes_at(r, outgoing.shape[2])
    local = pltpu.make_async_copy(outgoing.at[me], got.at[me, :, mine], own.at[0])
    local.start()
    sends, forwards = [], []
    for k, (dx, dy) in enumerate(steps):
        tx, ty = (x + dx) % NX, (y + dy) % ny
        sends.append(remote(outgoing.at[tx * ny + ty], got.at[me, :, mine], send.at[k], recv.at[k], (z, tx, r, ty)))
        sends[-1].start()
    forwards.append(remote(outgoing.at[me], got.at[me, :, mine], fsend.at[len(steps)], frecv.at[len(steps)], sibling))
    forwards[-1].start()
    for k, (dx, dy) in reversed(list(enumerate(steps))):
        sends[k].wait_recv()
        source = (x + NX - dx) % NX * ny + (y + ny - dy) % ny
        piece = got.at[source, :, mine]
        forwards.append(remote(piece, piece, fsend.at[k], frecv.at[k], sibling))
        forwards[-1].start()
    for copy in forwards:
        copy.wait()
    for copy in sends:
        copy.wait_send()
    local.wait()


def return_kernel(part, back, other, total, send, recv, csend, crecv):
    z, x, r, y = here()
    ny = lax.axis_size("col")
    steps = plane_steps(ny)
    sibling = (z, x, 1 - r, y)
    greet([(z, (x + dx) % NX, r, (y + dy) % ny) for dx, dy in steps] + [sibling])
    me = x * ny + y
    half = back.shape[2]
    keep, give = lanes_at(r, half), lanes_at(1 - r, half)
    steps = steps + [(0, 0)]
    swaps, sends = [], []
    for k, (dx, dy) in enumerate(steps):
        to = (x + dx) % NX * ny + (y + dy) % ny
        swaps.append(remote(part.at[to, :, give], other.at[to], csend.at[k], crecv.at[k], sibling))
        swaps[-1].start()
    for k, (dx, dy) in enumerate(steps):
        tx, ty = (x + dx) % NX, (y + dy) % ny
        to = tx * ny + ty
        swaps[k].wait_recv()
        value = (part[to, :, keep].astype(F32) + other[to].astype(F32)).astype(BF)
        if dx or dy:
            total[to] = value
            sends.append(remote(total.at[to], back.at[me], send.at[k], recv.at[k], (z, tx, r, ty)))
            sends[-1].start()
        else:
            back[me] = value
    for copy in sends:
        copy.wait()
    for copy in swaps:
        copy.wait_send()


def ring_sum(n, i, up, down, ref, where, subs, came, leave, send, recv, copies):
    half = n // 2

    def go(way, s, u, src, dst):
        copy = remote(src, dst, send.at[way, s, u], recv.at[way, s, u], (up, down)[way])
        copy.start()
        copies[way, s, u] = copy

    for u, (whole, low, top) in enumerate(subs):
        for way, part in ((0, low), (1, top)):
            go(way, 0, u, ref.at[where((i + half) % n, part)], came.at[(way, 0) + part])
    yield
    for s in range(1, half):
        for u, (whole, low, top) in enumerate(subs):
            for way in (0, 1):
                d = (i + half - s) % n if way == 0 else (i + half + s) % n
                copies[way, s - 1, u].wait_recv()
                summed, plain = whole, None
                if s == 1:
                    summed, plain = (low, top) if way == 0 else (top, low)
                    leave[(way, 0) + plain] = ref[where(d, plain)]
                value = ref[where(d, summed)].astype(F32) + came[(way, s - 1) + summed].astype(F32)
                leave[(way, s - 1) + summed] = value.astype(BF)
                go(way, s, u, leave.at[(way, s - 1) + whole], came.at[(way, s) + whole])
        yield
    for u in range(len(subs)):
        for way in (0, 1):
            copies[way, half - 1, u].wait_recv()


def ring_gather(n, i, up, down, ref, where, whole, low, top, send, recv, copies):
    half = n // 2
    for s in range(half):
        for way, device in ((0, up), (1, down)):
            d = (i + n - s) % n if way == 0 else (i + s) % n
            if s:
                copies[way, s - 1].wait_recv()
            part = whole if s < half - 1 else (low, top)[way]
            piece = ref.at[where(d, part)]
            copies[way, s] = remote(piece, piece, send.at[way, s, 0], recv.at[way, s, 0], device)
            copies[way, s].start()
        yield
    for way in (0, 1):
        copies[way, half - 1].wait_recv()


def together(*rings):
    rings = list(rings)
    while rings:
        for ring in list(rings):
            try:
                next(ring)
            except StopIteration:
                rings.remove(ring)


def gap_kernel(nz, parts, teacher, gaps, loss, xcame, xleave, ycame, yleave, xsum, ysum, xcame2, xleave2, ycame2, yleave2,
               tcame, tleave, total, send, recv):
    z, x, r, y = here()
    ny = lax.axis_size("col")
    up, down = ((z + 1) % nz, x, r, y), ((z + nz - 1) % nz, x, r, y)
    east, west = (z, (x + 1) % NX, r, y), (z, (x + NX - 1) % NX, r, y)
    north, south = (z, x, r, (y + 1) % ny), (z, x, r, (y + ny - 1) % ny)
    greet([east, west, north, south, up, down])
    span = teacher.shape[2]
    wing = span // 2
    every = slice(None)
    first, second = pl.ds(0, wing), pl.ds(wing, wing)
    copies = [{} for _ in range(9)]

    def sems(k):
        return send.at[k], recv.at[k], copies[k]

    def trio(axis_size):
        return (pl.ds(0, axis_size),), (pl.ds(0, axis_size // 2),), (pl.ds(axis_size // 2, axis_size // 2),)

    def lanes(start, size):
        return tuple((every, pl.ds(start + o, s)) for o, s in ((0, size), (0, size // 2), (size // 2, size // 2)))

    teach = ring_sum(nz, z, up, down, teacher, lambda d, p: (d,) + p, [lanes(0, span)], tcame, tleave, *sems(0))
    ring_x = ring_sum(NX, x, east, west, parts, lambda d, p: (d,) + p + (every, first), [trio(ny)], xcame, xleave, *sems(1))
    ring_y = ring_sum(ny, y, north, south, parts, lambda d, p: p + (d, every, second), [trio(NX)], ycame, yleave, *sems(2))
    next(ring_x)
    next(ring_y)
    next(teach)
    together(ring_x, ring_y)
    xsum[...] = (parts[x, :, :, first].astype(F32) + xcame[0, NX // 2 - 1].astype(F32) + xcame[1, NX // 2 - 1].astype(F32)).astype(BF)
    ring_y = ring_sum(ny, y, north, south, xsum, lambda d, p: (d,) + p, [lanes(0, wing)], ycame2, yleave2, *sems(3))
    next(ring_y)
    ysum[...] = (parts[:, y, :, second].astype(F32) + ycame[0, ny // 2 - 1].astype(F32) + ycame[1, ny // 2 - 1].astype(F32)).astype(BF)
    ring_x = ring_sum(NX, x, east, west, ysum, lambda d, p: (d,) + p, [lanes(0, wing)], xcame2, xleave2, *sems(4))
    next(ring_x)
    together(teach, ring_y, ring_x)
    taught = teacher[z].astype(F32) + tcame[0, nz // 2 - 1].astype(F32) + tcame[1, nz // 2 - 1].astype(F32)
    total[...] = -taught
    total[:, first] += xsum[y].astype(F32) + ycame2[0, ny // 2 - 1].astype(F32) + ycame2[1, ny // 2 - 1].astype(F32)
    total[:, second] += ysum[x].astype(F32) + xcame2[0, NX // 2 - 1].astype(F32) + xcame2[1, NX // 2 - 1].astype(F32)
    gaps[x, y] = total[...].astype(BF)
    gather_y = ring_gather(ny, y, north, south, gaps, lambda d, p: (x, d) + p, *lanes(0, wing), *sems(5))
    gather_x = ring_gather(NX, x, east, west, gaps, lambda d, p: (d, y) + p, *lanes(wing, wing), *sems(6))
    next(gather_y)
    next(gather_x)
    squares = jnp.zeros(loss.shape, F32)
    for tile in range(span // 128):
        value = total[:, pl.ds(tile * 128, 128)]
        squares += value * value
    loss[...] = squares
    together(gather_y, gather_x)
    gather_x = ring_gather(NX, x, east, west, gaps, lambda d, p: (d,) + p + (every, first), *trio(ny), *sems(7))
    gather_y = ring_gather(ny, y, north, south, gaps, lambda d, p: p + (d, every, second), *trio(NX), *sems(8))
    together(gather_x, gather_y)
    for group in copies:
        for copy in group.values():
            copy.wait_send()


def grad_kernel(nz, term, loss, grad, losses, chunks, came, leave, total, send, recv, csend, crecv, xsend, xrecv, lsend, lrecv, own):
    z, x, r, y = here()
    ny = lax.axis_size("col")
    up, down = ((z + 1) % nz, x, r, y), ((z + nz - 1) % nz, x, r, y)
    sibling = (z, x, 1 - r, y)
    mates = [(z, x, r, (y + d) % ny) for d in range(1, ny)] + [(z, x, 1 - r, (y + d) % ny) for d in range(ny)]
    across = [(d, (x + d) % NX) for d in (2, 1, 3)]
    greet([up, down] + mates + [(z, tx, r, y) for _, tx in across])
    rows, span = chunks.shape[1], chunks.shape[2]
    keep = pl.ds(pl.multiple_of(r * rows, rows), rows)
    give = pl.ds(pl.multiple_of((1 - r) * rows, rows), rows)
    per = nz // 2
    local, swaps = [], []
    for q in range(per):
        columns = pl.ds(q * span, span)
        swaps.append(remote(term.at[give, columns], chunks.at[r * per + q], csend.at[q], crecv.at[q], sibling))
        swaps[-1].start()
        local.append(pltpu.make_async_copy(term.at[keep, columns], chunks.at[r * per + q], own.at[q]))
        local[-1].start()
    slot = r * ny + y
    local.append(pltpu.make_async_copy(loss, losses.at[slot], own.at[per]))
    local[-1].start()
    tells = []
    for k, device in enumerate(mates):
        tells.append(remote(loss, losses.at[slot], lsend.at[k], lrecv.at[k], device))
        tells[-1].start()
    for copy in local:
        copy.wait()
    for copy in swaps:
        copy.wait_recv()
    subs = []
    for u in (0, 1):
        band = pl.ds(u * (rows // 2), rows // 2)
        subs.append(((band, pl.ds(0, span)), (band, pl.ds(0, span // 2)), (band, pl.ds(span // 2, span // 2))))
    ring = {}
    together(ring_sum(nz, z, up, down, chunks, lambda d, p: (d,) + p, subs, came, leave, send, recv, ring))
    value = chunks[z].astype(F32) + came[0, per - 1].astype(F32) + came[1, per - 1].astype(F32)
    total[...] = value.astype(BF)
    lanes = span // NX
    outs = []
    for d, tx in across:
        outs.append(remote(total.at[:, lanes_at(tx, lanes)], grad.at[x], xsend.at[d - 1], xrecv.at[d - 1], (z, tx, r, y)))
        outs[-1].start()
    last = pltpu.make_async_copy(total.at[:, lanes_at(x, lanes)], grad.at[x], own.at[per + 1])
    last.start()
    last.wait()
    for copy in outs + tells:
        copy.wait()
    for copy in swaps + list(ring.values()):
        copy.wait_send()


def routing(routes, weights, plane, ny, cap):
    nz, block, _ = routes.shape
    experts = NX * ny
    local = routes - plane * experts
    ids = jnp.arange(experts, dtype=jnp.int32)
    hit = local[..., None] == ids
    named = jnp.any(hit, axis=2)
    weight = jnp.sum(jnp.where(hit, weights[..., None], 0.0), axis=2)
    count = named.astype(jnp.int32)
    slot = jnp.cumsum(count, axis=1) - count
    place = named[..., None] & (slot[..., None] == jnp.arange(cap, dtype=jnp.int32))
    same = jnp.eye(nz, dtype=bool)
    full = place[:, :, :, None, :] & same[:, None, None, :, None]
    combine = jnp.where(full, weight[:, :, :, None, None], 0.0)
    rows = experts * nz * cap
    return full.reshape(nz * block, rows).astype(BF), combine.reshape(nz * block, rows)


def on_device(tokens, routes, route_weights, teacher_in, teacher_out, student_in, student_out):
    nz, nr, ny = lax.axis_size("z"), lax.axis_size("row"), lax.axis_size("col")
    z, x, r, y = here()
    tok, width = tokens.shape
    block, top = routes.shape
    blk = student_in.shape[1]
    ff = student_in.shape[2]
    sub = ff // NX
    half = width // nr
    experts = NX * ny
    cap = max(2, 3 * block * top // (2 * nz * experts))
    blocks = nz * NX
    shape = jax.ShapeDtypeStruct

    parts = jnp.concatenate([jnp.swapaxes(student_in, 1, 2), student_out[None]], axis=0)
    parts = pad_lanes(parts)
    lanes = parts.shape[-1]
    wide = blocks * lanes
    padded = pad_lanes(tokens.reshape(tok, blocks, blk)).reshape(tok, wide)
    mine = lax.dynamic_slice(tokens, (y * block, r * half), (block, half))
    meta = jnp.concatenate([routes.astype(F32), route_weights], axis=1)
    meta = jnp.pad(meta, ((0, 0), (0, 128 - 2 * top)))
    steps = nz // 2
    plane_tokens, column, metas, shard = kernel_call(
        functools.partial(tokens_kernel, nz), 1,
        [shape((NX, tok, wide), BF), shape((nz, block, half), BF), shape((nz, block, 128), F32), shape((3, sub, NX * lanes), BF)],
        [dma(3), dma(3), dma(2, 3), dma(2, 3), dma(3, 3), dma(3, 3)] + [dma(2, steps)] * 4 + [dma(4, 3)] * 2 + [dma(6)],
        padded, mine, meta, parts.reshape(3, NX, sub, lanes),
    )
    student = lax.all_gather(shard, "z", axis=2, tiled=True)
    routes_z = metas[:, :, :top].astype(jnp.int32)
    place, combine = routing(routes_z, metas[:, :, top:2 * top], z, ny, cap)
    slots = nz * cap
    outgoing = dot(place, column.reshape(nz * block, half), ((0,), (0,))).astype(BF)
    (arrived,) = kernel_call(
        dispatch_kernel, 2,
        [shape((experts, slots, width), BF)],
        [dma(experts)] * 4 + [dma(1)],
        outgoing.reshape(experts, slots, half),
    )
    arrived = arrived.reshape(experts * slots, width)
    gate = dot(arrived, teacher_in[0, 0], ((1,), (0,)))
    up = dot(arrived, teacher_in[0, 1], ((1,), (0,)))
    act = (jax.nn.silu(gate) * up).astype(BF)
    part = dot(act, teacher_out[0], ((1,), (0,))).astype(BF)
    (back,) = kernel_call(
        return_kernel, 3,
        [shape((experts, slots, half), BF)],
        [pltpu.VMEM((experts, slots, half), BF)] * 2 + [dma(experts)] * 4,
        part.reshape(experts, slots, width),
    )
    back = back.reshape(experts * slots, half)
    high = combine.astype(BF)
    low = (combine - high.astype(F32)).astype(BF)
    teacher = dot(jnp.concatenate([high, low], axis=1), jnp.concatenate([back, back], axis=0), ((1,), (0,))).astype(BF)
    teacher = pad_lanes(teacher.reshape(nz, block, blocks // nr, blk)).reshape(nz, block, wide // nr)

    plane_tokens = plane_tokens.reshape(NX * tok, wide)
    gate = dot(plane_tokens, student[0], ((1,), (1,)))
    up = dot(plane_tokens, student[1], ((1,), (1,)))
    hidden = (jax.nn.silu(gate) * up).astype(BF)
    hidden_both = lax.all_gather(hidden, "row", axis=1, tiled=True)
    span = wide // nr
    y_part = sum(dot(hidden_both[:, i * sub:(i + 1) * sub], student[2, :, i * span:(i + 1) * span], ((1,), (0,))) for i in range(nr)).astype(BF)
    wing = span // 2
    buffers = [(2, 2, ny, block, wing), (2, 1, ny, block, wing), (2, 2, NX, block, wing), (2, 1, NX, block, wing)]
    buffers += [(ny, block, wing), (NX, block, wing)] + [(2, 2, block, wing), (2, 1, block, wing)] * 2
    buffers += [(2, steps, block, span), (2, steps - 1, block, span)]
    gap_round, loss = kernel_call(
        functools.partial(gap_kernel, nz), 4,
        [shape((NX, ny, block, span), BF), shape((block, 128), F32)],
        [pltpu.VMEM(b, BF) for b in buffers] + [pltpu.VMEM((block, span), F32)] + [dma(9, 2, steps, 1)] * 2,
        y_part.reshape(NX, ny, block, span), teacher,
    )
    term = (dot(hidden_both, gap_round.reshape(experts * block, span), ((0,), (0,))) / tok).astype(BF)
    chunk = NX * lanes
    grad, losses = kernel_call(
        functools.partial(grad_kernel, nz), 5,
        [shape((NX, sub, lanes), BF), shape((nr * ny, block, 128), F32)],
        [pltpu.VMEM((nz, sub, chunk), BF), pltpu.VMEM((2, steps, sub, chunk), BF)]
        + [pltpu.VMEM((2, steps - 1, sub, chunk), BF), pltpu.VMEM((sub, chunk), BF)]
        + [dma(2, steps, 2)] * 2 + [dma(steps)] * 2 + [dma(3)] * 2 + [dma(2 * ny - 1)] * 2 + [dma(steps + 2)],
        term, loss,
    )
    token_loss = jnp.sum(losses.reshape(nr, ny * block, 128), axis=(0, 2)) / width
    grad = grad.reshape(ff, lanes)[:, :blk].astype(F32)
    return token_loss, grad


def solution(mesh):
    dp = ("z", "x")
    in_specs = (
        P(dp, None),
        P(dp + ("col",), None),
        P(dp + ("col",), None),
        P(dp + ("col",), None, None, "row"),
        P(dp + ("col",), "row", None),
        P(None, dp, ("row", "col")),
        P(("row", "col"), dp),
    )
    out_specs = (P(dp), P(("row", "col"), dp))
    return jax.shard_map(
        on_device, mesh=split_mesh(mesh), in_specs=in_specs, out_specs=out_specs, check_vma=False
    )
```

```python
import functools

import jax
import jax.numpy as jnp
from jax import lax
from jax.experimental import pallas as pl
from jax.experimental.pallas import tpu as pltpu
from jax.sharding import Mesh, PartitionSpec as P

NX = 4
MESH = pl.DeviceIdType.MESH
F32 = jnp.float32
BF = jnp.bfloat16


def split_mesh(mesh):
    dp, row, col = mesh.devices.shape
    return Mesh(mesh.devices.reshape(dp // NX, NX, row, col), ("z", "x", "row", "col"))


def dot(a, b, dims):
    return lax.dot_general(a, b, (dims, ((), ())), preferred_element_type=F32)


def pad_lanes(a):
    lanes = a.shape[-1]
    wide = -(-lanes // 128) * 128
    return jnp.pad(a, [(0, 0)] * (a.ndim - 1) + [(0, wide - lanes)])


def here():
    return tuple(lax.axis_index(a) for a in ("z", "x", "row", "col"))


def remote(src, dst, send, recv, device):
    return pltpu.make_async_remote_copy(
        src_ref=src, dst_ref=dst, send_sem=send, recv_sem=recv, device_id=device, device_id_type=MESH
    )


def greet(devices):
    barrier = pltpu.get_barrier_semaphore()
    for device in devices:
        pl.semaphore_signal(barrier, inc=1, device_id=device, device_id_type=MESH)
    pl.semaphore_wait(barrier, len(devices))


def lanes_at(start, size):
    return pl.ds(pl.multiple_of(start * size, size), size)


def kernel_call(body, number, outs, scratch, *args, specs=None):
    whole = pl.BlockSpec(memory_space=pltpu.VMEM)
    return pl.pallas_call(
        body,
        out_shape=outs,
        in_specs=specs or [whole] * len(args),
        out_specs=[whole] * len(outs),
        scratch_shapes=scratch,
        compiler_params=pltpu.CompilerParams(
            collective_id=number, has_side_effects=True, vmem_limit_bytes=48 * 1024 * 1024
        ),
    )(*args)


def dma(*shape):
    return pltpu.SemaphoreType.DMA(shape)


def plane_steps(ny):
    steps = [(dx, dy) for dx in range(NX) for dy in range(ny) if dx or dy]
    far = lambda s: min(s[0], NX - s[0]) + min(s[1], ny - s[1])
    return sorted(steps, key=far, reverse=True)


def weights_kernel(nz, parts, shard, send, recv, own):
    z, x, r, y = here()
    per = nz // 2
    core = z // per
    plane_z = per * r + z % per
    moves = core != r
    peers = [(z, (x + d) % NX, r, y) for d in (1, 2, 3)]
    peers += [(plane_z, (x + d) % NX, core, y) for d in (1, 2, 3)]

    @pl.when(moves)
    def _():
        greet(peers + [(plane_z, x, core, y)])

    @pl.when(jnp.logical_not(moves))
    def _():
        greet(peers)

    slot = lanes_at(x, 128)
    copies = []
    for d in (2, 1, 3):
        to = (x + d) % NX
        for kind in (2, 0, 1):
            device = (plane_z, to, core, y) if kind == 2 else (z, to, r, y)
            copies.append(remote(parts.at[kind, to], shard.at[kind, :, slot], send.at[d, kind], recv.at[d, kind], device))
            copies[-1].start()
    for kind in (0, 1):
        copies.append(pltpu.make_async_copy(parts.at[kind, x], shard.at[kind, :, slot], own.at[kind]))
        copies[-1].start()
    down_own = remote(parts.at[2, x], shard.at[2, :, slot], send.at[0, 2], recv.at[0, 2], (plane_z, x, core, y))
    down_here = pltpu.make_async_copy(parts.at[2, x], shard.at[2, :, slot], own.at[2])

    @pl.when(moves)
    def _():
        down_own.start()
        down_own.wait()

    @pl.when(jnp.logical_not(moves))
    def _():
        down_here.start()
        down_here.wait()

    for copy in copies:
        copy.wait()


def tokens_kernel(nz, padded, mine, meta, plane, column, metas, xs, xr, ys, yr, cs, cr, zs, zr, ms, mr, own):
    z, x, r, y = here()
    up, down = (z + 1) % nz, (z + nz - 1) % nz
    ny = lax.axis_size("col")
    north, south = (y + 1) % ny, (y + ny - 1) % ny
    sibling = (z, x, 1 - r, y)
    greet(
        [(z, (x + d) % NX, r, y) for d in (1, 2, 3)]
        + [(z, x, r, north), (z, x, r, south), (up, x, r, y), (down, x, r, y), sibling]
    )
    rows, wide = padded.shape
    high, span = rows // 2, wide // 2
    quarter = span // 2
    mine_rows = pl.ds(pl.multiple_of(r * high, high), high)
    parity = y % 2
    held = lanes_at(parity, span)
    started = []

    def go(copy):
        copy.start()
        started.append(copy)
        return copy

    def z_step(s):
        half = mine.shape[1] // 2
        a, b = (z + nz - s + 1) % nz, (z + s - 1) % nz
        if s == 1:
            one, two, three, four = mine, mine, meta, meta
        else:
            one, two, three, four = column.at[a], column.at[b], metas.at[a], metas.at[b]
        to_a, to_b = column.at[a], column.at[b]
        if s == nz // 2:
            low, top = pl.ds(0, half), pl.ds(half, half)
            one, to_a, two, to_b = column.at[a, :, low], column.at[a, :, low], column.at[b, :, top], column.at[b, :, top]
        out = [
            go(remote(one, to_a, zs.at[0, s - 1], zr.at[0, s - 1], (up, x, r, y))),
            go(remote(two, to_b, zs.at[1, s - 1], zr.at[1, s - 1], (down, x, r, y))),
            go(remote(three, metas.at[a], ms.at[0, s - 1], mr.at[0, s - 1], (up, x, r, y))),
        ]
        if s < nz // 2:
            out.append(go(remote(four, metas.at[b], ms.at[1, s - 1], mr.at[1, s - 1], (down, x, r, y))))
        return out

    def arrived(copies):
        for copy in copies:
            copy.wait_recv()

    def x_step(d):
        device = (z, (x + d) % NX, r, y)
        return go(remote(padded.at[mine_rows, held], plane.at[x, mine_rows, held], xs.at[d - 1], xr.at[d - 1], device))

    from_sib, from_y = [], []

    def onward(d, copy):
        copy.wait_recv()
        source = (x + NX - d) % NX
        for side, device in ((0, (z, x, r, north)), (1, (z, x, r, south))):
            piece = plane.at[source, mine_rows, lanes_at(parity * 2 + side, quarter)]
            from_y.append((d, side, go(remote(piece, piece, ys.at[side, d - 1], yr.at[side, d - 1], device))))
        piece = plane.at[source, mine_rows, held]
        from_sib.append(go(remote(piece, piece, cs.at[0, d - 1], cr.at[0, d - 1], sibling)))

    first, third = x_step(1), x_step(3)
    ring = z_step(1)
    local = [
        pltpu.make_async_copy(padded, plane.at[x], own.at[0]),
        pltpu.make_async_copy(mine, column.at[z], own.at[1]),
        pltpu.make_async_copy(meta, metas.at[z], own.at[2]),
    ]
    for copy in local:
        copy.start()
    arrived(ring)
    ring = z_step(2)
    onward(1, first)
    second = x_step(2)
    onward(3, third)
    arrived(ring)
    ring = z_step(3)
    arrived(ring)
    ring = z_step(4)
    onward(2, second)
    for d, side, copy in from_y:
        copy.wait_recv()
        source = (x + NX - d) % NX
        piece = plane.at[source, mine_rows, lanes_at((1 - parity) * 2 + side, quarter)]
        from_sib.append(go(remote(piece, piece, cs.at[1 + side, d - 1], cr.at[1 + side, d - 1], sibling)))
    arrived(ring)
    arrived(from_sib)
    for copy in started:
        copy.wait_send()
    for copy in local:
        copy.wait()


def teacher_kernel(outgoing, inner, outer, back, w_in, w_out, got, act, part, other, total,
                   send, recv, fsend, frecv, csend, crecv, bsend, brecv, own):
    z, x, r, y = here()
    ny = lax.axis_size("col")
    steps = plane_steps(ny)[::-1]
    sibling = (z, x, 1 - r, y)
    greet([(z, (x + dx) % NX, r, (y + dy) % ny) for dx, dy in steps] + [sibling])
    steps = [(0, 0)] + steps
    me = x * ny + y
    half = outgoing.shape[2]
    keep, give = lanes_at(r, half), lanes_at(1 - r, half)
    near = len(steps) // 2
    groups = (range(near), range(near, len(steps)))
    local = pltpu.make_async_copy(outgoing.at[me], got.at[0, :, keep], own.at[0])
    local.start()
    loads = [pltpu.make_async_copy(inner, w_in, own.at[1]), pltpu.make_async_copy(outer, w_out, own.at[2])]
    sends, forwards, swaps, returns = {}, {}, {}, []

    def forward(k, src):
        forwards[k] = remote(src, got.at[k, :, keep], fsend.at[k], frecv.at[k], sibling)
        forwards[k].start()

    for k, (dx, dy) in enumerate(steps):
        if k:
            tx, ty = (x + dx) % NX, (y + dy) % ny
            sends[k] = remote(outgoing.at[tx * ny + ty], got.at[k, :, keep], send.at[k], recv.at[k], (z, tx, r, ty))
            sends[k].start()
        if k == near - 1:
            loads[0].start()
    loads[1].start()
    forward(0, outgoing.at[me])

    def finish(g):
        swaps[g].wait_recv()
        for k in groups[g]:
            dx, dy = steps[k]
            tx, ty = (x + NX - dx) % NX, (y + ny - dy) % ny
            value = (part[k, :, keep].astype(F32) + other[k].astype(F32)).astype(BF)
            if k:
                total[k] = value
                returns.append(remote(total.at[k], back.at[me], bsend.at[k], brecv.at[k], (z, tx, r, ty)))
                returns[-1].start()
            else:
                back[me] = value

    for g, group in enumerate(groups):
        slots = pl.ds(group[0], near)
        for k in group:
            if k:
                sends[k].wait_recv()
                forward(k, got.at[k, :, keep])
        if g == 0:
            local.wait()
            loads[0].wait()
        for k in group:
            forwards[k].wait_recv()
        rows = near * outgoing.shape[1]
        tile = w_in.shape[2] // 2

        @pl.loop(0, 2)
        def _(j):
            lhs = got[slots].reshape(rows, got.shape[2])
            cut = pl.ds(pl.multiple_of(j * tile, tile), tile)
            gate = jnp.dot(lhs, w_in[0, :, cut], preferred_element_type=F32)
            up = jnp.dot(lhs, w_in[1, :, cut], preferred_element_type=F32)
            act[:, cut] = (gate / (1.0 + jnp.exp(-gate)) * up).astype(BF)

        if g == 0:
            loads[1].wait()
        wide = half // 2

        def down(side):
            @pl.loop(0, 2)
            def _(j):
                cut = pl.ds(pl.multiple_of(side * half + j * wide, wide), wide)
                value = jnp.dot(act[...], w_out[:, cut], preferred_element_type=F32).astype(BF)
                part[slots, :, cut] = value.reshape(near, outgoing.shape[1], wide)

        down(1 - r)
        swaps[g] = remote(part.at[slots, :, give], other.at[slots], csend.at[g], crecv.at[g], sibling)
        swaps[g].start()
        down(r)
        finish(g)
    for copy in returns:
        copy.wait()
    for copy in list(sends.values()) + list(forwards.values()) + list(swaps.values()):
        copy.wait_send()


def ring_sum(n, i, up, down, ref, where, subs, came, leave, send, recv, copies):
    half = n // 2

    def go(way, s, u, src, dst):
        copy = remote(src, dst, send.at[way, s, u], recv.at[way, s, u], (up, down)[way])
        copy.start()
        copies[way, s, u] = copy

    for u, (whole, low, top) in enumerate(subs):
        for way, part in ((0, low), (1, top)):
            go(way, 0, u, ref.at[where((i + half) % n, part)], came.at[(way, 0) + part])
    yield
    for s in range(1, half):
        for u, (whole, low, top) in enumerate(subs):
            for way in (0, 1):
                d = (i + half - s) % n if way == 0 else (i + half + s) % n
                copies[way, s - 1, u].wait_recv()
                summed, plain = whole, None
                if s == 1:
                    summed, plain = (low, top) if way == 0 else (top, low)
                    leave[(way, 0) + plain] = ref[where(d, plain)]
                value = ref[where(d, summed)].astype(F32) + came[(way, s - 1) + summed].astype(F32)
                leave[(way, s - 1) + summed] = value.astype(BF)
                go(way, s, u, leave.at[(way, s - 1) + whole], came.at[(way, s) + whole])
        yield
    for u in range(len(subs)):
        for way in (0, 1):
            copies[way, half - 1, u].wait_recv()


def ring_gather(n, i, up, down, ref, where, whole, low, top, send, recv, copies):
    half = n // 2
    for s in range(half):
        for way, device in ((0, up), (1, down)):
            d = (i + n - s) % n if way == 0 else (i + s) % n
            if s:
                copies[way, s - 1].wait_recv()
            part = whole if s < half - 1 else (low, top)[way]
            piece = ref.at[where(d, part)]
            copies[way, s] = remote(piece, piece, send.at[way, s, 0], recv.at[way, s, 0], device)
            copies[way, s].start()
        yield
    for way in (0, 1):
        copies[way, half - 1].wait_recv()


def together(*rings):
    rings = list(rings)
    while rings:
        for ring in list(rings):
            try:
                next(ring)
            except StopIteration:
                rings.remove(ring)


def gap_kernel(nz, count, parts, teacher, gaps, loss, tcame, tleave, total, send, recv, *buffers):
    z, x, r, y = here()
    ny = lax.axis_size("col")
    up, down = ((z + 1) % nz, x, r, y), ((z + nz - 1) % nz, x, r, y)
    east, west = (z, (x + 1) % NX, r, y), (z, (x + NX - 1) % NX, r, y)
    north, south = (z, x, r, (y + 1) % ny), (z, x, r, (y + ny - 1) % ny)
    greet([east, west, north, south, up, down])
    span = teacher.shape[2]
    wing = span // count
    every = slice(None)
    copies = [{} for _ in range(4 * count + 1)]

    def sems(k):
        return send.at[k], recv.at[k], copies[k]

    def trio(axis_size):
        return (pl.ds(0, axis_size),), (pl.ds(0, axis_size // 2),), (pl.ds(axis_size // 2, axis_size // 2),)

    def lanes(start, size):
        return tuple((every, pl.ds(start + o, s)) for o, s in ((0, size), (0, size // 2), (size // 2, size // 2)))

    along_x, along_y = (NX, x, east, west), (ny, y, north, south)

    def flow(f):
        start = f * wing
        cut = pl.ds(start, wing)
        came, leave, mid, came2, leave2 = buffers[5 * f:5 * f + 5]
        x_first = f < count // 2
        one, two = (along_x, along_y) if x_first else (along_y, along_x)

        def outer(d, p):
            return (d,) + p + (every, cut) if x_first else p + (d, every, cut)

        def inner(d, p):
            return (x, d) + p if x_first else (d, y) + p

        yield from ring_sum(*one, parts, outer, [trio(two[0])], came, leave, *sems(4 * f))
        last = one[0] // 2 - 1
        kept = parts[x, :, :, cut] if x_first else parts[:, y, :, cut]
        mid[...] = (kept.astype(F32) + came[0, last].astype(F32) + came[1, last].astype(F32)).astype(BF)
        yield from ring_sum(*two, mid, lambda d, p: (d,) + p, [lanes(0, wing)], came2, leave2, *sems(4 * f + 1))
        last = two[0] // 2 - 1
        student = mid[two[1]].astype(F32) + came2[0, last].astype(F32) + came2[1, last].astype(F32)
        last = nz // 2 - 1
        taught = teacher[z, :, cut].astype(F32) + tcame[0, last, :, cut].astype(F32) + tcame[1, last, :, cut].astype(F32)
        gap = student - taught
        gaps[x, y, :, cut] = gap.astype(BF)
        total[:, cut] = gap
        yield from ring_gather(*two, gaps, inner, *lanes(start, wing), *sems(4 * f + 2))
        yield from ring_gather(*one, gaps, outer, *trio(two[0]), *sems(4 * f + 3))

    teach = ring_sum(nz, z, up, down, teacher, lambda d, p: (d,) + p, [lanes(0, span)], tcame, tleave, *sems(4 * count))
    half = count // 2
    flows = [flow(k) for pair in zip(range(half), range(half, count)) for k in pair]
    together(teach, *flows)
    squares = jnp.zeros(loss.shape, F32)
    for tile in range(span // 128):
        value = total[:, pl.ds(tile * 128, 128)]
        squares += value * value
    loss[...] = squares
    for group in copies:
        for copy in group.values():
            copy.wait_send()


def grad_kernel(nz, term, loss, grad, losses, chunks, came, leave, total, send, recv, csend, crecv, xsend, xrecv, lsend, lrecv, own):
    z, x, r, y = here()
    ny = lax.axis_size("col")
    up, down = ((z + 1) % nz, x, r, y), ((z + nz - 1) % nz, x, r, y)
    sibling = (z, x, 1 - r, y)
    mates = [(z, x, r, (y + d) % ny) for d in range(1, ny)] + [(z, x, 1 - r, (y + d) % ny) for d in range(ny)]
    across = [(d, (x + d) % NX) for d in (2, 1, 3)]
    greet([up, down] + mates + [(z, tx, r, y) for _, tx in across])
    rows, span = chunks.shape[1], chunks.shape[2]
    keep = pl.ds(pl.multiple_of(r * rows, rows), rows)
    give = pl.ds(pl.multiple_of((1 - r) * rows, rows), rows)
    per = nz // 2
    local, swaps = [], []
    for q in range(per):
        columns = pl.ds(q * span, span)
        swaps.append(remote(term.at[give, columns], chunks.at[r * per + q], csend.at[q], crecv.at[q], sibling))
        swaps[-1].start()
        local.append(pltpu.make_async_copy(term.at[keep, columns], chunks.at[r * per + q], own.at[q]))
        local[-1].start()
    slot = r * ny + y
    local.append(pltpu.make_async_copy(loss, losses.at[slot], own.at[per]))
    local[-1].start()
    tells = []
    for k, device in enumerate(mates):
        tells.append(remote(loss, losses.at[slot], lsend.at[k], lrecv.at[k], device))
        tells[-1].start()
    for copy in local:
        copy.wait()
    for copy in swaps:
        copy.wait_recv()
    subs = []
    for u in (0, 1):
        band = pl.ds(u * (rows // 2), rows // 2)
        subs.append(((band, pl.ds(0, span)), (band, pl.ds(0, span // 2)), (band, pl.ds(span // 2, span // 2))))
    ring = {}
    together(ring_sum(nz, z, up, down, chunks, lambda d, p: (d,) + p, subs, came, leave, send, recv, ring))
    value = chunks[z].astype(F32) + came[0, per - 1].astype(F32) + came[1, per - 1].astype(F32)
    total[...] = value.astype(BF)
    lanes = span // NX
    outs = []
    for d, tx in across:
        outs.append(remote(total.at[:, lanes_at(tx, lanes)], grad.at[x], xsend.at[d - 1], xrecv.at[d - 1], (z, tx, r, y)))
        outs[-1].start()
    last = pltpu.make_async_copy(total.at[:, lanes_at(x, lanes)], grad.at[x], own.at[per + 1])
    last.start()
    last.wait()
    for copy in outs + tells:
        copy.wait()
    for copy in swaps + list(ring.values()):
        copy.wait_send()


def routing(routes, weights, plane, ny, cap):
    nz, block, _ = routes.shape
    experts = NX * ny
    local = routes - plane * experts
    ids = jnp.arange(experts, dtype=jnp.int32)
    hit = local[..., None] == ids
    named = jnp.any(hit, axis=2)
    weight = jnp.sum(jnp.where(hit, weights[..., None], 0.0), axis=2)
    count = named.astype(jnp.int32)
    slot = jnp.cumsum(count, axis=1) - count
    place = named[..., None] & (slot[..., None] == jnp.arange(cap, dtype=jnp.int32))
    same = jnp.eye(nz, dtype=bool)
    full = place[:, :, :, None, :] & same[:, None, None, :, None]
    combine = jnp.where(full, weight[:, :, :, None, None], 0.0)
    rows = experts * nz * cap
    return full.reshape(nz * block, rows).astype(BF), combine.reshape(nz * block, rows)


def on_device(tokens, routes, route_weights, teacher_in, teacher_out, student_in, student_out):
    nz, nr, ny = lax.axis_size("z"), lax.axis_size("row"), lax.axis_size("col")
    z, x, r, y = here()
    tok, width = tokens.shape
    block, top = routes.shape
    blk = student_in.shape[1]
    ff = student_in.shape[2]
    sub = ff // NX
    half = width // nr
    experts = NX * ny
    cap = max(2, 3 * block * top // (2 * nz * experts))
    blocks = nz * NX
    shape = jax.ShapeDtypeStruct

    parts = jnp.concatenate([jnp.swapaxes(student_in, 1, 2), student_out[None]], axis=0)
    parts = pad_lanes(parts)
    lanes = parts.shape[-1]
    wide = blocks * lanes
    (shard,) = kernel_call(
        functools.partial(weights_kernel, nz), 0,
        [shape((3, sub, NX * lanes), BF)],
        [dma(4, 3), dma(4, 3), dma(3)],
        parts.reshape(3, NX, sub, lanes),
    )
    padded = pad_lanes(tokens.reshape(tok, blocks, blk)).reshape(tok, wide)
    mine = lax.dynamic_slice(tokens, (y * block, r * half), (block, half))
    meta = jnp.concatenate([routes.astype(F32), route_weights], axis=1)
    meta = jnp.pad(meta, ((0, 0), (0, 128 - 2 * top)))
    shard, mine = lax.optimization_barrier((shard, mine))
    student = lax.all_gather(shard, "z", axis=2, tiled=True)

    steps = nz // 2
    plane_tokens, column, metas = kernel_call(
        functools.partial(tokens_kernel, nz), 1,
        [shape((NX, tok, wide), BF), shape((nz, block, half), BF), shape((nz, block, 128), F32)],
        [dma(3), dma(3), dma(2, 3), dma(2, 3), dma(3, 3), dma(3, 3)] + [dma(2, steps)] * 4 + [dma(3)],
        padded, mine, meta,
    )
    routes_z = metas[:, :, :top].astype(jnp.int32)
    place, combine = routing(routes_z, metas[:, :, top:2 * top], z, ny, cap)
    slots = nz * cap
    outgoing = dot(place, column.reshape(nz * block, half), ((0,), (0,))).astype(BF)
    hid = teacher_in.shape[3]
    whole, far = pl.BlockSpec(memory_space=pltpu.VMEM), pl.BlockSpec(memory_space=pl.ANY)
    buffers = [(2, width, hid), (hid, width), (experts, slots, width), (experts // 2 * slots, hid)]
    buffers += [(experts, slots, width)] + [(experts, slots, half)] * 2
    (back,) = kernel_call(
        teacher_kernel, 2,
        [shape((experts, slots, half), BF)],
        [pltpu.VMEM(b, BF) for b in buffers] + [dma(experts)] * 4 + [dma(2)] * 2 + [dma(experts)] * 2 + [dma(3)],
        outgoing.reshape(experts, slots, half), teacher_in[0], teacher_out[0],
        specs=[whole, far, far],
    )
    back = back.reshape(experts * slots, half)
    high = combine.astype(BF)
    low = (combine - high.astype(F32)).astype(BF)
    teacher = dot(jnp.concatenate([high, low], axis=1), jnp.concatenate([back, back], axis=0), ((1,), (0,))).astype(BF)
    teacher = pad_lanes(teacher.reshape(nz, block, blocks // nr, blk)).reshape(nz, block, wide // nr)

    plane_tokens = plane_tokens.reshape(NX * tok, wide)
    gate = dot(plane_tokens, student[0], ((1,), (1,)))
    up = dot(plane_tokens, student[1], ((1,), (1,)))
    hidden = (jax.nn.silu(gate) * up).astype(BF)
    hidden_both = lax.all_gather(hidden, "row", axis=1, tiled=True)
    span = wide // nr
    y_part = sum(dot(hidden_both[:, i * sub:(i + 1) * sub], student[2, :, i * span:(i + 1) * span], ((1,), (0,))) for i in range(nr)).astype(BF)
    count = 4
    wing = span // count
    buffers = [(2, steps, block, span), (2, steps - 1, block, span)]
    flows = []
    for f in range(count):
        one, two = (NX, ny) if f < count // 2 else (ny, NX)
        flows += [(2, one // 2, two, block, wing), (2, one // 2 - 1, two, block, wing), (two, block, wing)]
        flows += [(2, two // 2, block, wing), (2, two // 2 - 1, block, wing)]
    gap_round, loss = kernel_call(
        functools.partial(gap_kernel, nz, count), 4,
        [shape((NX, ny, block, span), BF), shape((block, 128), F32)],
        [pltpu.VMEM(b, BF) for b in buffers] + [pltpu.VMEM((block, span), F32)] + [dma(4 * count + 1, 2, steps, 1)] * 2
        + [pltpu.VMEM(b, BF) for b in flows],
        y_part.reshape(NX, ny, block, span), teacher,
    )
    term = (dot(hidden_both, gap_round.reshape(experts * block, span), ((0,), (0,))) / tok).astype(BF)
    chunk = NX * lanes
    grad, losses = kernel_call(
        functools.partial(grad_kernel, nz), 5,
        [shape((NX, sub, lanes), BF), shape((nr * ny, block, 128), F32)],
        [pltpu.VMEM((nz, sub, chunk), BF), pltpu.VMEM((2, steps, sub, chunk), BF)]
        + [pltpu.VMEM((2, steps - 1, sub, chunk), BF), pltpu.VMEM((sub, chunk), BF)]
        + [dma(2, steps, 2)] * 2 + [dma(steps)] * 2 + [dma(3)] * 2 + [dma(2 * ny - 1)] * 2 + [dma(steps + 2)],
        term, loss,
    )
    token_loss = jnp.sum(losses.reshape(nr, ny * block, 128), axis=(0, 2)) / width
    grad = grad.reshape(ff, lanes)[:, :blk].astype(F32)
    return token_loss, grad


def solution(mesh):
    dp = ("z", "x")
    in_specs = (
        P(dp, None),
        P(dp + ("col",), None),
        P(dp + ("col",), None),
        P(dp + ("col",), None, None, "row"),
        P(dp + ("col",), "row", None),
        P(None, dp, ("row", "col")),
        P(("row", "col"), dp),
    )
    out_specs = (P(dp), P(("row", "col"), dp))
    return jax.shard_map(
        on_device, mesh=split_mesh(mesh), in_specs=in_specs, out_specs=out_specs, check_vma=False
    )
```

```python
import functools

import jax
import jax.numpy as jnp
from jax import lax
from jax.experimental import pallas as pl
from jax.experimental.pallas import tpu as pltpu
from jax.sharding import Mesh, PartitionSpec as P

NX = 4
MESH = pl.DeviceIdType.MESH
F32 = jnp.float32
BF = jnp.bfloat16


def split_mesh(mesh):
    dp, row, col = mesh.devices.shape
    return Mesh(mesh.devices.reshape(dp // NX, NX, row, col), ("z", "x", "row", "col"))


def dot(a, b, dims):
    return lax.dot_general(a, b, (dims, ((), ())), preferred_element_type=F32)


def pad_lanes(a):
    lanes = a.shape[-1]
    wide = -(-lanes // 128) * 128
    return jnp.pad(a, [(0, 0)] * (a.ndim - 1) + [(0, wide - lanes)])


def here():
    return tuple(lax.axis_index(a) for a in ("z", "x", "row", "col"))


def remote(src, dst, send, recv, device):
    return pltpu.make_async_remote_copy(
        src_ref=src, dst_ref=dst, send_sem=send, recv_sem=recv, device_id=device, device_id_type=MESH
    )


def greet(devices):
    barrier = pltpu.get_barrier_semaphore()
    for device in devices:
        pl.semaphore_signal(barrier, inc=1, device_id=device, device_id_type=MESH)
    pl.semaphore_wait(barrier, len(devices))


def lanes_at(start, size):
    return pl.ds(pl.multiple_of(start * size, size), size)


def kernel_call(body, number, outs, scratch, *args, specs=None, out_specs=None):
    whole = pl.BlockSpec(memory_space=pltpu.VMEM)
    return pl.pallas_call(
        body,
        out_shape=outs,
        in_specs=specs or [whole] * len(args),
        out_specs=out_specs or [whole] * len(outs),
        scratch_shapes=scratch,
        compiler_params=pltpu.CompilerParams(
            collective_id=number, has_side_effects=True, vmem_limit_bytes=56 * 1024 * 1024
        ),
    )(*args)


def dma(*shape):
    return pltpu.SemaphoreType.DMA(shape)


def plane_steps(ny):
    steps = [(dx, dy) for dx in range(NX) for dy in range(ny) if dx or dy]
    far = lambda s: min(s[0], NX - s[0]) + min(s[1], ny - s[1])
    return sorted(steps, key=far, reverse=True)


def token_gather(padded, plane, xs, xr, ys, yr, cs, cr, own, started):
    z, x, r, y = here()
    ny = lax.axis_size("col")
    north, south = (y + 1) % ny, (y + ny - 1) % ny
    sibling = (z, x, 1 - r, y)
    rows, wide = padded.shape
    high, span = rows // 2, wide // 2
    quarter = span // 2
    mine_rows = pl.ds(pl.multiple_of(r * high, high), high)
    parity = y % 2
    held = lanes_at(parity, span)

    def go(copy):
        copy.start()
        started.append(copy)
        return copy

    def x_step(d):
        device = (z, (x + d) % NX, r, y)
        return go(remote(padded.at[mine_rows, held], plane.at[x, mine_rows, held], xs.at[d - 1], xr.at[d - 1], device))

    from_sib, from_y = [], []

    def onward(d, copy):
        copy.wait_recv()
        source = (x + NX - d) % NX
        for side, device in ((0, (z, x, r, north)), (1, (z, x, r, south))):
            piece = plane.at[source, mine_rows, lanes_at(parity * 2 + side, quarter)]
            from_y.append((d, side, go(remote(piece, piece, ys.at[side, d - 1], yr.at[side, d - 1], device))))
        piece = plane.at[source, mine_rows, held]
        from_sib.append(go(remote(piece, piece, cs.at[0, d - 1], cr.at[0, d - 1], sibling)))

    def inward():
        while from_y:
            d, side, copy = from_y.pop(0)
            copy.wait_recv()
            source = (x + NX - d) % NX
            piece = plane.at[source, mine_rows, lanes_at((1 - parity) * 2 + side, quarter)]
            from_sib.append(go(remote(piece, piece, cs.at[1 + side, d - 1], cr.at[1 + side, d - 1], sibling)))

    first, third = x_step(1), x_step(3)
    local = pltpu.make_async_copy(padded, plane.at[x], own)
    local.start()
    yield
    onward(1, first)
    onward(3, third)
    second = x_step(2)
    yield
    inward()
    onward(2, second)
    yield
    inward()
    for copy in from_sib:
        copy.wait_recv()
    local.wait()


def block_gather(nz, mine, meta, column, metas, zs, zr, ms, mr, own, started):
    z, x, r, y = here()
    up, down = (z + 1) % nz, (z + nz - 1) % nz
    half = mine.shape[1] // 2

    def go(copy):
        copy.start()
        started.append(copy)
        return copy

    local = [pltpu.make_async_copy(mine, column.at[z], own.at[0]), pltpu.make_async_copy(meta, metas.at[z], own.at[1])]
    for copy in local:
        copy.start()
    ring = []
    for s in range(1, nz // 2 + 1):
        for copy in ring:
            copy.wait_recv()
        a, b = (z + nz - s + 1) % nz, (z + s - 1) % nz
        one, two, three, four = (mine, mine, meta, meta) if s == 1 else (column.at[a], column.at[b], metas.at[a], metas.at[b])
        to_a, to_b = column.at[a], column.at[b]
        if s == nz // 2:
            low, top = pl.ds(0, half), pl.ds(half, half)
            one, to_a, two, to_b = column.at[a, :, low], column.at[a, :, low], column.at[b, :, top], column.at[b, :, top]
        ring = [
            go(remote(one, to_a, zs.at[0, s - 1], zr.at[0, s - 1], (up, x, r, y))),
            go(remote(two, to_b, zs.at[1, s - 1], zr.at[1, s - 1], (down, x, r, y))),
            go(remote(three, metas.at[a], ms.at[0, s - 1], mr.at[0, s - 1], (up, x, r, y))),
        ]
        if s < nz // 2:
            ring.append(go(remote(four, metas.at[b], ms.at[1, s - 1], mr.at[1, s - 1], (down, x, r, y))))
        yield
    for copy in ring:
        copy.wait_recv()
    for copy in local:
        copy.wait()


def place_rows(nz, cap, column, metas, outgoing, weighted):
    z = lax.axis_index("z")
    block, half = column.shape[1], column.shape[2]
    experts = outgoing.shape[0]
    top = metas.shape[1] // 2
    count = nz * block
    named = jnp.concatenate([metas[b, :top, :block] for b in range(nz)], axis=1)
    weights = jnp.concatenate([metas[b, top:, :block] for b in range(nz)], axis=1)
    ids = (z * experts + lax.broadcasted_iota(jnp.int32, (experts, 1), 0)).astype(F32)
    hit = jnp.zeros((experts, count), F32)
    weight = jnp.zeros((experts, count), F32)
    for k in range(top):
        hit += jnp.where(named[k:k + 1] == ids, 1.0, 0.0)
        weight += jnp.where(named[k:k + 1] == ids, weights[k:k + 1], 0.0)
    before, after = lax.broadcasted_iota(jnp.int32, (count, count), 0), lax.broadcasted_iota(jnp.int32, (count, count), 1)
    earlier = jnp.where((before < after) & (before // block == after // block), 1.0, 0.0).astype(BF)
    slot = jnp.dot(hit.astype(BF), earlier, preferred_element_type=F32)
    lane = lax.broadcasted_iota(jnp.int32, (nz, count), 1) // block
    inside = jnp.where(lane == lax.broadcasted_iota(jnp.int32, (nz, count), 0), 1.0, 0.0)
    rows = column[...].reshape(count, half)
    for s in range(cap):
        chosen = jnp.where(slot == float(s), hit, 0.0)
        placing = (chosen[:, None, :] * inside[None]).reshape(experts * nz, count).astype(BF)
        value = jnp.dot(placing, rows, preferred_element_type=F32).astype(BF)
        outgoing[:, s * nz:(s + 1) * nz, :] = value.reshape(experts, nz, half)
        chosen = jnp.where(slot == float(s), weight, 0.0)
        weighted[s] = (chosen[:, None, :] * inside[None]).reshape(experts * nz, count)


def weigh_rows(nz, cap, weighted, back, teacher, blk):
    experts, half = back.shape[0], back.shape[2]
    count = weighted.shape[2]
    total = jnp.zeros((count, half), F32)
    for s in range(cap):
        rows = back[:, s * nz:(s + 1) * nz, :].reshape(experts * nz, half)
        value = weighted[s]
        high = value.astype(BF)
        low = (value - high.astype(F32)).astype(BF)
        for term in (high, low):
            total += lax.dot_general(term, rows, (((0,), (0,)), ((), ())), preferred_element_type=F32)
    lanes = -(-blk // 128) * 128
    empty = jnp.zeros((count, lanes - blk), F32)
    for b in range(half // blk):
        piece = jnp.concatenate([total[:, b * blk:(b + 1) * blk], empty], axis=1).astype(BF)
        teacher[:, :, b * lanes:(b + 1) * lanes] = piece.reshape(nz, count // nz, lanes)


def front_kernel(nz, cap, blk, parts, mine, meta, padded, inner, outer, hidden, student_down, teacher,
                 student, plane, metas, weighted, back, w_in, w_out, column, outgoing, got, act, part, other, total,
                 ws, wr, rs, rr, zs, zr, ms, mr, xs, xr, ys, yr, cs, cr, send, recv, fsend, frecv, csend, crecv, bsend, brecv, own):
    z, x, r, y = here()
    ny = lax.axis_size("col")
    steps = plane_steps(ny)[::-1]
    sibling = (z, x, 1 - r, y)
    up, down_z = ((z + 1) % nz, x, r, y), ((z + nz - 1) % nz, x, r, y)
    per = nz // 2
    core = z // per
    plane_z = per * r + z % per
    moves = core != r
    loads = [pltpu.make_async_copy(inner, w_in, own.at[1]), pltpu.make_async_copy(outer, w_out, own.at[2])]
    for copy in loads:
        copy.start()
    peers = [(z, (x + dx) % NX, r, (y + dy) % ny) for dx, dy in steps]
    peers += [sibling, up, down_z] + [(plane_z, (x + d) % NX, core, y) for d in (1, 2, 3)]

    @pl.when(moves)
    def _():
        greet(peers + [(plane_z, x, core, y)])

    @pl.when(jnp.logical_not(moves))
    def _():
        greet(peers)

    started = []
    blocks = block_gather(nz, mine, meta, column, metas, zs, zr, ms, mr, own.at[pl.ds(3, 2)], started)
    tokens = token_gather(padded, plane, xs, xr, ys, yr, cs, cr, own.at[5], started)
    next(blocks)

    span = NX * 128
    exchange = [[], [], []]
    homes = [student.at[0], student.at[1], student_down]
    lane = pl.ds(pl.multiple_of(z * span + x * 128, 128), 128)
    lane_down = pl.ds(pl.multiple_of(plane_z * span + x * 128, 128), 128)
    for kind in (0, 1, 2):
        for d in (2, 1, 3):
            to = (x + d) % NX
            device, cut = ((plane_z, to, core, y), lane_down) if kind == 2 else ((z, to, r, y), lane)
            copy = remote(parts.at[kind, to], homes[kind].at[:, cut], ws.at[d, kind], wr.at[d, kind], device)
            copy.start()
            started.append(copy)
            exchange[kind].append(copy)
    down_own = remote(parts.at[2, x], student_down.at[:, lane_down], ws.at[0, 2], wr.at[0, 2], (plane_z, x, core, y))
    down_here = pltpu.make_async_copy(parts.at[2, x], student_down.at[:, lane], own.at[6])

    @pl.when(moves)
    def _():
        down_own.start()

    @pl.when(jnp.logical_not(moves))
    def _():
        down_here.start()

    local = [pltpu.make_async_copy(parts.at[k, x], student.at[k, :, lane], own.at[7 + k]) for k in (0, 1)]
    for copy in local:
        copy.start()
    next(tokens)

    def chunk(d, p):
        return (slice(None), pl.ds(pl.multiple_of(d * span + p[0], 128), p[1]))

    rings = [{}, {}, {}]
    gathers = [
        ring_gather(nz, z, up, down_z, homes[kind], chunk, (0, span), (0, span // 2), (span // 2, span // 2),
                    rs.at[kind], rr.at[kind], rings[kind])
        for kind in range(3)
    ]

    def serve(*kinds):
        for kind in kinds:
            next(gathers[kind], None)

    for _ in range(per - 1):
        next(blocks)
    for copy in local:
        copy.wait()
    for kind in (0, 1):
        for copy in exchange[kind]:
            copy.wait_recv()
        next(gathers[kind])
    for copy in exchange[2]:
        copy.wait_recv()

    @pl.when(moves)
    def _():
        down_own.wait()

    @pl.when(jnp.logical_not(moves))
    def _():
        down_here.wait()

    next(tokens)
    next(blocks, None)

    place_rows(nz, cap, column, metas, outgoing, weighted)
    steps = [(0, 0)] + steps
    me = x * ny + y
    half = outgoing.shape[2]
    keep, give = lanes_at(r, half), lanes_at(1 - r, half)
    near = len(steps) // 2
    groups = (range(near), range(near, len(steps)))
    sends, forwards, swaps, returns = {}, {}, {}, []

    def forward(k, src):
        forwards[k] = remote(src, got.at[k, :, keep], fsend.at[k], frecv.at[k], sibling)
        forwards[k].start()

    for k, (dx, dy) in enumerate(steps):
        if k:
            tx, ty = (x + dx) % NX, (y + dy) % ny
            sends[k] = remote(outgoing.at[tx * ny + ty], got.at[k, :, keep], send.at[k], recv.at[k], (z, tx, r, ty))
            sends[k].start()
    own_rows = pltpu.make_async_copy(outgoing.at[me], got.at[0, :, keep], own.at[0])
    own_rows.start()
    forward(0, outgoing.at[me])
    serve(0, 1)

    def finish(g):
        swaps[g].wait_recv()
        for k in groups[g]:
            dx, dy = steps[k]
            tx, ty = (x + NX - dx) % NX, (y + ny - dy) % ny
            value = (part[k, :, keep].astype(F32) + other[k].astype(F32)).astype(BF)
            if k:
                total[k] = value
                returns.append(remote(total.at[k], back.at[me], bsend.at[k], brecv.at[k], (z, tx, r, ty)))
                returns[-1].start()
            else:
                back[me] = value

    for g, group in enumerate(groups):
        slots = pl.ds(group[0], near)
        for k in group:
            if k:
                sends[k].wait_recv()
                forward(k, got.at[k, :, keep])
        if g == 0:
            own_rows.wait()
            loads[0].wait()
        for k in group:
            forwards[k].wait_recv()
        rows = near * outgoing.shape[1]
        tile = w_in.shape[2] // 2

        @pl.loop(0, 2)
        def _(j):
            lhs = got[slots].reshape(rows, got.shape[2])
            cut = pl.ds(pl.multiple_of(j * tile, tile), tile)
            gate = jnp.dot(lhs, w_in[0, :, cut], preferred_element_type=F32)
            up_part = jnp.dot(lhs, w_in[1, :, cut], preferred_element_type=F32)
            act[:, cut] = (gate / (1.0 + jnp.exp(-gate)) * up_part).astype(BF)

        if g == 0:
            loads[1].wait()
        wide = half // 2

        def down(side):
            @pl.loop(0, 2)
            def _(j):
                cut = pl.ds(pl.multiple_of(side * half + j * wide, wide), wide)
                value = jnp.dot(act[...], w_out[:, cut], preferred_element_type=F32).astype(BF)
                part[slots, :, cut] = value.reshape(near, outgoing.shape[1], wide)

        down(1 - r)
        swaps[g] = remote(part.at[slots, :, give], other.at[slots], csend.at[g], crecv.at[g], sibling)
        swaps[g].start()
        down(r)
        if g == 0:
            serve(0, 1)
        finish(g)
        next(tokens, None)
        if g == 1:
            serve(0, 1, 2)

    serve(0, 1)
    tok = plane.shape[1]
    for i in range(NX // 2):
        rows = plane[2 * i:2 * i + 2].reshape(2 * tok, plane.shape[2])
        gate = lax.dot_general(rows, student[0], (((1,), (1,)), ((), ())), preferred_element_type=F32)
        up_part = lax.dot_general(rows, student[1], (((1,), (1,)), ((), ())), preferred_element_type=F32)
        hidden[2 * i * tok:2 * (i + 1) * tok] = (gate / (1.0 + jnp.exp(-gate)) * up_part).astype(BF)
        serve(2)
    for copy in returns:
        copy.wait_recv()
    weigh_rows(nz, cap, weighted, back, teacher, blk)
    serve(2)
    serve(2)
    for copy in started + returns + list(sends.values()) + list(forwards.values()) + list(swaps.values()):
        copy.wait_send()
    for ring in rings:
        for copy in ring.values():
            copy.wait_send()


def ring_sum(n, i, up, down, ref, where, subs, came, leave, send, recv, copies):
    half = n // 2

    def go(way, s, u, src, dst):
        copy = remote(src, dst, send.at[way, s, u], recv.at[way, s, u], (up, down)[way])
        copy.start()
        copies[way, s, u] = copy

    for u, (whole, low, top) in enumerate(subs):
        for way, part in ((0, low), (1, top)):
            go(way, 0, u, ref.at[where((i + half) % n, part)], came.at[(way, 0) + part])
    yield
    for s in range(1, half):
        for u, (whole, low, top) in enumerate(subs):
            for way in (0, 1):
                d = (i + half - s) % n if way == 0 else (i + half + s) % n
                copies[way, s - 1, u].wait_recv()
                summed, plain = whole, None
                if s == 1:
                    summed, plain = (low, top) if way == 0 else (top, low)
                    leave[(way, 0) + plain] = ref[where(d, plain)]
                value = ref[where(d, summed)].astype(F32) + came[(way, s - 1) + summed].astype(F32)
                leave[(way, s - 1) + summed] = value.astype(BF)
                go(way, s, u, leave.at[(way, s - 1) + whole], came.at[(way, s) + whole])
        yield
    for u in range(len(subs)):
        for way in (0, 1):
            copies[way, half - 1, u].wait_recv()


def ring_gather(n, i, up, down, ref, where, whole, low, top, send, recv, copies):
    half = n // 2
    for s in range(half):
        for way, device in ((0, up), (1, down)):
            d = (i + n - s) % n if way == 0 else (i + s) % n
            if s:
                copies[way, s - 1].wait_recv()
            part = whole if s < half - 1 else (low, top)[way]
            piece = ref.at[where(d, part)]
            copies[way, s] = remote(piece, piece, send.at[way, s, 0], recv.at[way, s, 0], device)
            copies[way, s].start()
        yield
    for way in (0, 1):
        copies[way, half - 1].wait_recv()


def together(*rings):
    rings = list(rings)
    while rings:
        for ring in list(rings):
            try:
                next(ring)
            except StopIteration:
                rings.remove(ring)


def tail_kernel(nz, count, tok, hidden, weights, teacher, grad, losses, hid, w_out, tcame, tleave, chunks, give, came, leave, total, loss,
                send, recv, zsend, zrecv, csend, crecv, hsend, hrecv, xsend, xrecv, lsend, lrecv, own, *buffers):
    z, x, r, y = here()
    ny = lax.axis_size("col")
    up, down = ((z + 1) % nz, x, r, y), ((z + nz - 1) % nz, x, r, y)
    east, west = (z, (x + 1) % NX, r, y), (z, (x + NX - 1) % NX, r, y)
    north, south = (z, x, r, (y + 1) % ny), (z, x, r, (y + ny - 1) % ny)
    sibling = (z, x, 1 - r, y)
    mates = [(z, x, r, (y + d) % ny) for d in range(1, ny)] + [(z, x, 1 - r, (y + d) % ny) for d in range(ny)]
    across = [(d, (x + d) % NX) for d in (2, 1, 3)]
    load = pltpu.make_async_copy(weights, w_out, own.at[0])
    load.start()
    keep_hid = pltpu.make_async_copy(hidden, hid.at[r], own.at[1])
    keep_hid.start()
    greet([up, down] + mates + [(z, tx, r, y) for _, tx in across])
    span = teacher.shape[2]
    wing = span // count
    per = nz // 2
    every = slice(None)
    copies = [{} for _ in range(4 * count + 1)]
    swap_hid = remote(hidden, hid.at[r], hsend, hrecv, sibling)
    swap_hid.start()
    loss[...] = jnp.zeros_like(loss)

    def sems(k):
        return send.at[k], recv.at[k], copies[k]

    def trio(axis_size):
        return (pl.ds(0, axis_size),), (pl.ds(0, axis_size // 2),), (pl.ds(axis_size // 2, axis_size // 2),)

    def lanes(size):
        return tuple((every, pl.ds(o, s)) for o, s in ((0, size), (0, size // 2), (size // 2, size // 2)))

    along_x, along_y = (NX, x, east, west), (ny, y, north, south)
    swaps = []

    def flow(f):
        cut = pl.ds(f * wing, wing)
        parts, gaps, scame, sleave, mid, came2, leave2 = buffers[7 * f:7 * f + 7]
        x_first = f < count // 2
        one, two = (along_x, along_y) if x_first else (along_y, along_x)

        def outer(d, p):
            return (d,) + p if x_first else p + (d,)

        def inner(d, p):
            return (x, d) + p if x_first else (d, y) + p

        @pl.loop(0, NX)
        def _(i):
            rows = pl.ds(pl.multiple_of(i * tok, tok), tok)
            value = jnp.dot(hid[0, rows], w_out[:, cut], preferred_element_type=F32)
            value += jnp.dot(hid[1, rows], w_out[:, pl.ds(span + f * wing, wing)], preferred_element_type=F32)
            parts[i] = value.astype(BF).reshape(parts.shape[1:])

        yield from ring_sum(*one, parts, outer, [trio(two[0])], scame, sleave, *sems(4 * f))
        last = one[0] // 2 - 1
        kept = parts[x] if x_first else parts[:, y]
        mid[...] = (kept.astype(F32) + scame[0, last].astype(F32) + scame[1, last].astype(F32)).astype(BF)
        yield from ring_sum(*two, mid, lambda d, p: (d,) + p, [lanes(wing)], came2, leave2, *sems(4 * f + 1))
        last = two[0] // 2 - 1
        student = mid[two[1]].astype(F32) + came2[0, last].astype(F32) + came2[1, last].astype(F32)
        taught = teacher[z, :, cut].astype(F32) + tcame[0, per - 1, :, cut].astype(F32) + tcame[1, per - 1, :, cut].astype(F32)
        gap = student - taught
        gaps[x, y] = gap.astype(BF)
        square = gap * gap
        loss[...] += sum(square[:, t * 128:(t + 1) * 128] for t in range(wing // 128))
        yield from ring_gather(*two, gaps, inner, *lanes(wing), *sems(4 * f + 2))
        yield from ring_gather(*one, gaps, outer, *trio(two[0]), *sems(4 * f + 3))
        whole = gaps[...].reshape(NX * tok, wing)

        def term(core):
            value = lax.dot_general(hid[core], whole, (((0,), (0,)), ((), ())), preferred_element_type=F32)
            return (value / tok).astype(BF)

        give[f] = term(1 - r)
        slot = r * per + f
        swaps.append(remote(give.at[f], chunks.at[slot], csend.at[f], crecv.at[f], sibling))
        swaps[-1].start()
        chunks[slot] = term(r)

    teach = ring_sum(nz, z, up, down, teacher, lambda d, p: (d,) + p, [lanes(span)], tcame, tleave, *sems(4 * count))
    next(teach)
    load.wait()
    keep_hid.wait()
    swap_hid.wait_recv()
    half = count // 2
    flows = [flow(k) for pair in zip(range(half), range(half, count)) for k in pair]
    for one in flows:
        next(one)
    together(teach, *flows)
    place = r * ny + y
    tells = [remote(loss, losses.at[place], lsend.at[k], lrecv.at[k], device) for k, device in enumerate(mates)]
    keep_loss = pltpu.make_async_copy(loss, losses.at[place], own.at[2])
    for copy in tells + [keep_loss]:
        copy.start()
    for copy in swaps:
        copy.wait_recv()
    rows, span = chunks.shape[1], chunks.shape[2]
    subs = []
    for u in (0, 1):
        band = pl.ds(u * (rows // 2), rows // 2)
        subs.append(((band, pl.ds(0, span)), (band, pl.ds(0, span // 2)), (band, pl.ds(span // 2, span // 2))))
    ring = {}
    together(ring_sum(nz, z, up, down, chunks, lambda d, p: (d,) + p, subs, came, leave, zsend, zrecv, ring))
    value = chunks[z].astype(F32) + came[0, per - 1].astype(F32) + came[1, per - 1].astype(F32)
    total[...] = value.astype(BF)
    size = span // NX
    outs = []
    for d, tx in across:
        outs.append(remote(total.at[:, lanes_at(tx, size)], grad.at[x], xsend.at[d - 1], xrecv.at[d - 1], (z, tx, r, y)))
        outs[-1].start()
    last = pltpu.make_async_copy(total.at[:, lanes_at(x, size)], grad.at[x], own.at[3])
    last.start()
    for copy in [last, keep_loss] + outs + tells:
        copy.wait()
    for copy in swaps + [swap_hid] + list(ring.values()) + [c for group in copies for c in group.values()]:
        copy.wait_send()


def on_device(tokens, routes, route_weights, teacher_in, teacher_out, student_in, student_out):
    nz, nr, ny = lax.axis_size("z"), lax.axis_size("row"), lax.axis_size("col")
    z, x, r, y = here()
    tok, width = tokens.shape
    block, top = routes.shape
    blk = student_in.shape[1]
    ff = student_in.shape[2]
    sub = ff // NX
    half = width // nr
    experts = NX * ny
    cap = max(2, 3 * block * top // (2 * nz * experts))
    blocks = nz * NX
    shape = jax.ShapeDtypeStruct

    parts = jnp.concatenate([jnp.swapaxes(student_in, 1, 2), student_out[None]], axis=0)
    parts = pad_lanes(parts)
    lanes = parts.shape[-1]
    wide = blocks * lanes
    steps = nz // 2
    slots = nz * cap
    hid = teacher_in.shape[3]
    mine = lax.dynamic_slice(tokens, (y * block, r * half), (block, half))
    meta = jnp.concatenate([routes.astype(F32), route_weights], axis=1).T
    meta = jnp.pad(meta, ((0, 0), (0, 128 - block)))
    padded = pad_lanes(tokens.reshape(tok, blocks, blk)).reshape(tok, wide)
    whole, far = pl.BlockSpec(memory_space=pltpu.VMEM), pl.BlockSpec(memory_space=pl.ANY)
    bf, f32 = (lambda *b: pltpu.VMEM(b, BF)), (lambda *b: pltpu.VMEM(b, F32))
    buffers = [bf(2, sub, wide), bf(NX, tok, wide), f32(nz, 2 * top, 128), f32(cap, experts * nz, nz * block), bf(experts, slots, half)]
    buffers += [bf(2, width, hid), bf(hid, width), bf(nz, block, half), bf(experts, slots, half), bf(experts, slots, width)]
    buffers += [bf(experts // 2 * slots, hid), bf(experts, slots, width)] + [bf(experts, slots, half)] * 2
    sems = [(4, 3)] * 2 + [(3, 2, steps, 1)] * 2 + [(2, steps)] * 4 + [(3,)] * 2 + [(2, 3)] * 2 + [(3, 3)] * 2
    sems += [(experts,)] * 4 + [(2,)] * 2 + [(experts,)] * 2 + [(9,)]
    hidden, student_down, teacher = kernel_call(
        functools.partial(front_kernel, nz, cap, blk), 0,
        [shape((NX * tok, sub), BF), shape((sub, wide), BF), shape((nz, block, wide // nr), BF)],
        buffers + [dma(*b) for b in sems],
        parts.reshape(3, NX, sub, lanes), mine, meta, padded, teacher_in[0], teacher_out[0],
        specs=[whole, whole, whole, whole, far, far],
    )

    span = wide // nr
    count = steps
    wing = span // count
    chunk = NX * lanes
    flows = []
    for f in range(count):
        one, two = (NX, ny) if f < count // 2 else (ny, NX)
        flows += [(NX, ny, block, wing)] * 2
        flows += [(2, one // 2, two, block, wing), (2, one // 2 - 1, two, block, wing), (two, block, wing)]
        flows += [(2, two // 2, block, wing), (2, two // 2 - 1, block, wing)]
    buffers = [(nr, NX * tok, sub), (sub, wide), (2, steps, block, span), (2, steps - 1, block, span), (nz, sub, chunk), (steps, sub, chunk)]
    buffers += [(2, steps, sub, chunk), (2, steps - 1, sub, chunk), (sub, chunk)]
    grad, losses = kernel_call(
        functools.partial(tail_kernel, nz, count, tok), 4,
        [shape((NX, sub, lanes), BF), shape((nr * ny, block, 128), F32)],
        [pltpu.VMEM(b, BF) for b in buffers] + [pltpu.VMEM((block, 128), F32)]
        + [dma(4 * count + 1, 2, steps, 1)] * 2 + [dma(2, steps, 2)] * 2 + [dma(steps)] * 2 + [pltpu.SemaphoreType.DMA] * 2 + [dma(3)] * 2
        + [dma(2 * ny - 1)] * 2 + [dma(4)]
        + [pltpu.VMEM(b, BF) for b in flows],
        hidden, student_down, teacher,
        specs=[whole, far, whole],
    )
    token_loss = jnp.sum(losses.reshape(nr, ny * block, 128), axis=(0, 2)) / width
    grad = grad.reshape(ff, lanes)[:, :blk].astype(F32)
    return token_loss, grad


def solution(mesh):
    dp = ("z", "x")
    in_specs = (
        P(dp, None),
        P(dp + ("col",), None),
        P(dp + ("col",), None),
        P(dp + ("col",), None, None, "row"),
        P(dp + ("col",), "row", None),
        P(None, dp, ("row", "col")),
        P(("row", "col"), dp),
    )
    out_specs = (P(dp), P(("row", "col"), dp))
    return jax.shard_map(
        on_device, mesh=split_mesh(mesh), in_specs=in_specs, out_specs=out_specs, check_vma=False
    )
```

```python
import functools

import jax
import jax.numpy as jnp
from jax import lax
from jax.experimental import pallas as pl
from jax.experimental.pallas import tpu as pltpu
from jax.sharding import Mesh, PartitionSpec as P

NX = 4
MESH = pl.DeviceIdType.MESH
F32 = jnp.float32
BF = jnp.bfloat16


def split_mesh(mesh):
    dp, row, col = mesh.devices.shape
    return Mesh(mesh.devices.reshape(dp // NX, NX, row, col), ("z", "x", "row", "col"))


def dot(a, b, dims):
    return lax.dot_general(a, b, (dims, ((), ())), preferred_element_type=F32)


def pad_lanes(a):
    lanes = a.shape[-1]
    wide = -(-lanes // 128) * 128
    return jnp.pad(a, [(0, 0)] * (a.ndim - 1) + [(0, wide - lanes)])


def here():
    return tuple(lax.axis_index(a) for a in ("z", "x", "row", "col"))


def remote(src, dst, send, recv, device):
    return pltpu.make_async_remote_copy(
        src_ref=src, dst_ref=dst, send_sem=send, recv_sem=recv, device_id=device, device_id_type=MESH
    )


def greet(devices):
    barrier = pltpu.get_barrier_semaphore()
    for device in devices:
        pl.semaphore_signal(barrier, inc=1, device_id=device, device_id_type=MESH)
    pl.semaphore_wait(barrier, len(devices))


def lanes_at(start, size):
    return pl.ds(pl.multiple_of(start * size, size), size)


def kernel_call(body, number, outs, scratch, *args, specs=None, out_specs=None):
    whole = pl.BlockSpec(memory_space=pltpu.VMEM)
    return pl.pallas_call(
        body,
        out_shape=outs,
        in_specs=specs or [whole] * len(args),
        out_specs=out_specs or [whole] * len(outs),
        scratch_shapes=scratch,
        compiler_params=pltpu.CompilerParams(
            collective_id=number, has_side_effects=True, vmem_limit_bytes=56 * 1024 * 1024
        ),
    )(*args)


def dma(*shape):
    return pltpu.SemaphoreType.DMA(shape)


def plane_steps(ny):
    steps = [(dx, dy) for dx in range(NX) for dy in range(ny) if dx or dy]
    far = lambda s: min(s[0], NX - s[0]) + min(s[1], ny - s[1])
    return sorted(steps, key=far, reverse=True)


def token_gather(tokens, blk, plane, xs, xr, ys, yr, cs, cr, started):
    z, x, r, y = here()
    ny = lax.axis_size("col")
    north, south = (y + 1) % ny, (y + ny - 1) % ny
    sibling = (z, x, 1 - r, y)
    rows, wide = plane.shape[1], plane.shape[2]
    high, span = rows // 2, wide // 2
    quarter = span // 2
    mine_rows = pl.ds(pl.multiple_of(r * high, high), high)
    parity = y % 2
    held = lanes_at(parity, span)

    def go(copy):
        copy.start()
        started.append(copy)
        return copy

    def x_step(d):
        device = (z, (x + d) % NX, r, y)
        piece = plane.at[x, mine_rows, held]
        return go(remote(piece, piece, xs.at[d - 1], xr.at[d - 1], device))

    from_sib, from_y = [], []

    def onward(d, copy):
        copy.wait_recv()
        source = (x + NX - d) % NX
        for side, device in ((0, (z, x, r, north)), (1, (z, x, r, south))):
            piece = plane.at[source, mine_rows, lanes_at(parity * 2 + side, quarter)]
            from_y.append((d, side, go(remote(piece, piece, ys.at[side, d - 1], yr.at[side, d - 1], device))))
        piece = plane.at[source, mine_rows, held]
        from_sib.append(go(remote(piece, piece, cs.at[0, d - 1], cr.at[0, d - 1], sibling)))

    def inward():
        while from_y:
            d, side, copy = from_y.pop(0)
            copy.wait_recv()
            source = (x + NX - d) % NX
            piece = plane.at[source, mine_rows, lanes_at((1 - parity) * 2 + side, quarter)]
            from_sib.append(go(remote(piece, piece, cs.at[1 + side, d - 1], cr.at[1 + side, d - 1], sibling)))

    band = 32
    lanes = -(-blk // 128) * 128

    @pl.loop(0, rows // band)
    def _(i):
        cut = pl.ds(pl.multiple_of(i * band, band), band)
        value = tokens[cut].astype(F32)
        empty = jnp.zeros((band, lanes - blk), F32)
        for b in range(wide // lanes):
            piece = jnp.concatenate([value[:, b * blk:(b + 1) * blk], empty], axis=1)
            plane[x, cut, b * lanes:(b + 1) * lanes] = piece.astype(BF)

    first, third = x_step(1), x_step(3)
    yield
    onward(1, first)
    onward(3, third)
    second = x_step(2)
    yield
    inward()
    onward(2, second)
    yield
    inward()
    for copy in from_sib:
        copy.wait_recv()


def block_gather(nz, mine, meta, column, metas, zs, zr, ms, mr, own, started):
    z, x, r, y = here()
    up, down = (z + 1) % nz, (z + nz - 1) % nz
    half = mine.shape[1] // 2

    def go(copy):
        copy.start()
        started.append(copy)
        return copy

    local = [pltpu.make_async_copy(mine, column.at[z], own.at[0]), pltpu.make_async_copy(meta, metas.at[z], own.at[1])]
    for copy in local:
        copy.start()
    ring = []
    for s in range(1, nz // 2 + 1):
        for copy in ring:
            copy.wait_recv()
        a, b = (z + nz - s + 1) % nz, (z + s - 1) % nz
        one, two, three, four = (mine, mine, meta, meta) if s == 1 else (column.at[a], column.at[b], metas.at[a], metas.at[b])
        to_a, to_b = column.at[a], column.at[b]
        if s == nz // 2:
            low, top = pl.ds(0, half), pl.ds(half, half)
            one, to_a, two, to_b = column.at[a, :, low], column.at[a, :, low], column.at[b, :, top], column.at[b, :, top]
        ring = [
            go(remote(one, to_a, zs.at[0, s - 1], zr.at[0, s - 1], (up, x, r, y))),
            go(remote(two, to_b, zs.at[1, s - 1], zr.at[1, s - 1], (down, x, r, y))),
            go(remote(three, metas.at[a], ms.at[0, s - 1], mr.at[0, s - 1], (up, x, r, y))),
        ]
        if s < nz // 2:
            ring.append(go(remote(four, metas.at[b], ms.at[1, s - 1], mr.at[1, s - 1], (down, x, r, y))))
        yield
    for copy in ring:
        copy.wait_recv()
    for copy in local:
        copy.wait()


def place_rows(nz, cap, column, metas, outgoing, weighted):
    z = lax.axis_index("z")
    block, half = column.shape[1], column.shape[2]
    experts = outgoing.shape[0]
    top = metas.shape[1] // 2
    count = nz * block
    named = jnp.concatenate([metas[b, :top, :block] for b in range(nz)], axis=1)
    weights = jnp.concatenate([metas[b, top:, :block] for b in range(nz)], axis=1)
    ids = (z * experts + lax.broadcasted_iota(jnp.int32, (experts, 1), 0)).astype(F32)
    hit = jnp.zeros((experts, count), F32)
    weight = jnp.zeros((experts, count), F32)
    for k in range(top):
        hit += jnp.where(named[k:k + 1] == ids, 1.0, 0.0)
        weight += jnp.where(named[k:k + 1] == ids, weights[k:k + 1], 0.0)
    before, after = lax.broadcasted_iota(jnp.int32, (count, count), 0), lax.broadcasted_iota(jnp.int32, (count, count), 1)
    earlier = jnp.where((before < after) & (before // block == after // block), 1.0, 0.0).astype(BF)
    slot = jnp.dot(hit.astype(BF), earlier, preferred_element_type=F32)
    lane = lax.broadcasted_iota(jnp.int32, (nz, count), 1) // block
    inside = jnp.where(lane == lax.broadcasted_iota(jnp.int32, (nz, count), 0), 1.0, 0.0)
    rows = column[...].reshape(count, half)
    for s in range(cap):
        chosen = jnp.where(slot == float(s), hit, 0.0)
        placing = (chosen[:, None, :] * inside[None]).reshape(experts * nz, count).astype(BF)
        value = jnp.dot(placing, rows, preferred_element_type=F32).astype(BF)
        outgoing[:, s * nz:(s + 1) * nz, :] = value.reshape(experts, nz, half)
        chosen = jnp.where(slot == float(s), weight, 0.0)
        weighted[s] = (chosen[:, None, :] * inside[None]).reshape(experts * nz, count)


def weigh_rows(nz, cap, weighted, back, teacher, blk):
    experts, half = back.shape[0], back.shape[2]
    count = weighted.shape[2]
    total = jnp.zeros((count, half), F32)
    for s in range(cap):
        rows = back[:, s * nz:(s + 1) * nz, :].reshape(experts * nz, half)
        value = weighted[s]
        high = value.astype(BF)
        low = (value - high.astype(F32)).astype(BF)
        for term in (high, low):
            total += lax.dot_general(term, rows, (((0,), (0,)), ((), ())), preferred_element_type=F32)
    lanes = -(-blk // 128) * 128
    empty = jnp.zeros((count, lanes - blk), F32)
    for b in range(half // blk):
        piece = jnp.concatenate([total[:, b * blk:(b + 1) * blk], empty], axis=1).astype(BF)
        teacher[:, :, b * lanes:(b + 1) * lanes] = piece.reshape(nz, count // nz, lanes)


def front_kernel(nz, cap, blk, parts, meta, own_tokens, inner, outer, hidden, down_both, teacher,
                 student, student_down, mine, plane, metas, weighted, back, w_in, w_out, column, outgoing, got, act, part, other, total,
                 ws, wr, rs, rr, zs, zr, ms, mr, xs, xr, ys, yr, cs, cr, send, recv, fsend, frecv, csend, crecv, bsend, brecv, dsend, drecv, own):
    z, x, r, y = here()
    ny = lax.axis_size("col")
    steps = plane_steps(ny)[::-1]
    sibling = (z, x, 1 - r, y)
    up, down_z = ((z + 1) % nz, x, r, y), ((z + nz - 1) % nz, x, r, y)
    per = nz // 2
    loads = [pltpu.make_async_copy(inner, w_in, own.at[1]), pltpu.make_async_copy(outer, w_out, own.at[2])]
    for copy in loads:
        copy.start()
    peers = [(z, (x + dx) % NX, r, (y + dy) % ny) for dx, dy in steps]
    greet(peers + [sibling, up, down_z])
    started = []
    block, half = mine.shape
    mine[...] = own_tokens[pl.ds(pl.multiple_of(y * block, 8), block), lanes_at(r, half)]
    blocks = block_gather(nz, mine, meta, column, metas, zs, zr, ms, mr, own.at[pl.ds(3, 2)], started)
    tokens = token_gather(own_tokens, blk, plane, xs, xr, ys, yr, cs, cr, started)
    next(blocks)

    span = NX * 128
    exchange = [[], [], []]
    homes = [student.at[0], student.at[1], student_down]
    lane = lanes_at(x, 128)
    for kind in (0, 1, 2):
        for d in (2, 1, 3):
            to = (x + d) % NX
            copy = remote(parts.at[kind, to], homes[kind].at[z, :, lane], ws.at[d - 1, kind], wr.at[d - 1, kind], (z, to, r, y))
            copy.start()
            started.append(copy)
            exchange[kind].append(copy)
    local = [pltpu.make_async_copy(parts.at[k, x], homes[k].at[z, :, lane], own.at[5 + k]) for k in range(3)]
    for copy in local:
        copy.start()
    next(tokens)

    def chunk(d, p):
        return (d, slice(None), pl.ds(*p))

    rings = [{}, {}, {}]
    gathers = [
        ring_gather(nz, z, up, down_z, homes[kind], chunk, (0, span), (0, span // 2), (span // 2, span // 2),
                    rs.at[kind], rr.at[kind], rings[kind])
        for kind in range(3)
    ]

    def serve(*kinds):
        for kind in kinds:
            next(gathers[kind], None)

    for _ in range(per - 2):
        next(blocks)
    for kind in range(3):
        local[kind].wait()
        for copy in exchange[kind]:
            copy.wait_recv()
        if kind < 2:
            serve(kind)
        if kind == 0:
            next(blocks)
    next(tokens)
    next(blocks, None)

    place_rows(nz, cap, column, metas, outgoing, weighted)
    steps = [(0, 0)] + steps
    me = x * ny + y
    keep, give = lanes_at(r, half), lanes_at(1 - r, half)
    near = len(steps) // 2
    groups = (range(near), range(near, len(steps)))
    sends, forwards, swaps, returns = {}, {}, {}, []

    def forward(k, src):
        forwards[k] = remote(src, got.at[k, :, keep], fsend.at[k], frecv.at[k], sibling)
        forwards[k].start()

    for k, (dx, dy) in enumerate(steps):
        if k:
            tx, ty = (x + dx) % NX, (y + dy) % ny
            sends[k] = remote(outgoing.at[tx * ny + ty], got.at[k, :, keep], send.at[k], recv.at[k], (z, tx, r, ty))
            sends[k].start()
    own_rows = pltpu.make_async_copy(outgoing.at[me], got.at[0, :, keep], own.at[0])
    own_rows.start()
    forward(0, outgoing.at[me])
    serve(0, 1)

    def finish(g):
        swaps[g].wait_recv()
        for k in groups[g]:
            dx, dy = steps[k]
            tx, ty = (x + NX - dx) % NX, (y + ny - dy) % ny
            value = (part[k, :, keep].astype(F32) + other[k].astype(F32)).astype(BF)
            if k:
                total[k] = value
                returns.append(remote(total.at[k], back.at[me], bsend.at[k], brecv.at[k], (z, tx, r, ty)))
                returns[-1].start()
            else:
                back[me] = value

    for g, group in enumerate(groups):
        slots = pl.ds(group[0], near)
        for k in group:
            if k:
                sends[k].wait_recv()
                forward(k, got.at[k, :, keep])
        if g == 0:
            own_rows.wait()
            loads[0].wait()
        for k in group:
            forwards[k].wait_recv()
        rows = near * outgoing.shape[1]
        tile = w_in.shape[2] // 2

        @pl.loop(0, 2)
        def _(j):
            lhs = got[slots].reshape(rows, got.shape[2])
            cut = pl.ds(pl.multiple_of(j * tile, tile), tile)
            gate = jnp.dot(lhs, w_in[0, :, cut], preferred_element_type=F32)
            up_part = jnp.dot(lhs, w_in[1, :, cut], preferred_element_type=F32)
            act[:, cut] = (gate / (1.0 + jnp.exp(-gate)) * up_part).astype(BF)

        if g == 0:
            loads[1].wait()
        wide = half // 2

        def down(side):
            @pl.loop(0, 2)
            def _(j):
                cut = pl.ds(pl.multiple_of(side * half + j * wide, wide), wide)
                value = jnp.dot(act[...], w_out[:, cut], preferred_element_type=F32).astype(BF)
                part[slots, :, cut] = value.reshape(near, outgoing.shape[1], wide)

        down(1 - r)
        swaps[g] = remote(part.at[slots, :, give], other.at[slots], csend.at[g], crecv.at[g], sibling)
        swaps[g].start()
        down(r)
        if g == 0:
            serve(0, 1, 2)
        finish(g)
        if g == 1:
            serve(0, 1)
        next(tokens, None)

    serve(0, 1, 2)
    tok = plane.shape[1]

    def units(kind, i):
        total = jnp.zeros((2 * tok, student.shape[2]), F32)
        for d in range(nz):
            rows = plane[2 * i:2 * i + 2, :, d * span:(d + 1) * span].reshape(2 * tok, span)
            total += lax.dot_general(rows, student[kind, d], (((1,), (1,)), ((), ())), preferred_element_type=F32)
        return total

    for i in range(NX // 2):
        gate = units(0, i)
        hidden[2 * i * tok:2 * (i + 1) * tok] = (gate / (1.0 + jnp.exp(-gate)) * units(1, i)).astype(BF)
        serve(2)
    for copy in returns:
        copy.wait_recv()
    changes = []
    for i in (1, 2, 3, 0):
        if i == 0:
            weigh_rows(nz, cap, weighted, back, teacher, blk)
            serve(2)
        q = (z + i) % per
        src = student_down.at[(1 - r) * per + q]
        changes.append(remote(src, down_both.at[r, q], dsend.at[i], drecv.at[i], sibling))
        changes[-1].start()
    local = [pltpu.make_async_copy(student_down.at[r * per + q], down_both.at[r, q], own.at[5 + q]) for q in range(per)]
    for copy in local:
        copy.start()
    for copy in local + changes:
        copy.wait()
    for copy in started + returns + list(sends.values()) + list(forwards.values()) + list(swaps.values()):
        copy.wait_send()
    for ring in rings:
        for copy in ring.values():
            copy.wait_send()


def ring_sum(n, i, up, down, ref, where, subs, came, leave, send, recv, copies):
    half = n // 2

    def go(way, s, u, src, dst):
        copy = remote(src, dst, send.at[way, s, u], recv.at[way, s, u], (up, down)[way])
        copy.start()
        copies[way, s, u] = copy

    for u, (whole, low, top) in enumerate(subs):
        for way, part in ((0, low), (1, top)):
            go(way, 0, u, ref.at[where((i + half) % n, part)], came.at[(way, 0) + part])
    yield
    for s in range(1, half):
        for u, (whole, low, top) in enumerate(subs):
            for way in (0, 1):
                d = (i + half - s) % n if way == 0 else (i + half + s) % n
                copies[way, s - 1, u].wait_recv()
                summed, plain = whole, None
                if s == 1:
                    summed, plain = (low, top) if way == 0 else (top, low)
                    leave[(way, 0) + plain] = ref[where(d, plain)]
                value = ref[where(d, summed)].astype(F32) + came[(way, s - 1) + summed].astype(F32)
                leave[(way, s - 1) + summed] = value.astype(BF)
                go(way, s, u, leave.at[(way, s - 1) + whole], came.at[(way, s) + whole])
        yield
    for u in range(len(subs)):
        for way in (0, 1):
            copies[way, half - 1, u].wait_recv()


def ring_gather(n, i, up, down, ref, where, whole, low, top, send, recv, copies):
    half = n // 2
    for s in range(half):
        for way, device in ((0, up), (1, down)):
            d = (i + n - s) % n if way == 0 else (i + s) % n
            if s:
                copies[way, s - 1].wait_recv()
            part = whole if s < half - 1 else (low, top)[way]
            piece = ref.at[where(d, part)]
            copies[way, s] = remote(piece, piece, send.at[way, s, 0], recv.at[way, s, 0], device)
            copies[way, s].start()
        yield
    for way in (0, 1):
        copies[way, half - 1].wait_recv()


def together(*rings):
    rings = list(rings)
    while rings:
        for ring in list(rings):
            try:
                next(ring)
            except StopIteration:
                rings.remove(ring)


def tail_kernel(nz, count, tok, hidden, weights, teacher, grad, losses, hid, w_out, tcame, tleave, chunks, give, came, leave, total, loss,
                send, recv, zsend, zrecv, csend, crecv, hsend, hrecv, xsend, xrecv, lsend, lrecv, own, *buffers):
    z, x, r, y = here()
    ny = lax.axis_size("col")
    up, down = ((z + 1) % nz, x, r, y), ((z + nz - 1) % nz, x, r, y)
    east, west = (z, (x + 1) % NX, r, y), (z, (x + NX - 1) % NX, r, y)
    north, south = (z, x, r, (y + 1) % ny), (z, x, r, (y + ny - 1) % ny)
    sibling = (z, x, 1 - r, y)
    mates = [(z, x, r, (y + d) % ny) for d in range(1, ny)] + [(z, x, 1 - r, (y + d) % ny) for d in range(ny)]
    across = [(d, (x + d) % NX) for d in (2, 1, 3)]
    load = pltpu.make_async_copy(weights, w_out, own.at[0])
    load.start()
    keep_hid = pltpu.make_async_copy(hidden, hid.at[r], own.at[1])
    keep_hid.start()
    greet([up, down] + mates + [(z, tx, r, y) for _, tx in across])
    span = teacher.shape[2]
    wing = span // count
    per = nz // 2
    every = slice(None)
    copies = [{} for _ in range(4 * count + 1)]
    swap_hid = remote(hidden, hid.at[r], hsend, hrecv, sibling)
    swap_hid.start()
    loss[...] = jnp.zeros_like(loss)

    def sems(k):
        return send.at[k], recv.at[k], copies[k]

    def trio(axis_size):
        return (pl.ds(0, axis_size),), (pl.ds(0, axis_size // 2),), (pl.ds(axis_size // 2, axis_size // 2),)

    def lanes(size):
        return tuple((every, pl.ds(o, s)) for o, s in ((0, size), (0, size // 2), (size // 2, size // 2)))

    along_x, along_y = (NX, x, east, west), (ny, y, north, south)
    swaps = []

    def flow(f):
        cut = pl.ds(f * wing, wing)
        parts, gaps, scame, sleave, mid, came2, leave2 = buffers[7 * f:7 * f + 7]
        x_first = f < count // 2
        one, two = (along_x, along_y) if x_first else (along_y, along_x)

        def outer(d, p):
            return (d,) + p if x_first else p + (d,)

        def inner(d, p):
            return (x, d) + p if x_first else (d, y) + p

        @pl.loop(0, NX)
        def _(i):
            rows = pl.ds(pl.multiple_of(i * tok, tok), tok)
            value = jnp.dot(hid[0, rows], w_out[0, f], preferred_element_type=F32)
            value += jnp.dot(hid[1, rows], w_out[1, f], preferred_element_type=F32)
            parts[i] = value.astype(BF).reshape(parts.shape[1:])

        yield from ring_sum(*one, parts, outer, [trio(two[0])], scame, sleave, *sems(4 * f))
        last = one[0] // 2 - 1
        kept = parts[x] if x_first else parts[:, y]
        mid[...] = (kept.astype(F32) + scame[0, last].astype(F32) + scame[1, last].astype(F32)).astype(BF)
        yield from ring_sum(*two, mid, lambda d, p: (d,) + p, [lanes(wing)], came2, leave2, *sems(4 * f + 1))
        last = two[0] // 2 - 1
        student = mid[two[1]].astype(F32) + came2[0, last].astype(F32) + came2[1, last].astype(F32)
        taught = teacher[z, :, cut].astype(F32) + tcame[0, per - 1, :, cut].astype(F32) + tcame[1, per - 1, :, cut].astype(F32)
        gap = student - taught
        gaps[x, y] = gap.astype(BF)
        square = gap * gap
        loss[...] += sum(square[:, t * 128:(t + 1) * 128] for t in range(wing // 128))
        yield from ring_gather(*two, gaps, inner, *lanes(wing), *sems(4 * f + 2))
        yield from ring_gather(*one, gaps, outer, *trio(two[0]), *sems(4 * f + 3))
        whole = gaps[...].reshape(NX * tok, wing)

        def term(core):
            value = lax.dot_general(hid[core], whole, (((0,), (0,)), ((), ())), preferred_element_type=F32)
            return (value / tok).astype(BF)

        give[f] = term(1 - r)
        slot = r * per + f
        swaps.append(remote(give.at[f], chunks.at[slot], csend.at[f], crecv.at[f], sibling))
        swaps[-1].start()
        chunks[slot] = term(r)

    teach = ring_sum(nz, z, up, down, teacher, lambda d, p: (d,) + p, [lanes(span)], tcame, tleave, *sems(4 * count))
    next(teach)
    load.wait()
    keep_hid.wait()
    swap_hid.wait_recv()
    half = count // 2
    flows = [flow(k) for pair in zip(range(half), range(half, count)) for k in pair]
    for one in flows:
        next(one)
    together(teach, *flows)
    place = r * ny + y
    tells = [remote(loss, losses.at[place], lsend.at[k], lrecv.at[k], device) for k, device in enumerate(mates)]
    keep_loss = pltpu.make_async_copy(loss, losses.at[place], own.at[2])
    for copy in tells + [keep_loss]:
        copy.start()
    for copy in swaps:
        copy.wait_recv()
    rows, span = chunks.shape[1], chunks.shape[2]
    subs = []
    for u in (0, 1):
        band = pl.ds(u * (rows // 2), rows // 2)
        subs.append(((band, pl.ds(0, span)), (band, pl.ds(0, span // 2)), (band, pl.ds(span // 2, span // 2))))
    ring = {}
    together(ring_sum(nz, z, up, down, chunks, lambda d, p: (d,) + p, subs, came, leave, zsend, zrecv, ring))
    value = chunks[z].astype(F32) + came[0, per - 1].astype(F32) + came[1, per - 1].astype(F32)
    total[...] = value.astype(BF)
    size = span // NX
    outs = []
    for d, tx in across:
        outs.append(remote(total.at[:, lanes_at(tx, size)], grad.at[x], xsend.at[d - 1], xrecv.at[d - 1], (z, tx, r, y)))
        outs[-1].start()
    last = pltpu.make_async_copy(total.at[:, lanes_at(x, size)], grad.at[x], own.at[3])
    last.start()
    for copy in [last, keep_loss] + outs + tells:
        copy.wait()
    for copy in swaps + [swap_hid] + list(ring.values()) + [c for group in copies for c in group.values()]:
        copy.wait_send()


def on_device(tokens, routes, route_weights, teacher_in, teacher_out, student_in, student_out):
    nz, nr, ny = lax.axis_size("z"), lax.axis_size("row"), lax.axis_size("col")
    z, x, r, y = here()
    tok, width = tokens.shape
    block, top = routes.shape
    blk = student_in.shape[1]
    ff = student_in.shape[2]
    sub = ff // NX
    half = width // nr
    experts = NX * ny
    cap = max(2, 3 * block * top // (2 * nz * experts))
    blocks = nz * NX
    shape = jax.ShapeDtypeStruct

    parts = jnp.concatenate([jnp.swapaxes(student_in, 1, 2), student_out[None]], axis=0)
    parts = pad_lanes(parts)
    lanes = parts.shape[-1]
    wide = blocks * lanes
    steps = nz // 2
    slots = nz * cap
    hid = teacher_in.shape[3]
    meta = jnp.concatenate([routes.astype(F32), route_weights], axis=1).T
    meta = jnp.pad(meta, ((0, 0), (0, 128 - block)))
    whole, far = pl.BlockSpec(memory_space=pltpu.VMEM), pl.BlockSpec(memory_space=pl.ANY)
    bf, f32 = (lambda *b: pltpu.VMEM(b, BF)), (lambda *b: pltpu.VMEM(b, F32))
    buffers = [bf(2, nz, sub, NX * lanes), bf(nz, sub, NX * lanes), bf(block, half), bf(NX, tok, wide), f32(nz, 2 * top, 128), f32(cap, experts * nz, nz * block), bf(experts, slots, half)]
    buffers += [bf(2, width, hid), bf(hid, width), bf(nz, block, half), bf(experts, slots, half), bf(experts, slots, width)]
    buffers += [bf(experts // 2 * slots, hid), bf(experts, slots, width)] + [bf(experts, slots, half)] * 2
    sems = [(3, 3)] * 2 + [(3, 2, steps, 1)] * 2 + [(2, steps)] * 4 + [(3,)] * 2 + [(2, 3)] * 2 + [(3, 3)] * 2
    sems += [(experts,)] * 4 + [(2,)] * 2 + [(experts,)] * 2 + [(steps,)] * 2 + [(9,)]
    hidden, student_down, teacher = kernel_call(
        functools.partial(front_kernel, nz, cap, blk), 0,
        [shape((NX * tok, sub), BF), shape((nr, steps, sub, NX * lanes), BF), shape((nz, block, wide // nr), BF)],
        buffers + [dma(*b) for b in sems],
        parts.reshape(3, NX, sub, lanes), meta, tokens, teacher_in[0], teacher_out[0],
        specs=[whole, whole, whole, far, far],
    )

    span = wide // nr
    count = steps
    wing = span // count
    chunk = NX * lanes
    flows = []
    for f in range(count):
        one, two = (NX, ny) if f < count // 2 else (ny, NX)
        flows += [(NX, ny, block, wing)] * 2
        flows += [(2, one // 2, two, block, wing), (2, one // 2 - 1, two, block, wing), (two, block, wing)]
        flows += [(2, two // 2, block, wing), (2, two // 2 - 1, block, wing)]
    buffers = [(nr, NX * tok, sub), (nr, steps, sub, chunk), (2, steps, block, span), (2, steps - 1, block, span), (nz, sub, chunk), (steps, sub, chunk)]
    buffers += [(2, steps, sub, chunk), (2, steps - 1, sub, chunk), (sub, chunk)]
    grad, losses = kernel_call(
        functools.partial(tail_kernel, nz, count, tok), 4,
        [shape((NX, sub, lanes), BF), shape((nr * ny, block, 128), F32)],
        [pltpu.VMEM(b, BF) for b in buffers] + [pltpu.VMEM((block, 128), F32)]
        + [dma(4 * count + 1, 2, steps, 1)] * 2 + [dma(2, steps, 2)] * 2 + [dma(steps)] * 2 + [pltpu.SemaphoreType.DMA] * 2 + [dma(3)] * 2
        + [dma(2 * ny - 1)] * 2 + [dma(4)]
        + [pltpu.VMEM(b, BF) for b in flows],
        hidden, student_down, teacher,
        specs=[whole, far, whole],
    )
    token_loss = jnp.sum(losses.reshape(nr, ny * block, 128), axis=(0, 2)) / width
    grad = grad.reshape(ff, lanes)[:, :blk].astype(F32)
    return token_loss, grad


def solution(mesh):
    dp = ("z", "x")
    in_specs = (
        P(dp, None),
        P(dp + ("col",), None),
        P(dp + ("col",), None),
        P(dp + ("col",), None, None, "row"),
        P(dp + ("col",), "row", None),
        P(None, dp, ("row", "col")),
        P(("row", "col"), dp),
    )
    out_specs = (P(dp), P(("row", "col"), dp))
    return jax.shard_map(
        on_device, mesh=split_mesh(mesh), in_specs=in_specs, out_specs=out_specs, check_vma=False
    )
```

```python
import functools

import jax
import jax.numpy as jnp
from jax import lax
from jax.experimental import pallas as pl
from jax.experimental.pallas import tpu as pltpu
from jax.sharding import Mesh, PartitionSpec as P

NX = 4
MESH = pl.DeviceIdType.MESH
F32 = jnp.float32
BF = jnp.bfloat16


def split_mesh(mesh):
    dp, row, col = mesh.devices.shape
    return Mesh(mesh.devices.reshape(dp // NX, NX, row, col), ("z", "x", "row", "col"))


def dot(a, b, dims):
    return lax.dot_general(a, b, (dims, ((), ())), preferred_element_type=F32)


def pad_lanes(a):
    lanes = a.shape[-1]
    wide = -(-lanes // 128) * 128
    return jnp.pad(a, [(0, 0)] * (a.ndim - 1) + [(0, wide - lanes)])


def here():
    return tuple(lax.axis_index(a) for a in ("z", "x", "row", "col"))


def remote(src, dst, send, recv, device):
    return pltpu.make_async_remote_copy(
        src_ref=src, dst_ref=dst, send_sem=send, recv_sem=recv, device_id=device, device_id_type=MESH
    )


def greet(devices):
    barrier = pltpu.get_barrier_semaphore()
    for device in devices:
        pl.semaphore_signal(barrier, inc=1, device_id=device, device_id_type=MESH)
    pl.semaphore_wait(barrier, len(devices))


def lanes_at(start, size):
    return pl.ds(pl.multiple_of(start * size, size), size)


def kernel_call(body, number, outs, scratch, *args, specs=None, out_specs=None):
    whole = pl.BlockSpec(memory_space=pltpu.VMEM)
    return pl.pallas_call(
        body,
        out_shape=outs,
        in_specs=specs or [whole] * len(args),
        out_specs=out_specs or [whole] * len(outs),
        scratch_shapes=scratch,
        compiler_params=pltpu.CompilerParams(
            collective_id=number, has_side_effects=True, vmem_limit_bytes=56 * 1024 * 1024
        ),
    )(*args)


def dma(*shape):
    return pltpu.SemaphoreType.DMA(shape)


def plane_steps(ny):
    steps = [(dx, dy) for dx in range(NX) for dy in range(ny) if dx or dy]
    far = lambda s: min(s[0], NX - s[0]) + min(s[1], ny - s[1])
    return sorted(steps, key=far, reverse=True)


def token_gather(tokens, blk, plane, xs, xr, ys, yr, cs, cr, started):
    z, x, r, y = here()
    ny = lax.axis_size("col")
    north, south = (y + 1) % ny, (y + ny - 1) % ny
    sibling = (z, x, 1 - r, y)
    rows, wide = plane.shape[1], plane.shape[2]
    high, span = rows // 2, wide // 2
    quarter = span // 2
    mine_rows = pl.ds(pl.multiple_of(r * high, high), high)
    parity = y % 2
    held = lanes_at(parity, span)

    def go(copy):
        copy.start()
        started.append(copy)
        return copy

    def x_step(d):
        device = (z, (x + d) % NX, r, y)
        piece = plane.at[x, mine_rows, held]
        return go(remote(piece, piece, xs.at[d - 1], xr.at[d - 1], device))

    from_sib, from_y = [], []

    def onward(d, copy):
        copy.wait_recv()
        source = (x + NX - d) % NX
        for side, device in ((0, (z, x, r, north)), (1, (z, x, r, south))):
            piece = plane.at[source, mine_rows, lanes_at(parity * 2 + side, quarter)]
            from_y.append((d, side, go(remote(piece, piece, ys.at[side, d - 1], yr.at[side, d - 1], device))))
        piece = plane.at[source, mine_rows, held]
        from_sib.append(go(remote(piece, piece, cs.at[0, d - 1], cr.at[0, d - 1], sibling)))

    def inward():
        while from_y:
            d, side, copy = from_y.pop(0)
            copy.wait_recv()
            source = (x + NX - d) % NX
            piece = plane.at[source, mine_rows, lanes_at((1 - parity) * 2 + side, quarter)]
            from_sib.append(go(remote(piece, piece, cs.at[1 + side, d - 1], cr.at[1 + side, d - 1], sibling)))

    band = 32
    lanes = -(-blk // 128) * 128

    @pl.loop(0, rows // band)
    def _(i):
        cut = pl.ds(pl.multiple_of(i * band, band), band)
        value = tokens[cut].astype(F32)
        empty = jnp.zeros((band, lanes - blk), F32)
        for b in range(wide // lanes):
            piece = jnp.concatenate([value[:, b * blk:(b + 1) * blk], empty], axis=1)
            plane[x, cut, b * lanes:(b + 1) * lanes] = piece.astype(BF)

    first, third = x_step(1), x_step(3)
    yield
    onward(1, first)
    onward(3, third)
    second = x_step(2)
    yield
    inward()
    onward(2, second)
    yield
    inward()
    for copy in from_sib:
        copy.wait_recv()


def block_gather(nz, mine, meta, column, metas, zs, zr, ms, mr, own, started):
    z, x, r, y = here()
    up, down = (z + 1) % nz, (z + nz - 1) % nz
    half = mine.shape[1] // 2

    def go(copy):
        copy.start()
        started.append(copy)
        return copy

    local = [pltpu.make_async_copy(mine, column.at[z], own.at[0]), pltpu.make_async_copy(meta, metas.at[z], own.at[1])]
    for copy in local:
        copy.start()
    ring = []
    for s in range(1, nz // 2 + 1):
        for copy in ring:
            copy.wait_recv()
        a, b = (z + nz - s + 1) % nz, (z + s - 1) % nz
        one, two, three, four = (mine, mine, meta, meta) if s == 1 else (column.at[a], column.at[b], metas.at[a], metas.at[b])
        to_a, to_b = column.at[a], column.at[b]
        if s == nz // 2:
            low, top = pl.ds(0, half), pl.ds(half, half)
            one, to_a, two, to_b = column.at[a, :, low], column.at[a, :, low], column.at[b, :, top], column.at[b, :, top]
        ring = [
            go(remote(one, to_a, zs.at[0, s - 1], zr.at[0, s - 1], (up, x, r, y))),
            go(remote(two, to_b, zs.at[1, s - 1], zr.at[1, s - 1], (down, x, r, y))),
            go(remote(three, metas.at[a], ms.at[0, s - 1], mr.at[0, s - 1], (up, x, r, y))),
        ]
        if s < nz // 2:
            ring.append(go(remote(four, metas.at[b], ms.at[1, s - 1], mr.at[1, s - 1], (down, x, r, y))))
        yield
    for copy in ring:
        copy.wait_recv()
    for copy in local:
        copy.wait()


def place_rows(nz, cap, column, metas, outgoing, weighted):
    z = lax.axis_index("z")
    block, half = column.shape[1], column.shape[2]
    experts = outgoing.shape[0]
    top = metas.shape[1] // 2
    count = nz * block
    named = jnp.concatenate([metas[b, :top, :block] for b in range(nz)], axis=1)
    weights = jnp.concatenate([metas[b, top:, :block] for b in range(nz)], axis=1)
    ids = (z * experts + lax.broadcasted_iota(jnp.int32, (experts, 1), 0)).astype(F32)
    hit = jnp.zeros((experts, count), F32)
    weight = jnp.zeros((experts, count), F32)
    for k in range(top):
        hit += jnp.where(named[k:k + 1] == ids, 1.0, 0.0)
        weight += jnp.where(named[k:k + 1] == ids, weights[k:k + 1], 0.0)
    before, after = lax.broadcasted_iota(jnp.int32, (count, count), 0), lax.broadcasted_iota(jnp.int32, (count, count), 1)
    earlier = jnp.where((before < after) & (before // block == after // block), 1.0, 0.0).astype(BF)
    slot = jnp.dot(hit.astype(BF), earlier, preferred_element_type=F32)
    lane = lax.broadcasted_iota(jnp.int32, (nz, count), 1) // block
    inside = jnp.where(lane == lax.broadcasted_iota(jnp.int32, (nz, count), 0), 1.0, 0.0)
    rows = column[...].reshape(count, half)
    for s in range(cap):
        chosen = jnp.where(slot == float(s), hit, 0.0)
        placing = (chosen[:, None, :] * inside[None]).reshape(experts * nz, count).astype(BF)
        value = jnp.dot(placing, rows, preferred_element_type=F32).astype(BF)
        outgoing[:, s * nz:(s + 1) * nz, :] = value.reshape(experts, nz, half)
        chosen = jnp.where(slot == float(s), weight, 0.0)
        weighted[s] = (chosen[:, None, :] * inside[None]).reshape(experts * nz, count)


def weigh_rows(nz, cap, weighted, back, teacher, blk):
    experts, half = back.shape[0], back.shape[2]
    count = weighted.shape[2]
    total = jnp.zeros((count, half), F32)
    for s in range(cap):
        rows = back[:, s * nz:(s + 1) * nz, :].reshape(experts * nz, half)
        value = weighted[s]
        high = value.astype(BF)
        low = (value - high.astype(F32)).astype(BF)
        for term in (high, low):
            total += lax.dot_general(term, rows, (((0,), (0,)), ((), ())), preferred_element_type=F32)
    lanes = -(-blk // 128) * 128
    empty = jnp.zeros((count, lanes - blk), F32)
    for b in range(half // blk):
        piece = jnp.concatenate([total[:, b * blk:(b + 1) * blk], empty], axis=1).astype(BF)
        teacher[:, :, b * lanes:(b + 1) * lanes] = piece.reshape(nz, count // nz, lanes)


def front_kernel(nz, cap, blk, parts, meta, own_tokens, inner, outer, hidden, down_both, teacher,
                 student, student_down, mine, plane, metas, weighted, back, w_in, w_out, column, outgoing, got, act, part, other, total,
                 ws, wr, rs, rr, zs, zr, ms, mr, xs, xr, ys, yr, cs, cr, send, recv, fsend, frecv, csend, crecv, bsend, brecv, dsend, drecv, own):
    z, x, r, y = here()
    ny = lax.axis_size("col")
    steps = plane_steps(ny)[::-1]
    sibling = (z, x, 1 - r, y)
    up, down_z = ((z + 1) % nz, x, r, y), ((z + nz - 1) % nz, x, r, y)
    per = nz // 2
    loads = [pltpu.make_async_copy(inner, w_in, own.at[1]), pltpu.make_async_copy(outer, w_out, own.at[2])]
    for copy in loads:
        copy.start()
    peers = [(z, (x + dx) % NX, r, (y + dy) % ny) for dx, dy in steps]
    greet(peers + [sibling, up, down_z])
    started = []
    block, half = mine.shape
    mine[...] = own_tokens[pl.ds(pl.multiple_of(y * block, 8), block), lanes_at(r, half)]
    blocks = block_gather(nz, mine, meta, column, metas, zs, zr, ms, mr, own.at[pl.ds(3, 2)], started)
    tokens = token_gather(own_tokens, blk, plane, xs, xr, ys, yr, cs, cr, started)
    next(blocks)

    span = NX * 128
    exchange = [[], [], []]
    homes = [student.at[0], student.at[1], student_down]
    lane = lanes_at(x, 128)
    for kind in (0, 1, 2):
        for d in (2, 1, 3):
            to = (x + d) % NX
            copy = remote(parts.at[kind, to], homes[kind].at[z, :, lane], ws.at[d - 1, kind], wr.at[d - 1, kind], (z, to, r, y))
            copy.start()
            started.append(copy)
            exchange[kind].append(copy)
    local = [pltpu.make_async_copy(parts.at[k, x], homes[k].at[z, :, lane], own.at[5 + k]) for k in range(3)]
    for copy in local:
        copy.start()
    next(tokens)

    def chunk(d, p):
        return (d, slice(None), pl.ds(*p))

    rings = [{}, {}, {}]
    idle = 128 - blk
    riders = 2 * NX - 1
    packed = riders * idle == blk
    last = slice(span - 128, span)

    def spot(d, i):
        return i // NX, d, slice(None), slice(i % NX * 128, (i % NX + 1) * 128)

    def pack():
        value = student[1, z, :, last].astype(F32)
        for i in range(riders):
            kept = student[spot(z, i)].astype(F32)[:, :blk]
            student[spot(z, i)] = jnp.concatenate([kept, value[:, i * idle:(i + 1) * idle]], axis=1).astype(BF)

    def unpack():
        @pl.loop(0, nz)
        def _(d):
            pieces = [student[spot(d, i)].astype(F32)[:, blk:] for i in range(riders)]
            empty = jnp.zeros((student.shape[2], idle), F32)
            student[1, d, :, last] = jnp.concatenate(pieces + [empty], axis=1).astype(BF)

    sizes = [span, span - 128 if packed else span, span]
    gathers = [
        ring_gather(nz, z, up, down_z, homes[kind], chunk, (0, sizes[kind]), (0, span // 2), (span // 2, sizes[kind] - span // 2),
                    rs.at[kind], rr.at[kind], rings[kind])
        for kind in range(3)
    ]

    def serve(*kinds):
        for kind in kinds:
            next(gathers[kind], None)

    for _ in range(per - 2):
        next(blocks)
    for kind in range(3):
        local[kind].wait()
        for copy in exchange[kind]:
            copy.wait_recv()
        if kind == 1:
            if packed:
                pack()
            serve(0, 1)
        if kind == 0:
            next(blocks)
    next(tokens)
    next(blocks, None)

    place_rows(nz, cap, column, metas, outgoing, weighted)
    steps = [(0, 0)] + steps
    me = x * ny + y
    keep, give = lanes_at(r, half), lanes_at(1 - r, half)
    near = len(steps) // 2
    groups = (range(near), range(near, len(steps)))
    sends, forwards, swaps, returns = {}, {}, {}, []

    def forward(k, src):
        forwards[k] = remote(src, got.at[k, :, keep], fsend.at[k], frecv.at[k], sibling)
        forwards[k].start()

    for k, (dx, dy) in enumerate(steps):
        if k:
            tx, ty = (x + dx) % NX, (y + dy) % ny
            sends[k] = remote(outgoing.at[tx * ny + ty], got.at[k, :, keep], send.at[k], recv.at[k], (z, tx, r, ty))
            sends[k].start()
    own_rows = pltpu.make_async_copy(outgoing.at[me], got.at[0, :, keep], own.at[0])
    own_rows.start()
    forward(0, outgoing.at[me])
    serve(0, 1)

    def finish(g):
        swaps[g].wait_recv()
        for k in groups[g]:
            dx, dy = steps[k]
            tx, ty = (x + NX - dx) % NX, (y + ny - dy) % ny
            value = (part[k, :, keep].astype(F32) + other[k].astype(F32)).astype(BF)
            if k:
                total[k] = value
                returns.append(remote(total.at[k], back.at[me], bsend.at[k], brecv.at[k], (z, tx, r, ty)))
                returns[-1].start()
            else:
                back[me] = value

    for g, group in enumerate(groups):
        slots = pl.ds(group[0], near)
        for k in group:
            if k:
                sends[k].wait_recv()
                forward(k, got.at[k, :, keep])
        if g == 0:
            own_rows.wait()
            loads[0].wait()
        for k in group:
            forwards[k].wait_recv()
        rows = near * outgoing.shape[1]
        tile = w_in.shape[2] // 2

        @pl.loop(0, 2)
        def _(j):
            lhs = got[slots].reshape(rows, got.shape[2])
            cut = pl.ds(pl.multiple_of(j * tile, tile), tile)
            gate = jnp.dot(lhs, w_in[0, :, cut], preferred_element_type=F32)
            up_part = jnp.dot(lhs, w_in[1, :, cut], preferred_element_type=F32)
            act[:, cut] = (gate / (1.0 + jnp.exp(-gate)) * up_part).astype(BF)

        if g == 0:
            loads[1].wait()
        wide = half // 2

        def down(side):
            @pl.loop(0, 2)
            def _(j):
                cut = pl.ds(pl.multiple_of(side * half + j * wide, wide), wide)
                value = jnp.dot(act[...], w_out[:, cut], preferred_element_type=F32).astype(BF)
                part[slots, :, cut] = value.reshape(near, outgoing.shape[1], wide)

        down(1 - r)
        swaps[g] = remote(part.at[slots, :, give], other.at[slots], csend.at[g], crecv.at[g], sibling)
        swaps[g].start()
        down(r)
        if g == 0:
            serve(0, 1, 2)
        finish(g)
        if g == 1:
            serve(0, 1, 2)
        next(tokens, None)

    serve(0, 1, 2)
    if packed:
        unpack()
    tok = plane.shape[1]

    def units(kind, i):
        total = jnp.zeros((2 * tok, student.shape[2]), F32)
        for d in range(nz):
            rows = plane[2 * i:2 * i + 2, :, d * span:(d + 1) * span].reshape(2 * tok, span)
            total += lax.dot_general(rows, student[kind, d], (((1,), (1,)), ((), ())), preferred_element_type=F32)
        return total

    for i in range(NX // 2):
        gate = units(0, i)
        hidden[2 * i * tok:2 * (i + 1) * tok] = (gate / (1.0 + jnp.exp(-gate)) * units(1, i)).astype(BF)
        if i == 0:
            serve(2)
    for copy in returns:
        copy.wait_recv()
    changes = []
    for i in (1, 2, 3, 0):
        if i == 0:
            weigh_rows(nz, cap, weighted, back, teacher, blk)
            serve(2)
        q = (z + i) % per
        src = student_down.at[(1 - r) * per + q]
        changes.append(remote(src, down_both.at[r, q], dsend.at[i], drecv.at[i], sibling))
        changes[-1].start()
    local = [pltpu.make_async_copy(student_down.at[r * per + q], down_both.at[r, q], own.at[5 + q]) for q in range(per)]
    for copy in local:
        copy.start()
    for copy in local + changes:
        copy.wait()
    for copy in started + returns + list(sends.values()) + list(forwards.values()) + list(swaps.values()):
        copy.wait_send()
    for ring in rings:
        for copy in ring.values():
            copy.wait_send()


def ring_sum(n, i, up, down, ref, where, subs, came, leave, send, recv, copies, done=None):
    half = n // 2

    def go(way, s, u, src, dst):
        copy = remote(src, dst, send.at[way, s, u], recv.at[way, s, u], (up, down)[way])
        copy.start()
        copies[way, s, u] = copy

    for u, (whole, low, top) in enumerate(subs):
        for way, part in ((0, low), (1, top)):
            go(way, 0, u, ref.at[where((i + half) % n, part)], came.at[(way, 0) + part])
    yield
    for s in range(1, half):
        for u, (whole, low, top) in enumerate(subs):
            for way in (0, 1):
                d = (i + half - s) % n if way == 0 else (i + half + s) % n
                copies[way, s - 1, u].wait_recv()
                summed, plain = whole, None
                if s == 1:
                    summed, plain = (low, top) if way == 0 else (top, low)
                    leave[(way, 0) + plain] = ref[where(d, plain)]
                value = ref[where(d, summed)].astype(F32) + came[(way, s - 1) + summed].astype(F32)
                leave[(way, s - 1) + summed] = value.astype(BF)
                go(way, s, u, leave.at[(way, s - 1) + whole], came.at[(way, s) + whole])
        yield
    for u in range(len(subs)):
        for way in (0, 1):
            copies[way, half - 1, u].wait_recv()
        if done:
            done(u)


def ring_gather(n, i, up, down, ref, where, whole, low, top, send, recv, copies):
    half = n // 2
    for s in range(half):
        for way, device in ((0, up), (1, down)):
            d = (i + n - s) % n if way == 0 else (i + s) % n
            if s:
                copies[way, s - 1].wait_recv()
            part = whole if s < half - 1 else (low, top)[way]
            piece = ref.at[where(d, part)]
            copies[way, s] = remote(piece, piece, send.at[way, s, 0], recv.at[way, s, 0], device)
            copies[way, s].start()
        yield
    for way in (0, 1):
        copies[way, half - 1].wait_recv()


def together(*rings):
    rings = list(rings)
    while rings:
        for ring in list(rings):
            try:
                next(ring)
            except StopIteration:
                rings.remove(ring)


def tail_kernel(nz, count, tok, hidden, weights, teacher, grad, losses, hid, w_out, tcame, tleave, chunks, give, came, leave, total, loss,
                send, recv, zsend, zrecv, csend, crecv, hsend, hrecv, xsend, xrecv, lsend, lrecv, own, *buffers):
    z, x, r, y = here()
    ny = lax.axis_size("col")
    up, down = ((z + 1) % nz, x, r, y), ((z + nz - 1) % nz, x, r, y)
    east, west = (z, (x + 1) % NX, r, y), (z, (x + NX - 1) % NX, r, y)
    north, south = (z, x, r, (y + 1) % ny), (z, x, r, (y + ny - 1) % ny)
    sibling = (z, x, 1 - r, y)
    mates = [(z, x, r, (y + d) % ny) for d in range(1, ny)] + [(z, x, 1 - r, (y + d) % ny) for d in range(ny)]
    across = [(d, (x + d) % NX) for d in (2, 1, 3)]
    load = pltpu.make_async_copy(weights, w_out, own.at[0])
    load.start()
    keep_hid = pltpu.make_async_copy(hidden, hid.at[r], own.at[1])
    keep_hid.start()
    greet([up, down] + mates + [(z, tx, r, y) for _, tx in across])
    span = teacher.shape[2]
    wing = span // count
    per = nz // 2
    every = slice(None)
    copies = [{} for _ in range(4 * count + 1)]
    swap_hid = remote(hidden, hid.at[r], hsend, hrecv, sibling)
    swap_hid.start()
    loss[...] = jnp.zeros_like(loss)

    def sems(k):
        return send.at[k], recv.at[k], copies[k]

    def trio(axis_size):
        return (pl.ds(0, axis_size),), (pl.ds(0, axis_size // 2),), (pl.ds(axis_size // 2, axis_size // 2),)

    def lanes(size):
        return tuple((every, pl.ds(o, s)) for o, s in ((0, size), (0, size // 2), (size // 2, size // 2)))

    along_x, along_y = (NX, x, east, west), (ny, y, north, south)
    swaps = []

    def flow(f):
        cut = pl.ds(f * wing, wing)
        parts, gaps, scame, sleave, mid, came2, leave2 = buffers[7 * f:7 * f + 7]
        x_first = f < count // 2
        one, two = (along_x, along_y) if x_first else (along_y, along_x)

        def outer(d, p):
            return (d,) + p if x_first else p + (d,)

        def inner(d, p):
            return (x, d) + p if x_first else (d, y) + p

        @pl.loop(0, NX)
        def _(i):
            rows = pl.ds(pl.multiple_of(i * tok, tok), tok)
            value = jnp.dot(hid[0, rows], w_out[0, f], preferred_element_type=F32)
            value += jnp.dot(hid[1, rows], w_out[1, f], preferred_element_type=F32)
            parts[i] = value.astype(BF).reshape(parts.shape[1:])

        yield from ring_sum(*one, parts, outer, [trio(two[0])], scame, sleave, *sems(4 * f))
        last = one[0] // 2 - 1
        kept = parts[x] if x_first else parts[:, y]
        mid[...] = (kept.astype(F32) + scame[0, last].astype(F32) + scame[1, last].astype(F32)).astype(BF)
        yield from ring_sum(*two, mid, lambda d, p: (d,) + p, [lanes(wing)], came2, leave2, *sems(4 * f + 1))
        last = two[0] // 2 - 1
        student = mid[two[1]].astype(F32) + came2[0, last].astype(F32) + came2[1, last].astype(F32)
        taught = teacher[z, :, cut].astype(F32) + tcame[0, per - 1, :, cut].astype(F32) + tcame[1, per - 1, :, cut].astype(F32)
        gap = student - taught
        gaps[x, y] = gap.astype(BF)
        square = gap * gap
        loss[...] += sum(square[:, t * 128:(t + 1) * 128] for t in range(wing // 128))
        yield from ring_gather(*two, gaps, inner, *lanes(wing), *sems(4 * f + 2))
        yield from ring_gather(*one, gaps, outer, *trio(two[0]), *sems(4 * f + 3))
        whole = gaps[...].reshape(NX * tok, wing)

        def term(core):
            value = lax.dot_general(hid[core], whole, (((0,), (0,)), ((), ())), preferred_element_type=F32)
            return (value / tok).astype(BF)

        give[f] = term(1 - r)
        slot = r * per + f
        swaps.append(remote(give.at[f], chunks.at[slot], csend.at[f], crecv.at[f], sibling))
        swaps[-1].start()
        chunks[slot] = term(r)

    teach = ring_sum(nz, z, up, down, teacher, lambda d, p: (d,) + p, [lanes(span)], tcame, tleave, *sems(4 * count))
    next(teach)
    load.wait()
    keep_hid.wait()
    swap_hid.wait_recv()
    half = count // 2
    flows = [flow(k) for pair in zip(range(half), range(half, count)) for k in pair]
    for one in flows:
        next(one)
    together(teach, *flows)
    place = r * ny + y
    tells = [remote(loss, losses.at[place], lsend.at[k], lrecv.at[k], device) for k, device in enumerate(mates)]
    keep_loss = pltpu.make_async_copy(loss, losses.at[place], own.at[2])
    for copy in tells + [keep_loss]:
        copy.start()
    for copy in swaps:
        copy.wait_recv()
    rows, span = chunks.shape[1], chunks.shape[2]
    subs = []
    for u in (0, 1):
        band = pl.ds(u * (rows // 2), rows // 2)
        subs.append(((band, pl.ds(0, span)), (band, pl.ds(0, span // 2)), (band, pl.ds(span // 2, span // 2))))
    ring = {}
    size = span // NX
    outs = []

    def spread(u):
        band = subs[u][0][0]
        value = chunks[z, band].astype(F32) + came[0, per - 1, band].astype(F32) + came[1, per - 1, band].astype(F32)
        total[band] = value.astype(BF)
        for d, tx in across:
            copy = remote(total.at[band, lanes_at(tx, size)], grad.at[x, band], xsend.at[d - 1, u], xrecv.at[d - 1, u], (z, tx, r, y))
            copy.start()
            outs.append(copy)
        copy = pltpu.make_async_copy(total.at[band, lanes_at(x, size)], grad.at[x, band], own.at[3 + u])
        copy.start()
        outs.append(copy)

    together(ring_sum(nz, z, up, down, chunks, lambda d, p: (d,) + p, subs, came, leave, zsend, zrecv, ring, spread))
    for copy in [keep_loss] + outs + tells:
        copy.wait()
    for copy in swaps + [swap_hid] + list(ring.values()) + [c for group in copies for c in group.values()]:
        copy.wait_send()


def on_device(tokens, routes, route_weights, teacher_in, teacher_out, student_in, student_out):
    nz, nr, ny = lax.axis_size("z"), lax.axis_size("row"), lax.axis_size("col")
    z, x, r, y = here()
    tok, width = tokens.shape
    block, top = routes.shape
    blk = student_in.shape[1]
    ff = student_in.shape[2]
    sub = ff // NX
    half = width // nr
    experts = NX * ny
    cap = max(2, 3 * block * top // (2 * nz * experts))
    blocks = nz * NX
    shape = jax.ShapeDtypeStruct

    parts = jnp.concatenate([jnp.swapaxes(student_in, 1, 2), student_out[None]], axis=0)
    parts = pad_lanes(parts)
    lanes = parts.shape[-1]
    wide = blocks * lanes
    steps = nz // 2
    slots = nz * cap
    hid = teacher_in.shape[3]
    meta = jnp.concatenate([routes.astype(F32), route_weights], axis=1).T
    meta = jnp.pad(meta, ((0, 0), (0, 128 - block)))
    whole, far = pl.BlockSpec(memory_space=pltpu.VMEM), pl.BlockSpec(memory_space=pl.ANY)
    bf, f32 = (lambda *b: pltpu.VMEM(b, BF)), (lambda *b: pltpu.VMEM(b, F32))
    buffers = [bf(2, nz, sub, NX * lanes), bf(nz, sub, NX * lanes), bf(block, half), bf(NX, tok, wide), f32(nz, 2 * top, 128), f32(cap, experts * nz, nz * block), bf(experts, slots, half)]
    buffers += [bf(2, width, hid), bf(hid, width), bf(nz, block, half), bf(experts, slots, half), bf(experts, slots, width)]
    buffers += [bf(experts // 2 * slots, hid), bf(experts, slots, width)] + [bf(experts, slots, half)] * 2
    sems = [(3, 3)] * 2 + [(3, 2, steps, 1)] * 2 + [(2, steps)] * 4 + [(3,)] * 2 + [(2, 3)] * 2 + [(3, 3)] * 2
    sems += [(experts,)] * 4 + [(2,)] * 2 + [(experts,)] * 2 + [(steps,)] * 2 + [(9,)]
    hidden, student_down, teacher = kernel_call(
        functools.partial(front_kernel, nz, cap, blk), 0,
        [shape((NX * tok, sub), BF), shape((nr, steps, sub, NX * lanes), BF), shape((nz, block, wide // nr), BF)],
        buffers + [dma(*b) for b in sems],
        parts.reshape(3, NX, sub, lanes), meta, tokens, teacher_in[0], teacher_out[0],
        specs=[whole, whole, whole, far, far],
    )

    span = wide // nr
    count = steps
    wing = span // count
    chunk = NX * lanes
    flows = []
    for f in range(count):
        one, two = (NX, ny) if f < count // 2 else (ny, NX)
        flows += [(NX, ny, block, wing)] * 2
        flows += [(2, one // 2, two, block, wing), (2, one // 2 - 1, two, block, wing), (two, block, wing)]
        flows += [(2, two // 2, block, wing), (2, two // 2 - 1, block, wing)]
    buffers = [(nr, NX * tok, sub), (nr, steps, sub, chunk), (2, steps, block, span), (2, steps - 1, block, span), (nz, sub, chunk), (steps, sub, chunk)]
    buffers += [(2, steps, sub, chunk), (2, steps - 1, sub, chunk), (sub, chunk)]
    grad, losses = kernel_call(
        functools.partial(tail_kernel, nz, count, tok), 4,
        [shape((NX, sub, lanes), BF), shape((nr * ny, block, 128), F32)],
        [pltpu.VMEM(b, BF) for b in buffers] + [pltpu.VMEM((block, 128), F32)]
        + [dma(4 * count + 1, 2, steps, 1)] * 2 + [dma(2, steps, 2)] * 2 + [dma(steps)] * 2 + [pltpu.SemaphoreType.DMA] * 2 + [dma(3, 2)] * 2
        + [dma(2 * ny - 1)] * 2 + [dma(5)]
        + [pltpu.VMEM(b, BF) for b in flows],
        hidden, student_down, teacher,
        specs=[whole, far, whole],
    )
    token_loss = jnp.sum(losses.reshape(nr, ny * block, 128), axis=(0, 2)) / width
    grad = grad.reshape(ff, lanes)[:, :blk].astype(F32)
    return token_loss, grad


def solution(mesh):
    dp = ("z", "x")
    in_specs = (
        P(dp, None),
        P(dp + ("col",), None),
        P(dp + ("col",), None),
        P(dp + ("col",), None, None, "row"),
        P(dp + ("col",), "row", None),
        P(None, dp, ("row", "col")),
        P(("row", "col"), dp),
    )
    out_specs = (P(dp), P(("row", "col"), dp))
    return jax.shard_map(
        on_device, mesh=split_mesh(mesh), in_specs=in_specs, out_specs=out_specs, check_vma=False
    )
```

```python
import functools

import jax
import jax.numpy as jnp
from jax import lax
from jax.experimental import pallas as pl
from jax.experimental.pallas import tpu as pltpu
from jax.sharding import Mesh, PartitionSpec as P

NX = 4
MESH = pl.DeviceIdType.MESH
F32 = jnp.float32
BF = jnp.bfloat16


def split_mesh(mesh):
    dp, row, col = mesh.devices.shape
    return Mesh(mesh.devices.reshape(dp // NX, NX, row, col), ("z", "x", "row", "col"))


def dot(a, b, dims):
    return lax.dot_general(a, b, (dims, ((), ())), preferred_element_type=F32)


def pad_lanes(a):
    lanes = a.shape[-1]
    wide = -(-lanes // 128) * 128
    return jnp.pad(a, [(0, 0)] * (a.ndim - 1) + [(0, wide - lanes)])


def here():
    return tuple(lax.axis_index(a) for a in ("z", "x", "row", "col"))


def remote(src, dst, send, recv, device):
    return pltpu.make_async_remote_copy(
        src_ref=src, dst_ref=dst, send_sem=send, recv_sem=recv, device_id=device, device_id_type=MESH
    )


def greet(devices):
    barrier = pltpu.get_barrier_semaphore()
    for device in devices:
        pl.semaphore_signal(barrier, inc=1, device_id=device, device_id_type=MESH)
    pl.semaphore_wait(barrier, len(devices))


def lanes_at(start, size):
    return pl.ds(pl.multiple_of(start * size, size), size)


def kernel_call(body, number, outs, scratch, *args, specs=None, out_specs=None):
    whole = pl.BlockSpec(memory_space=pltpu.VMEM)
    return pl.pallas_call(
        body,
        out_shape=outs,
        in_specs=specs or [whole] * len(args),
        out_specs=out_specs or [whole] * len(outs),
        scratch_shapes=scratch,
        compiler_params=pltpu.CompilerParams(
            collective_id=number, has_side_effects=True, vmem_limit_bytes=56 * 1024 * 1024
        ),
    )(*args)


def dma(*shape):
    return pltpu.SemaphoreType.DMA(shape)


def plane_steps(ny):
    steps = [(dx, dy) for dx in range(NX) for dy in range(ny) if dx or dy]
    far = lambda s: min(s[0], NX - s[0]) + min(s[1], ny - s[1])
    return sorted(steps, key=far, reverse=True)


def token_gather(tokens, blk, plane, xs, xr, ys, yr, cs, cr, started):
    z, x, r, y = here()
    ny = lax.axis_size("col")
    north, south = (y + 1) % ny, (y + ny - 1) % ny
    sibling = (z, x, 1 - r, y)
    rows, wide = plane.shape[1], plane.shape[2]
    high, span = rows // 2, wide // 2
    quarter = span // 2
    mine_rows = pl.ds(pl.multiple_of(r * high, high), high)
    parity = y % 2
    held = lanes_at(parity, span)

    def go(copy):
        copy.start()
        started.append(copy)
        return copy

    def x_step(d):
        device = (z, (x + d) % NX, r, y)
        piece = plane.at[x, mine_rows, held]
        return go(remote(piece, piece, xs.at[d - 1], xr.at[d - 1], device))

    from_sib, from_y = [], []

    def onward(d, copy):
        copy.wait_recv()
        source = (x + NX - d) % NX
        for side, device in ((0, (z, x, r, north)), (1, (z, x, r, south))):
            piece = plane.at[source, mine_rows, lanes_at(parity * 2 + side, quarter)]
            from_y.append((d, side, go(remote(piece, piece, ys.at[side, d - 1], yr.at[side, d - 1], device))))
        piece = plane.at[source, mine_rows, held]
        from_sib.append(go(remote(piece, piece, cs.at[0, d - 1], cr.at[0, d - 1], sibling)))

    def inward():
        while from_y:
            d, side, copy = from_y.pop(0)
            copy.wait_recv()
            source = (x + NX - d) % NX
            piece = plane.at[source, mine_rows, lanes_at((1 - parity) * 2 + side, quarter)]
            from_sib.append(go(remote(piece, piece, cs.at[1 + side, d - 1], cr.at[1 + side, d - 1], sibling)))

    band = 32
    lanes = -(-blk // 128) * 128

    @pl.loop(0, rows // band)
    def _(i):
        cut = pl.ds(pl.multiple_of(i * band, band), band)
        value = tokens[cut].astype(F32)
        empty = jnp.zeros((band, lanes - blk), F32)
        for b in range(wide // lanes):
            piece = jnp.concatenate([value[:, b * blk:(b + 1) * blk], empty], axis=1)
            plane[x, cut, b * lanes:(b + 1) * lanes] = piece.astype(BF)

    first, third = x_step(1), x_step(3)
    yield
    onward(1, first)
    onward(3, third)
    second = x_step(2)
    yield
    inward()
    onward(2, second)
    yield
    inward()
    for copy in from_sib:
        copy.wait_recv()


def block_gather(nz, mine, meta, column, metas, zs, zr, ms, mr, own, started):
    z, x, r, y = here()
    up, down = (z + 1) % nz, (z + nz - 1) % nz
    half = mine.shape[1] // 2

    def go(copy):
        copy.start()
        started.append(copy)
        return copy

    local = [pltpu.make_async_copy(mine, column.at[z], own.at[0]), pltpu.make_async_copy(meta, metas.at[z], own.at[1])]
    for copy in local:
        copy.start()
    ring = []
    for s in range(1, nz // 2 + 1):
        for copy in ring:
            copy.wait_recv()
        a, b = (z + nz - s + 1) % nz, (z + s - 1) % nz
        one, two, three, four = (mine, mine, meta, meta) if s == 1 else (column.at[a], column.at[b], metas.at[a], metas.at[b])
        to_a, to_b = column.at[a], column.at[b]
        if s == nz // 2:
            low, top = pl.ds(0, half), pl.ds(half, half)
            one, to_a, two, to_b = column.at[a, :, low], column.at[a, :, low], column.at[b, :, top], column.at[b, :, top]
        ring = [
            go(remote(one, to_a, zs.at[0, s - 1], zr.at[0, s - 1], (up, x, r, y))),
            go(remote(two, to_b, zs.at[1, s - 1], zr.at[1, s - 1], (down, x, r, y))),
            go(remote(three, metas.at[a], ms.at[0, s - 1], mr.at[0, s - 1], (up, x, r, y))),
        ]
        if s < nz // 2:
            ring.append(go(remote(four, metas.at[b], ms.at[1, s - 1], mr.at[1, s - 1], (down, x, r, y))))
        yield
    for copy in ring:
        copy.wait_recv()
    for copy in local:
        copy.wait()


def place_rows(nz, cap, column, metas, outgoing, weighted):
    z = lax.axis_index("z")
    block, half = column.shape[1], column.shape[2]
    experts = outgoing.shape[0]
    top = metas.shape[1] // 2
    count = nz * block
    named = jnp.concatenate([metas[b, :top, :block] for b in range(nz)], axis=1)
    weights = jnp.concatenate([metas[b, top:, :block] for b in range(nz)], axis=1)
    ids = (z * experts + lax.broadcasted_iota(jnp.int32, (experts, 1), 0)).astype(F32)
    hit = jnp.zeros((experts, count), F32)
    weight = jnp.zeros((experts, count), F32)
    for k in range(top):
        hit += jnp.where(named[k:k + 1] == ids, 1.0, 0.0)
        weight += jnp.where(named[k:k + 1] == ids, weights[k:k + 1], 0.0)
    before, after = lax.broadcasted_iota(jnp.int32, (count, count), 0), lax.broadcasted_iota(jnp.int32, (count, count), 1)
    earlier = jnp.where((before < after) & (before // block == after // block), 1.0, 0.0).astype(BF)
    slot = jnp.dot(hit.astype(BF), earlier, preferred_element_type=F32)
    lane = lax.broadcasted_iota(jnp.int32, (nz, count), 1) // block
    inside = jnp.where(lane == lax.broadcasted_iota(jnp.int32, (nz, count), 0), 1.0, 0.0)
    rows = column[...].reshape(count, half)
    for s in range(cap):
        chosen = jnp.where(slot == float(s), hit, 0.0)
        placing = (chosen[:, None, :] * inside[None]).reshape(experts * nz, count).astype(BF)
        value = jnp.dot(placing, rows, preferred_element_type=F32).astype(BF)
        outgoing[:, s * nz:(s + 1) * nz, :] = value.reshape(experts, nz, half)
        chosen = jnp.where(slot == float(s), weight, 0.0)
        weighted[s] = (chosen[:, None, :] * inside[None]).reshape(experts * nz, count)


def weigh_rows(nz, cap, weighted, back, teacher, blk):
    experts, half = back.shape[0], back.shape[2]
    count = weighted.shape[2]
    total = jnp.zeros((count, half), F32)
    for s in range(cap):
        rows = back[:, s * nz:(s + 1) * nz, :].reshape(experts * nz, half)
        value = weighted[s]
        high = value.astype(BF)
        low = (value - high.astype(F32)).astype(BF)
        for term in (high, low):
            total += lax.dot_general(term, rows, (((0,), (0,)), ((), ())), preferred_element_type=F32)
    lanes = -(-blk // 128) * 128
    empty = jnp.zeros((count, lanes - blk), F32)
    for b in range(half // blk):
        piece = jnp.concatenate([total[:, b * blk:(b + 1) * blk], empty], axis=1).astype(BF)
        teacher[:, :, b * lanes:(b + 1) * lanes] = piece.reshape(nz, count // nz, lanes)


def front_kernel(nz, cap, blk, parts, meta, own_tokens, inner, outer, hidden, down_both, teacher,
                 student, student_down, mine, plane, metas, weighted, back, w_in, w_out, column, outgoing, got, act, part, other, total,
                 ws, wr, rs, rr, zs, zr, ms, mr, xs, xr, ys, yr, cs, cr, send, recv, fsend, frecv, csend, crecv, bsend, brecv, dsend, drecv, own):
    z, x, r, y = here()
    ny = lax.axis_size("col")
    steps = plane_steps(ny)[::-1]
    sibling = (z, x, 1 - r, y)
    up, down_z = ((z + 1) % nz, x, r, y), ((z + nz - 1) % nz, x, r, y)
    per = nz // 2
    loads = [pltpu.make_async_copy(inner, w_in, own.at[1]), pltpu.make_async_copy(outer, w_out, own.at[2])]
    for copy in loads:
        copy.start()
    peers = [(z, (x + dx) % NX, r, (y + dy) % ny) for dx, dy in steps]
    greet(peers + [sibling, up, down_z])
    started = []
    block, half = mine.shape
    mine[...] = own_tokens[pl.ds(pl.multiple_of(y * block, 8), block), lanes_at(r, half)]
    blocks = block_gather(nz, mine, meta, column, metas, zs, zr, ms, mr, own.at[pl.ds(3, 2)], started)
    tokens = token_gather(own_tokens, blk, plane, xs, xr, ys, yr, cs, cr, started)
    next(blocks)

    span = NX * 128
    exchange = [[], [], []]
    homes = [student.at[0], student.at[1], student_down]
    lane = lanes_at(x, 128)
    for kind in (0, 1, 2):
        for d in (2, 1, 3):
            to = (x + d) % NX
            copy = remote(parts.at[kind, to], homes[kind].at[z, :, lane], ws.at[d - 1, kind], wr.at[d - 1, kind], (z, to, r, y))
            copy.start()
            started.append(copy)
            exchange[kind].append(copy)
    local = [pltpu.make_async_copy(parts.at[k, x], homes[k].at[z, :, lane], own.at[5 + k]) for k in range(3)]
    for copy in local:
        copy.start()
    next(tokens)

    def chunk(d, p):
        return (d, slice(None), pl.ds(*p))

    rings = [{}, {}, {}]
    idle = 128 - blk
    riders = 2 * NX - 1
    packed = riders * idle == blk
    last = slice(span - 128, span)

    def spot(d, i):
        return i // NX, d, slice(None), slice(i % NX * 128, (i % NX + 1) * 128)

    def pack():
        value = student[1, z, :, last].astype(F32)
        for i in range(riders):
            kept = student[spot(z, i)].astype(F32)[:, :blk]
            student[spot(z, i)] = jnp.concatenate([kept, value[:, i * idle:(i + 1) * idle]], axis=1).astype(BF)

    def unpack():
        @pl.loop(0, nz)
        def _(d):
            pieces = [student[spot(d, i)].astype(F32)[:, blk:] for i in range(riders)]
            empty = jnp.zeros((student.shape[2], idle), F32)
            student[1, d, :, last] = jnp.concatenate(pieces + [empty], axis=1).astype(BF)

    sizes = [span, span - 128 if packed else span, span]
    gathers = [
        ring_gather(nz, z, up, down_z, homes[kind], chunk, (0, sizes[kind]), (0, span // 2), (span // 2, sizes[kind] - span // 2),
                    rs.at[kind], rr.at[kind], rings[kind])
        for kind in range(3)
    ]

    def serve(*kinds):
        for kind in kinds:
            next(gathers[kind], None)

    for _ in range(per - 2):
        next(blocks)
    for kind in range(3):
        local[kind].wait()
        for copy in exchange[kind]:
            copy.wait_recv()
        if kind == 1:
            if packed:
                pack()
            serve(0, 1)
        if kind == 0:
            next(blocks)
    next(tokens)
    next(blocks, None)

    place_rows(nz, cap, column, metas, outgoing, weighted)
    steps = [(0, 0)] + steps
    me = x * ny + y
    keep, give = lanes_at(r, half), lanes_at(1 - r, half)
    near = len(steps) // 2
    groups = (range(near), range(near, len(steps)))
    sends, forwards, swaps, returns = {}, {}, {}, []

    def forward(k, src):
        forwards[k] = remote(src, got.at[k, :, keep], fsend.at[k], frecv.at[k], sibling)
        forwards[k].start()

    for k, (dx, dy) in enumerate(steps):
        if k:
            tx, ty = (x + dx) % NX, (y + dy) % ny
            sends[k] = remote(outgoing.at[tx * ny + ty], got.at[k, :, keep], send.at[k], recv.at[k], (z, tx, r, ty))
            sends[k].start()
    own_rows = pltpu.make_async_copy(outgoing.at[me], got.at[0, :, keep], own.at[0])
    own_rows.start()
    forward(0, outgoing.at[me])
    serve(0, 1)

    def finish(g):
        swaps[g].wait_recv()
        for k in groups[g]:
            dx, dy = steps[k]
            tx, ty = (x + NX - dx) % NX, (y + ny - dy) % ny
            value = (part[k, :, keep].astype(F32) + other[k].astype(F32)).astype(BF)
            if k:
                total[k] = value
                returns.append(remote(total.at[k], back.at[me], bsend.at[k], brecv.at[k], (z, tx, r, ty)))
                returns[-1].start()
            else:
                back[me] = value

    for g, group in enumerate(groups):
        slots = pl.ds(group[0], near)
        for k in group:
            if k:
                sends[k].wait_recv()
                forward(k, got.at[k, :, keep])
        if g == 0:
            own_rows.wait()
            loads[0].wait()
        for k in group:
            forwards[k].wait_recv()
        rows = near * outgoing.shape[1]
        tile = w_in.shape[2] // 2

        @pl.loop(0, 2)
        def _(j):
            lhs = got[slots].reshape(rows, got.shape[2])
            cut = pl.ds(pl.multiple_of(j * tile, tile), tile)
            gate = jnp.dot(lhs, w_in[0, :, cut], preferred_element_type=F32)
            up_part = jnp.dot(lhs, w_in[1, :, cut], preferred_element_type=F32)
            act[:, cut] = (gate / (1.0 + jnp.exp(-gate)) * up_part).astype(BF)

        if g == 0:
            loads[1].wait()
        wide = half // 2

        def down(side):
            @pl.loop(0, 2)
            def _(j):
                cut = pl.ds(pl.multiple_of(side * half + j * wide, wide), wide)
                value = jnp.dot(act[...], w_out[:, cut], preferred_element_type=F32).astype(BF)
                part[slots, :, cut] = value.reshape(near, outgoing.shape[1], wide)

        down(1 - r)
        swaps[g] = remote(part.at[slots, :, give], other.at[slots], csend.at[g], crecv.at[g], sibling)
        swaps[g].start()
        down(r)
        if g == 0:
            serve(0, 1, 2)
        finish(g)
        if g == 1:
            serve(0, 1, 2)
        next(tokens, None)

    serve(0, 1, 2)
    if packed:
        unpack()
    tok = plane.shape[1]

    def units(kind, i):
        total = jnp.zeros((2 * tok, student.shape[2]), F32)
        for d in range(nz):
            rows = plane[2 * i:2 * i + 2, :, d * span:(d + 1) * span].reshape(2 * tok, span)
            total += lax.dot_general(rows, student[kind, d], (((1,), (1,)), ((), ())), preferred_element_type=F32)
        return total

    for i in range(NX // 2):
        gate = units(0, i)
        hidden[r, 2 * i * tok:2 * (i + 1) * tok] = (gate / (1.0 + jnp.exp(-gate)) * units(1, i)).astype(BF)
        if i == 0:
            serve(2)
    for copy in returns:
        copy.wait_recv()
    changes = [remote(hidden.at[r], hidden.at[r], dsend.at[per], drecv.at[per], sibling)]
    changes[0].start()
    for i in (1, 2, 3, 0):
        if i == 0:
            weigh_rows(nz, cap, weighted, back, teacher, blk)
            serve(2)
        q = (z + i) % per
        src = student_down.at[(1 - r) * per + q]
        changes.append(remote(src, down_both.at[r, q], dsend.at[i], drecv.at[i], sibling))
        changes[-1].start()
    local = [pltpu.make_async_copy(student_down.at[r * per + q], down_both.at[r, q], own.at[5 + q]) for q in range(per)]
    for copy in local:
        copy.start()
    for copy in local + changes:
        copy.wait()
    for copy in started + returns + list(sends.values()) + list(forwards.values()) + list(swaps.values()):
        copy.wait_send()
    for ring in rings:
        for copy in ring.values():
            copy.wait_send()


def ring_sum(n, i, up, down, ref, where, subs, came, leave, send, recv, copies, done=None):
    half = n // 2

    def go(way, s, u, src, dst):
        copy = remote(src, dst, send.at[way, s, u], recv.at[way, s, u], (up, down)[way])
        copy.start()
        copies[way, s, u] = copy

    for u, (whole, low, top) in enumerate(subs):
        for way, part in ((0, low), (1, top)):
            go(way, 0, u, ref.at[where((i + half) % n, part)], came.at[(way, 0) + part])
    yield
    for s in range(1, half):
        for u, (whole, low, top) in enumerate(subs):
            for way in (0, 1):
                d = (i + half - s) % n if way == 0 else (i + half + s) % n
                copies[way, s - 1, u].wait_recv()
                summed, plain = whole, None
                if s == 1:
                    summed, plain = (low, top) if way == 0 else (top, low)
                    leave[(way, 0) + plain] = ref[where(d, plain)]
                value = ref[where(d, summed)].astype(F32) + came[(way, s - 1) + summed].astype(F32)
                leave[(way, s - 1) + summed] = value.astype(BF)
                go(way, s, u, leave.at[(way, s - 1) + whole], came.at[(way, s) + whole])
        yield
    for u in range(len(subs)):
        for way in (0, 1):
            copies[way, half - 1, u].wait_recv()
        if done:
            done(u)


def ring_gather(n, i, up, down, ref, where, whole, low, top, send, recv, copies):
    half = n // 2
    for s in range(half):
        for way, device in ((0, up), (1, down)):
            d = (i + n - s) % n if way == 0 else (i + s) % n
            if s:
                copies[way, s - 1].wait_recv()
            part = whole if s < half - 1 else (low, top)[way]
            piece = ref.at[where(d, part)]
            copies[way, s] = remote(piece, piece, send.at[way, s, 0], recv.at[way, s, 0], device)
            copies[way, s].start()
        yield
    for way in (0, 1):
        copies[way, half - 1].wait_recv()


def together(*rings):
    rings = list(rings)
    while rings:
        for ring in list(rings):
            try:
                next(ring)
            except StopIteration:
                rings.remove(ring)


def tail_kernel(nz, count, tok, hid, weights, teacher, grad, losses, w_out, tcame, tleave, chunks, give, came, leave, total, loss,
                send, recv, zsend, zrecv, csend, crecv, xsend, xrecv, lsend, lrecv, own, *buffers):
    z, x, r, y = here()
    ny = lax.axis_size("col")
    up, down = ((z + 1) % nz, x, r, y), ((z + nz - 1) % nz, x, r, y)
    east, west = (z, (x + 1) % NX, r, y), (z, (x + NX - 1) % NX, r, y)
    north, south = (z, x, r, (y + 1) % ny), (z, x, r, (y + ny - 1) % ny)
    sibling = (z, x, 1 - r, y)
    mates = [(z, x, r, (y + d) % ny) for d in range(1, ny)] + [(z, x, 1 - r, (y + d) % ny) for d in range(ny)]
    across = [(d, (x + d) % NX) for d in (2, 1, 3)]
    load = pltpu.make_async_copy(weights, w_out, own.at[0])
    load.start()
    greet([up, down] + mates + [(z, tx, r, y) for _, tx in across])
    span = teacher.shape[2]
    wing = span // count
    per = nz // 2
    every = slice(None)
    copies = [{} for _ in range(4 * count + 1)]
    loss[...] = jnp.zeros_like(loss)

    def sems(k):
        return send.at[k], recv.at[k], copies[k]

    def trio(axis_size):
        return (pl.ds(0, axis_size),), (pl.ds(0, axis_size // 2),), (pl.ds(axis_size // 2, axis_size // 2),)

    def lanes(size):
        return tuple((every, pl.ds(o, s)) for o, s in ((0, size), (0, size // 2), (size // 2, size // 2)))

    along_x, along_y = (NX, x, east, west), (ny, y, north, south)
    swaps = []

    def flow(f):
        cut = pl.ds(f * wing, wing)
        parts, gaps, scame, sleave, mid, came2, leave2 = buffers[7 * f:7 * f + 7]
        x_first = f < count // 2
        one, two = (along_x, along_y) if x_first else (along_y, along_x)

        def outer(d, p):
            return (d,) + p if x_first else p + (d,)

        def inner(d, p):
            return (x, d) + p if x_first else (d, y) + p

        @pl.loop(0, NX)
        def _(i):
            rows = pl.ds(pl.multiple_of(i * tok, tok), tok)
            value = jnp.dot(hid[0, rows], w_out[0, f], preferred_element_type=F32)
            value += jnp.dot(hid[1, rows], w_out[1, f], preferred_element_type=F32)
            parts[i] = value.astype(BF).reshape(parts.shape[1:])

        yield from ring_sum(*one, parts, outer, [trio(two[0])], scame, sleave, *sems(4 * f))
        last = one[0] // 2 - 1
        kept = parts[x] if x_first else parts[:, y]
        mid[...] = (kept.astype(F32) + scame[0, last].astype(F32) + scame[1, last].astype(F32)).astype(BF)
        yield from ring_sum(*two, mid, lambda d, p: (d,) + p, [lanes(wing)], came2, leave2, *sems(4 * f + 1))
        last = two[0] // 2 - 1
        student = mid[two[1]].astype(F32) + came2[0, last].astype(F32) + came2[1, last].astype(F32)
        taught = teacher[z, :, cut].astype(F32) + tcame[0, per - 1, :, cut].astype(F32) + tcame[1, per - 1, :, cut].astype(F32)
        gap = student - taught
        gaps[x, y] = gap.astype(BF)
        square = gap * gap
        loss[...] += sum(square[:, t * 128:(t + 1) * 128] for t in range(wing // 128))
        yield from ring_gather(*two, gaps, inner, *lanes(wing), *sems(4 * f + 2))
        yield from ring_gather(*one, gaps, outer, *trio(two[0]), *sems(4 * f + 3))
        whole = gaps[...].reshape(NX * tok, wing)

        def term(core):
            value = lax.dot_general(hid[core], whole, (((0,), (0,)), ((), ())), preferred_element_type=F32)
            return (value / tok).astype(BF)

        give[f] = term(1 - r)
        slot = r * per + f
        swaps.append(remote(give.at[f], chunks.at[slot], csend.at[f], crecv.at[f], sibling))
        swaps[-1].start()
        chunks[slot] = term(r)

    teach = ring_sum(nz, z, up, down, teacher, lambda d, p: (d,) + p, [lanes(span)], tcame, tleave, *sems(4 * count))
    next(teach)
    load.wait()
    half = count // 2
    flows = [flow(k) for pair in zip(range(half), range(half, count)) for k in pair]
    for one in flows:
        next(one)
    together(teach, *flows)
    place = r * ny + y
    tells = [remote(loss, losses.at[place], lsend.at[k], lrecv.at[k], device) for k, device in enumerate(mates)]
    keep_loss = pltpu.make_async_copy(loss, losses.at[place], own.at[2])
    for copy in tells + [keep_loss]:
        copy.start()
    for copy in swaps:
        copy.wait_recv()
    rows, span = chunks.shape[1], chunks.shape[2]
    subs = []
    for u in range(3):
        band = pl.ds(u * (rows // 3), rows // 3)
        subs.append(((band, pl.ds(0, span)), (band, pl.ds(0, span // 2)), (band, pl.ds(span // 2, span // 2))))
    ring = {}
    size = span // NX
    outs = []

    def spread(u):
        band = subs[u][0][0]
        value = chunks[z, band].astype(F32) + came[0, per - 1, band].astype(F32) + came[1, per - 1, band].astype(F32)
        total[band] = value.astype(BF)
        for d, tx in across:
            copy = remote(total.at[band, lanes_at(tx, size)], grad.at[x, band], xsend.at[d - 1, u], xrecv.at[d - 1, u], (z, tx, r, y))
            copy.start()
            outs.append(copy)
        copy = pltpu.make_async_copy(total.at[band, lanes_at(x, size)], grad.at[x, band], own.at[3 + u])
        copy.start()
        outs.append(copy)

    together(ring_sum(nz, z, up, down, chunks, lambda d, p: (d,) + p, subs, came, leave, zsend, zrecv, ring, spread))
    for copy in [keep_loss] + outs + tells:
        copy.wait()
    for copy in swaps + list(ring.values()) + [c for group in copies for c in group.values()]:
        copy.wait_send()


def on_device(tokens, routes, route_weights, teacher_in, teacher_out, student_in, student_out):
    nz, nr, ny = lax.axis_size("z"), lax.axis_size("row"), lax.axis_size("col")
    z, x, r, y = here()
    tok, width = tokens.shape
    block, top = routes.shape
    blk = student_in.shape[1]
    ff = student_in.shape[2]
    sub = ff // NX
    half = width // nr
    experts = NX * ny
    cap = max(2, 3 * block * top // (2 * nz * experts))
    blocks = nz * NX
    shape = jax.ShapeDtypeStruct

    parts = jnp.concatenate([jnp.swapaxes(student_in, 1, 2), student_out[None]], axis=0)
    parts = pad_lanes(parts)
    lanes = parts.shape[-1]
    wide = blocks * lanes
    steps = nz // 2
    slots = nz * cap
    hid = teacher_in.shape[3]
    meta = jnp.concatenate([routes.astype(F32), route_weights], axis=1).T
    meta = jnp.pad(meta, ((0, 0), (0, 128 - block)))
    whole, far = pl.BlockSpec(memory_space=pltpu.VMEM), pl.BlockSpec(memory_space=pl.ANY)
    bf, f32 = (lambda *b: pltpu.VMEM(b, BF)), (lambda *b: pltpu.VMEM(b, F32))
    buffers = [bf(2, nz, sub, NX * lanes), bf(nz, sub, NX * lanes), bf(block, half), bf(NX, tok, wide), f32(nz, 2 * top, 128), f32(cap, experts * nz, nz * block), bf(experts, slots, half)]
    buffers += [bf(2, width, hid), bf(hid, width), bf(nz, block, half), bf(experts, slots, half), bf(experts, slots, width)]
    buffers += [bf(experts // 2 * slots, hid), bf(experts, slots, width)] + [bf(experts, slots, half)] * 2
    sems = [(3, 3)] * 2 + [(3, 2, steps, 1)] * 2 + [(2, steps)] * 4 + [(3,)] * 2 + [(2, 3)] * 2 + [(3, 3)] * 2
    sems += [(experts,)] * 4 + [(2,)] * 2 + [(experts,)] * 2 + [(steps + 1,)] * 2 + [(9,)]
    hidden, student_down, teacher = kernel_call(
        functools.partial(front_kernel, nz, cap, blk), 0,
        [shape((nr, NX * tok, sub), BF), shape((nr, steps, sub, NX * lanes), BF), shape((nz, block, wide // nr), BF)],
        buffers + [dma(*b) for b in sems],
        parts.reshape(3, NX, sub, lanes), meta, tokens, teacher_in[0], teacher_out[0],
        specs=[whole, whole, whole, far, far],
    )

    span = wide // nr
    count = steps
    wing = span // count
    chunk = NX * lanes
    flows = []
    for f in range(count):
        one, two = (NX, ny) if f < count // 2 else (ny, NX)
        flows += [(NX, ny, block, wing)] * 2
        flows += [(2, one // 2, two, block, wing), (2, one // 2 - 1, two, block, wing), (two, block, wing)]
        flows += [(2, two // 2, block, wing), (2, two // 2 - 1, block, wing)]
    buffers = [(nr, steps, sub, chunk), (2, steps, block, span), (2, steps - 1, block, span), (nz, sub, chunk), (steps, sub, chunk)]
    buffers += [(2, steps, sub, chunk), (2, steps - 1, sub, chunk), (sub, chunk)]
    grad, losses = kernel_call(
        functools.partial(tail_kernel, nz, count, tok), 4,
        [shape((NX, sub, lanes), BF), shape((nr * ny, block, 128), F32)],
        [pltpu.VMEM(b, BF) for b in buffers] + [pltpu.VMEM((block, 128), F32)]
        + [dma(4 * count + 1, 2, steps, 1)] * 2 + [dma(2, steps, 3)] * 2 + [dma(steps)] * 2 + [dma(3, 3)] * 2
        + [dma(2 * ny - 1)] * 2 + [dma(6)]
        + [pltpu.VMEM(b, BF) for b in flows],
        hidden, student_down, teacher,
        specs=[whole, far, whole],
    )
    token_loss = jnp.sum(losses.reshape(nr, ny * block, 128), axis=(0, 2)) / width
    grad = grad.reshape(ff, lanes)[:, :blk].astype(F32)
    return token_loss, grad


def solution(mesh):
    dp = ("z", "x")
    in_specs = (
        P(dp, None),
        P(dp + ("col",), None),
        P(dp + ("col",), None),
        P(dp + ("col",), None, None, "row"),
        P(dp + ("col",), "row", None),
        P(None, dp, ("row", "col")),
        P(("row", "col"), dp),
    )
    out_specs = (P(dp), P(("row", "col"), dp))
    return jax.shard_map(
        on_device, mesh=split_mesh(mesh), in_specs=in_specs, out_specs=out_specs, check_vma=False
    )
```

```python
import functools

import jax
import jax.numpy as jnp
from jax import lax
from jax.experimental import pallas as pl
from jax.experimental.pallas import tpu as pltpu
from jax.sharding import Mesh, PartitionSpec as P

NX = 4
MESH = pl.DeviceIdType.MESH
F32 = jnp.float32
BF = jnp.bfloat16


def split_mesh(mesh):
    dp, row, col = mesh.devices.shape
    return Mesh(mesh.devices.reshape(dp // NX, NX, row, col), ("z", "x", "row", "col"))


def dot(a, b, dims):
    return lax.dot_general(a, b, (dims, ((), ())), preferred_element_type=F32)


def pad_lanes(a):
    lanes = a.shape[-1]
    wide = -(-lanes // 128) * 128
    return jnp.pad(a, [(0, 0)] * (a.ndim - 1) + [(0, wide - lanes)])


def here():
    return tuple(lax.axis_index(a) for a in ("z", "x", "row", "col"))


def remote(src, dst, send, recv, device):
    return pltpu.make_async_remote_copy(
        src_ref=src, dst_ref=dst, send_sem=send, recv_sem=recv, device_id=device, device_id_type=MESH
    )


def greet(devices):
    barrier = pltpu.get_barrier_semaphore()
    for device in devices:
        pl.semaphore_signal(barrier, inc=1, device_id=device, device_id_type=MESH)
    pl.semaphore_wait(barrier, len(devices))


def lanes_at(start, size):
    return pl.ds(pl.multiple_of(start * size, size), size)


def kernel_call(body, number, outs, scratch, *args, specs=None, out_specs=None):
    whole = pl.BlockSpec(memory_space=pltpu.VMEM)
    return pl.pallas_call(
        body,
        out_shape=outs,
        in_specs=specs or [whole] * len(args),
        out_specs=out_specs or [whole] * len(outs),
        scratch_shapes=scratch,
        compiler_params=pltpu.CompilerParams(
            collective_id=number, has_side_effects=True, vmem_limit_bytes=56 * 1024 * 1024
        ),
    )(*args)


def dma(*shape):
    return pltpu.SemaphoreType.DMA(shape)


def plane_steps(ny):
    steps = [(dx, dy) for dx in range(NX) for dy in range(ny) if dx or dy]
    far = lambda s: min(s[0], NX - s[0]) + min(s[1], ny - s[1])
    return sorted(steps, key=far, reverse=True)


def token_gather(tokens, blk, plane, xs, xr, ys, yr, cs, cr, started):
    z, x, r, y = here()
    ny = lax.axis_size("col")
    north, south = (y + 1) % ny, (y + ny - 1) % ny
    sibling = (z, x, 1 - r, y)
    rows, wide = plane.shape[1], plane.shape[2]
    high, span = rows // 2, wide // 2
    quarter = span // 2
    mine_rows = pl.ds(pl.multiple_of(r * high, high), high)
    parity = y % 2
    held = lanes_at(parity, span)

    def go(copy):
        copy.start()
        started.append(copy)
        return copy

    def x_step(d):
        device = (z, (x + d) % NX, r, y)
        piece = plane.at[x, mine_rows, held]
        return go(remote(piece, piece, xs.at[d - 1], xr.at[d - 1], device))

    from_sib, from_y = [], []

    def onward(d, copy):
        copy.wait_recv()
        source = (x + NX - d) % NX
        for side, device in ((0, (z, x, r, north)), (1, (z, x, r, south))):
            piece = plane.at[source, mine_rows, lanes_at(parity * 2 + side, quarter)]
            from_y.append((d, side, go(remote(piece, piece, ys.at[side, d - 1], yr.at[side, d - 1], device))))
        piece = plane.at[source, mine_rows, held]
        from_sib.append(go(remote(piece, piece, cs.at[0, d - 1], cr.at[0, d - 1], sibling)))

    def inward():
        while from_y:
            d, side, copy = from_y.pop(0)
            copy.wait_recv()
            source = (x + NX - d) % NX
            piece = plane.at[source, mine_rows, lanes_at((1 - parity) * 2 + side, quarter)]
            from_sib.append(go(remote(piece, piece, cs.at[1 + side, d - 1], cr.at[1 + side, d - 1], sibling)))

    band = 32
    lanes = -(-blk // 128) * 128

    @pl.loop(0, rows // band)
    def _(i):
        cut = pl.ds(pl.multiple_of(i * band, band), band)
        value = tokens[cut].astype(F32)
        empty = jnp.zeros((band, lanes - blk), F32)
        for b in range(wide // lanes):
            piece = jnp.concatenate([value[:, b * blk:(b + 1) * blk], empty], axis=1)
            plane[x, cut, b * lanes:(b + 1) * lanes] = piece.astype(BF)

    first, third = x_step(1), x_step(3)
    yield
    onward(1, first)
    onward(3, third)
    second = x_step(2)
    yield
    inward()
    onward(2, second)
    yield
    inward()
    for copy in from_sib:
        copy.wait_recv()


def block_gather(nz, mine, meta, column, metas, zs, zr, ms, mr, own, started):
    z, x, r, y = here()
    up, down = (z + 1) % nz, (z + nz - 1) % nz
    half = mine.shape[1] // 2

    def go(copy):
        copy.start()
        started.append(copy)
        return copy

    local = [pltpu.make_async_copy(mine, column.at[z], own.at[0]), pltpu.make_async_copy(meta, metas.at[z], own.at[1])]
    for copy in local:
        copy.start()
    ring = []
    for s in range(1, nz // 2 + 1):
        for copy in ring:
            copy.wait_recv()
        a, b = (z + nz - s + 1) % nz, (z + s - 1) % nz
        one, two, three, four = (mine, mine, meta, meta) if s == 1 else (column.at[a], column.at[b], metas.at[a], metas.at[b])
        to_a, to_b = column.at[a], column.at[b]
        if s == nz // 2:
            low, top = pl.ds(0, half), pl.ds(half, half)
            one, to_a, two, to_b = column.at[a, :, low], column.at[a, :, low], column.at[b, :, top], column.at[b, :, top]
        ring = [
            go(remote(one, to_a, zs.at[0, s - 1], zr.at[0, s - 1], (up, x, r, y))),
            go(remote(two, to_b, zs.at[1, s - 1], zr.at[1, s - 1], (down, x, r, y))),
            go(remote(three, metas.at[a], ms.at[0, s - 1], mr.at[0, s - 1], (up, x, r, y))),
        ]
        if s < nz // 2:
            ring.append(go(remote(four, metas.at[b], ms.at[1, s - 1], mr.at[1, s - 1], (down, x, r, y))))
        yield
    for copy in ring:
        copy.wait_recv()
    for copy in local:
        copy.wait()


def place_rows(nz, cap, column, metas, outgoing, weighted):
    z = lax.axis_index("z")
    block, half = column.shape[1], column.shape[2]
    experts = outgoing.shape[0]
    top = metas.shape[1] // 2
    count = nz * block
    named = jnp.concatenate([metas[b, :top, :block] for b in range(nz)], axis=1)
    weights = jnp.concatenate([metas[b, top:, :block] for b in range(nz)], axis=1)
    ids = (z * experts + lax.broadcasted_iota(jnp.int32, (experts, 1), 0)).astype(F32)
    hit = jnp.zeros((experts, count), F32)
    weight = jnp.zeros((experts, count), F32)
    for k in range(top):
        hit += jnp.where(named[k:k + 1] == ids, 1.0, 0.0)
        weight += jnp.where(named[k:k + 1] == ids, weights[k:k + 1], 0.0)
    before, after = lax.broadcasted_iota(jnp.int32, (count, count), 0), lax.broadcasted_iota(jnp.int32, (count, count), 1)
    earlier = jnp.where((before < after) & (before // block == after // block), 1.0, 0.0).astype(BF)
    slot = jnp.dot(hit.astype(BF), earlier, preferred_element_type=F32)
    lane = lax.broadcasted_iota(jnp.int32, (nz, count), 1) // block
    inside = jnp.where(lane == lax.broadcasted_iota(jnp.int32, (nz, count), 0), 1.0, 0.0)
    rows = column[...].reshape(count, half)
    for s in range(cap):
        chosen = jnp.where(slot == float(s), hit, 0.0)
        placing = (chosen[:, None, :] * inside[None]).reshape(experts * nz, count).astype(BF)
        value = jnp.dot(placing, rows, preferred_element_type=F32).astype(BF)
        outgoing[:, s * nz:(s + 1) * nz, :] = value.reshape(experts, nz, half)
        chosen = jnp.where(slot == float(s), weight, 0.0)
        weighted[s] = (chosen[:, None, :] * inside[None]).reshape(experts * nz, count)


def weigh_rows(nz, cap, weighted, back, teacher, blk):
    experts, half = back.shape[0], back.shape[2]
    count = weighted.shape[2]
    total = jnp.zeros((count, half), F32)
    for s in range(cap):
        rows = back[:, s * nz:(s + 1) * nz, :].reshape(experts * nz, half)
        value = weighted[s]
        high = value.astype(BF)
        low = (value - high.astype(F32)).astype(BF)
        for term in (high, low):
            total += lax.dot_general(term, rows, (((0,), (0,)), ((), ())), preferred_element_type=F32)
    lanes = -(-blk // 128) * 128
    empty = jnp.zeros((count, lanes - blk), F32)
    for b in range(half // blk):
        piece = jnp.concatenate([total[:, b * blk:(b + 1) * blk], empty], axis=1).astype(BF)
        teacher[:, :, b * lanes:(b + 1) * lanes] = piece.reshape(nz, count // nz, lanes)


def front_kernel(nz, cap, blk, parts, meta, own_tokens, inner, outer, hidden, down_both, teacher,
                 student, student_down, mine, plane, metas, weighted, back, w_in, w_out, column, outgoing, got, act, part, other, total,
                 ws, wr, rs, rr, zs, zr, ms, mr, xs, xr, ys, yr, cs, cr, send, recv, fsend, frecv, csend, crecv, bsend, brecv, dsend, drecv, own):
    z, x, r, y = here()
    ny = lax.axis_size("col")
    steps = plane_steps(ny)[::-1]
    sibling = (z, x, 1 - r, y)
    up, down_z = ((z + 1) % nz, x, r, y), ((z + nz - 1) % nz, x, r, y)
    per = nz // 2
    loads = [pltpu.make_async_copy(inner, w_in, own.at[1]), pltpu.make_async_copy(outer, w_out, own.at[2])]
    for copy in loads:
        copy.start()
    peers = [(z, (x + dx) % NX, r, (y + dy) % ny) for dx, dy in steps]
    greet(peers + [sibling, up, down_z])
    started = []
    block, half = mine.shape
    mine[...] = own_tokens[pl.ds(pl.multiple_of(y * block, 8), block), lanes_at(r, half)]
    blocks = block_gather(nz, mine, meta, column, metas, zs, zr, ms, mr, own.at[pl.ds(3, 2)], started)
    tokens = token_gather(own_tokens, blk, plane, xs, xr, ys, yr, cs, cr, started)
    next(blocks)

    span = NX * 128
    exchange = [[], [], []]
    homes = [student.at[0], student.at[1], student_down]
    lane = lanes_at(x, 128)
    for kind in (0, 1, 2):
        for d in (2, 1, 3):
            to = (x + d) % NX
            copy = remote(parts.at[kind, to], homes[kind].at[z, :, lane], ws.at[d - 1, kind], wr.at[d - 1, kind], (z, to, r, y))
            copy.start()
            started.append(copy)
            exchange[kind].append(copy)
    local = [pltpu.make_async_copy(parts.at[k, x], homes[k].at[z, :, lane], own.at[5 + k]) for k in range(3)]
    for copy in local:
        copy.start()
    next(tokens)

    def chunk(d, p):
        return (d, slice(None), pl.ds(*p))

    rings = [{}, {}, {}]
    idle = 128 - blk
    riders = 2 * NX - 1
    packed = riders * idle == blk
    last = slice(span - 128, span)

    def spot(d, i):
        return i // NX, d, slice(None), slice(i % NX * 128, (i % NX + 1) * 128)

    def pack():
        value = student[1, z, :, last].astype(F32)
        for i in range(riders):
            kept = student[spot(z, i)].astype(F32)[:, :blk]
            student[spot(z, i)] = jnp.concatenate([kept, value[:, i * idle:(i + 1) * idle]], axis=1).astype(BF)

    def unpack():
        @pl.loop(0, nz)
        def _(d):
            pieces = [student[spot(d, i)].astype(F32)[:, blk:] for i in range(riders)]
            empty = jnp.zeros((student.shape[2], idle), F32)
            student[1, d, :, last] = jnp.concatenate(pieces + [empty], axis=1).astype(BF)

    sizes = [span, span - 128 if packed else span, span]
    gathers = [
        ring_gather(nz, z, up, down_z, homes[kind], chunk, (0, sizes[kind]), (0, span // 2), (span // 2, sizes[kind] - span // 2),
                    rs.at[kind], rr.at[kind], rings[kind])
        for kind in range(3)
    ]

    def serve(*kinds):
        for kind in kinds:
            next(gathers[kind], None)

    for _ in range(per - 2):
        next(blocks)
    for kind in range(3):
        local[kind].wait()
        for copy in exchange[kind]:
            copy.wait_recv()
        if kind == 1:
            if packed:
                pack()
            serve(0, 1)
        if kind == 0:
            next(blocks)
    next(tokens)
    next(blocks, None)

    place_rows(nz, cap, column, metas, outgoing, weighted)
    steps = [(0, 0)] + steps
    me = x * ny + y
    keep, give = lanes_at(r, half), lanes_at(1 - r, half)
    near = len(steps) // 2
    groups = (range(near), range(near, len(steps)))
    sends, forwards, swaps, returns = {}, {}, {}, []

    def forward(k, src):
        forwards[k] = remote(src, got.at[k, :, keep], fsend.at[k], frecv.at[k], sibling)
        forwards[k].start()

    for k, (dx, dy) in enumerate(steps):
        if k:
            tx, ty = (x + dx) % NX, (y + dy) % ny
            sends[k] = remote(outgoing.at[tx * ny + ty], got.at[k, :, keep], send.at[k], recv.at[k], (z, tx, r, ty))
            sends[k].start()
    own_rows = pltpu.make_async_copy(outgoing.at[me], got.at[0, :, keep], own.at[0])
    own_rows.start()
    forward(0, outgoing.at[me])
    serve(0, 1)

    def finish(g):
        swaps[g].wait_recv()
        for k in groups[g]:
            dx, dy = steps[k]
            tx, ty = (x + NX - dx) % NX, (y + ny - dy) % ny
            value = (part[k, :, keep].astype(F32) + other[k].astype(F32)).astype(BF)
            if k:
                total[k] = value
                returns.append(remote(total.at[k], back.at[me], bsend.at[k], brecv.at[k], (z, tx, r, ty)))
                returns[-1].start()
            else:
                back[me] = value

    for g, group in enumerate(groups):
        slots = pl.ds(group[0], near)
        for k in group:
            if k:
                sends[k].wait_recv()
                forward(k, got.at[k, :, keep])
        if g == 0:
            own_rows.wait()
            loads[0].wait()
        for k in group:
            forwards[k].wait_recv()
        rows = near * outgoing.shape[1]
        tile = w_in.shape[2] // 2

        @pl.loop(0, 2)
        def _(j):
            lhs = got[slots].reshape(rows, got.shape[2])
            cut = pl.ds(pl.multiple_of(j * tile, tile), tile)
            gate = jnp.dot(lhs, w_in[0, :, cut], preferred_element_type=F32)
            up_part = jnp.dot(lhs, w_in[1, :, cut], preferred_element_type=F32)
            act[:, cut] = (gate / (1.0 + jnp.exp(-gate)) * up_part).astype(BF)

        if g == 0:
            loads[1].wait()
        wide = half // 2

        def down(side):
            @pl.loop(0, 2)
            def _(j):
                cut = pl.ds(pl.multiple_of(side * half + j * wide, wide), wide)
                value = jnp.dot(act[...], w_out[:, cut], preferred_element_type=F32).astype(BF)
                part[slots, :, cut] = value.reshape(near, outgoing.shape[1], wide)

        down(1 - r)
        swaps[g] = remote(part.at[slots, :, give], other.at[slots], csend.at[g], crecv.at[g], sibling)
        swaps[g].start()
        down(r)
        if g == 0:
            serve(0, 1, 2)
        finish(g)
        if g == 1:
            serve(0, 1, 2)
        next(tokens, None)

    serve(0, 1, 2)
    if packed:
        unpack()
    tok = plane.shape[1]

    def units(kind, i):
        total = jnp.zeros((2 * tok, student.shape[2]), F32)
        for d in range(nz):
            rows = plane[2 * i:2 * i + 2, :, d * span:(d + 1) * span].reshape(2 * tok, span)
            total += lax.dot_general(rows, student[kind, d], (((1,), (1,)), ((), ())), preferred_element_type=F32)
        return total

    for i in range(NX // 2):
        gate = units(0, i)
        hidden[r, 2 * i * tok:2 * (i + 1) * tok] = (gate / (1.0 + jnp.exp(-gate)) * units(1, i)).astype(BF)
        if i == 0:
            serve(2)
    for copy in returns:
        copy.wait_recv()
    local = []
    changes = [remote(hidden.at[r], hidden.at[r], dsend.at[per], drecv.at[per], sibling)]
    changes[0].start()
    for i in (1, 2, 3, 0):
        if i == 0:
            weigh_rows(nz, cap, weighted, back, teacher, blk)
            serve(2)
        q = (z + i) % per
        src = student_down.at[(1 - r) * per + q]
        changes.append(remote(src, down_both.at[r, q], dsend.at[i], drecv.at[i], sibling))
        changes[-1].start()
        local.append(pltpu.make_async_copy(student_down.at[r * per + q], down_both.at[r, q], own.at[5 + i]))
        local[-1].start()
    for copy in local + changes:
        copy.wait()
    for copy in started + returns + list(sends.values()) + list(forwards.values()) + list(swaps.values()):
        copy.wait_send()
    for ring in rings:
        for copy in ring.values():
            copy.wait_send()


def ring_sum(n, i, up, down, ref, where, subs, came, leave, send, recv, copies, done=None):
    half = n // 2

    def go(way, s, u, src, dst):
        copy = remote(src, dst, send.at[way, s, u], recv.at[way, s, u], (up, down)[way])
        copy.start()
        copies[way, s, u] = copy

    for u, (whole, low, top) in enumerate(subs):
        for way, part in ((0, low), (1, top)):
            go(way, 0, u, ref.at[where((i + half) % n, part)], came.at[(way, 0) + part])
    yield
    for s in range(1, half):
        for u, (whole, low, top) in enumerate(subs):
            for way in (0, 1):
                d = (i + half - s) % n if way == 0 else (i + half + s) % n
                copies[way, s - 1, u].wait_recv()
                summed, plain = whole, None
                if s == 1:
                    summed, plain = (low, top) if way == 0 else (top, low)
                    leave[(way, 0) + plain] = ref[where(d, plain)]
                value = ref[where(d, summed)].astype(F32) + came[(way, s - 1) + summed].astype(F32)
                leave[(way, s - 1) + summed] = value.astype(BF)
                go(way, s, u, leave.at[(way, s - 1) + whole], came.at[(way, s) + whole])
        yield
    for u in range(len(subs)):
        for way in (0, 1):
            copies[way, half - 1, u].wait_recv()
        if done:
            done(u)


def ring_gather(n, i, up, down, ref, where, whole, low, top, send, recv, copies):
    half = n // 2
    for s in range(half):
        for way, device in ((0, up), (1, down)):
            d = (i + n - s) % n if way == 0 else (i + s) % n
            if s:
                copies[way, s - 1].wait_recv()
            part = whole if s < half - 1 else (low, top)[way]
            piece = ref.at[where(d, part)]
            copies[way, s] = remote(piece, piece, send.at[way, s, 0], recv.at[way, s, 0], device)
            copies[way, s].start()
        yield
    for way in (0, 1):
        copies[way, half - 1].wait_recv()


def together(*rings):
    rings = list(rings)
    while rings:
        for ring in list(rings):
            try:
                next(ring)
            except StopIteration:
                rings.remove(ring)


def tail_kernel(nz, count, tok, hid, weights, teacher, grad, losses, w_out, tcame, tleave, chunks, give, came, leave, total, loss,
                send, recv, zsend, zrecv, csend, crecv, xsend, xrecv, lsend, lrecv, own, *buffers):
    z, x, r, y = here()
    ny = lax.axis_size("col")
    up, down = ((z + 1) % nz, x, r, y), ((z + nz - 1) % nz, x, r, y)
    east, west = (z, (x + 1) % NX, r, y), (z, (x + NX - 1) % NX, r, y)
    north, south = (z, x, r, (y + 1) % ny), (z, x, r, (y + ny - 1) % ny)
    sibling = (z, x, 1 - r, y)
    mates = [(z, x, r, (y + d) % ny) for d in range(1, ny)] + [(z, x, 1 - r, (y + d) % ny) for d in range(ny)]
    across = [(d, (x + d) % NX) for d in (2, 1, 3)]
    load = pltpu.make_async_copy(weights, w_out, own.at[0])
    load.start()
    greet([up, down] + mates + [(z, tx, r, y) for _, tx in across])
    span = teacher.shape[2]
    wing = span // count
    per = nz // 2
    every = slice(None)
    copies = [{} for _ in range(4 * count + 1)]
    loss[...] = jnp.zeros_like(loss)

    def sems(k):
        return send.at[k], recv.at[k], copies[k]

    def trio(axis_size):
        return (pl.ds(0, axis_size),), (pl.ds(0, axis_size // 2),), (pl.ds(axis_size // 2, axis_size // 2),)

    def lanes(size):
        return tuple((every, pl.ds(o, s)) for o, s in ((0, size), (0, size // 2), (size // 2, size // 2)))

    along_x, along_y = (NX, x, east, west), (ny, y, north, south)
    swaps = []

    def flow(f):
        cut = pl.ds(f * wing, wing)
        parts, gaps, scame, sleave, mid, came2, leave2 = buffers[7 * f:7 * f + 7]
        x_first = f < count // 2
        one, two = (along_x, along_y) if x_first else (along_y, along_x)

        def outer(d, p):
            return (d,) + p if x_first else p + (d,)

        def inner(d, p):
            return (x, d) + p if x_first else (d, y) + p

        @pl.loop(0, NX)
        def _(i):
            rows = pl.ds(pl.multiple_of(i * tok, tok), tok)
            value = jnp.dot(hid[0, rows], w_out[0, f], preferred_element_type=F32)
            value += jnp.dot(hid[1, rows], w_out[1, f], preferred_element_type=F32)
            parts[i] = value.astype(BF).reshape(parts.shape[1:])

        yield from ring_sum(*one, parts, outer, [trio(two[0])], scame, sleave, *sems(4 * f))
        last = one[0] // 2 - 1
        kept = parts[x] if x_first else parts[:, y]
        mid[...] = (kept.astype(F32) + scame[0, last].astype(F32) + scame[1, last].astype(F32)).astype(BF)
        yield from ring_sum(*two, mid, lambda d, p: (d,) + p, [lanes(wing)], came2, leave2, *sems(4 * f + 1))
        last = two[0] // 2 - 1
        student = mid[two[1]].astype(F32) + came2[0, last].astype(F32) + came2[1, last].astype(F32)
        taught = teacher[z, :, cut].astype(F32) + tcame[0, per - 1, :, cut].astype(F32) + tcame[1, per - 1, :, cut].astype(F32)
        gap = student - taught
        gaps[x, y] = gap.astype(BF)
        square = gap * gap
        loss[...] += sum(square[:, t * 128:(t + 1) * 128] for t in range(wing // 128))
        yield from ring_gather(*two, gaps, inner, *lanes(wing), *sems(4 * f + 2))
        yield from ring_gather(*one, gaps, outer, *trio(two[0]), *sems(4 * f + 3))
        whole = gaps[...].reshape(NX * tok, wing)

        def term(core):
            value = lax.dot_general(hid[core], whole, (((0,), (0,)), ((), ())), preferred_element_type=F32)
            return (value / tok).astype(BF)

        give[f] = term(1 - r)
        slot = r * per + f
        swaps.append(remote(give.at[f], chunks.at[slot], csend.at[f], crecv.at[f], sibling))
        swaps[-1].start()
        chunks[slot] = term(r)

    teach = ring_sum(nz, z, up, down, teacher, lambda d, p: (d,) + p, [lanes(span)], tcame, tleave, *sems(4 * count))
    next(teach)
    load.wait()
    half = count // 2
    flows = [flow(k) for pair in zip(range(half), range(half, count)) for k in pair]
    for one in flows:
        next(one)
    together(teach, *flows)
    place = r * ny + y
    tells = [remote(loss, losses.at[place], lsend.at[k], lrecv.at[k], device) for k, device in enumerate(mates)]
    keep_loss = pltpu.make_async_copy(loss, losses.at[place], own.at[2])
    for copy in tells + [keep_loss]:
        copy.start()
    for copy in swaps:
        copy.wait_recv()
    rows, span = chunks.shape[1], chunks.shape[2]
    subs = []
    for u in range(6):
        band = pl.ds(u * (rows // 6), rows // 6)
        subs.append(((band, pl.ds(0, span)), (band, pl.ds(0, span // 2)), (band, pl.ds(span // 2, span // 2))))
    ring = {}
    size = span // NX
    outs = []

    def spread(u):
        band = subs[u][0][0]
        value = chunks[z, band].astype(F32) + came[0, per - 1, band].astype(F32) + came[1, per - 1, band].astype(F32)
        total[band] = value.astype(BF)
        for d, tx in across:
            copy = remote(total.at[band, lanes_at(tx, size)], grad.at[x, band], xsend.at[d - 1, u], xrecv.at[d - 1, u], (z, tx, r, y))
            copy.start()
            outs.append(copy)
        copy = pltpu.make_async_copy(total.at[band, lanes_at(x, size)], grad.at[x, band], own.at[3 + u])
        copy.start()
        outs.append(copy)

    together(ring_sum(nz, z, up, down, chunks, lambda d, p: (d,) + p, subs, came, leave, zsend, zrecv, ring, spread))
    for copy in [keep_loss] + outs + tells:
        copy.wait()
    for copy in swaps + list(ring.values()) + [c for group in copies for c in group.values()]:
        copy.wait_send()


def on_device(tokens, routes, route_weights, teacher_in, teacher_out, student_in, student_out):
    nz, nr, ny = lax.axis_size("z"), lax.axis_size("row"), lax.axis_size("col")
    z, x, r, y = here()
    tok, width = tokens.shape
    block, top = routes.shape
    blk = student_in.shape[1]
    ff = student_in.shape[2]
    sub = ff // NX
    half = width // nr
    experts = NX * ny
    cap = max(2, 3 * block * top // (2 * nz * experts))
    blocks = nz * NX
    shape = jax.ShapeDtypeStruct

    parts = jnp.concatenate([jnp.swapaxes(student_in, 1, 2), student_out[None]], axis=0)
    parts = pad_lanes(parts)
    lanes = parts.shape[-1]
    wide = blocks * lanes
    steps = nz // 2
    slots = nz * cap
    hid = teacher_in.shape[3]
    meta = jnp.concatenate([routes.astype(F32), route_weights], axis=1).T
    meta = jnp.pad(meta, ((0, 0), (0, 128 - block)))
    whole, far = pl.BlockSpec(memory_space=pltpu.VMEM), pl.BlockSpec(memory_space=pl.ANY)
    bf, f32 = (lambda *b: pltpu.VMEM(b, BF)), (lambda *b: pltpu.VMEM(b, F32))
    buffers = [bf(2, nz, sub, NX * lanes), bf(nz, sub, NX * lanes), bf(block, half), bf(NX, tok, wide), f32(nz, 2 * top, 128), f32(cap, experts * nz, nz * block), bf(experts, slots, half)]
    buffers += [bf(2, width, hid), bf(hid, width), bf(nz, block, half), bf(experts, slots, half), bf(experts, slots, width)]
    buffers += [bf(experts // 2 * slots, hid), bf(experts, slots, width)] + [bf(experts, slots, half)] * 2
    sems = [(3, 3)] * 2 + [(3, 2, steps, 1)] * 2 + [(2, steps)] * 4 + [(3,)] * 2 + [(2, 3)] * 2 + [(3, 3)] * 2
    sems += [(experts,)] * 4 + [(2,)] * 2 + [(experts,)] * 2 + [(steps + 1,)] * 2 + [(9,)]
    hidden, student_down, teacher = kernel_call(
        functools.partial(front_kernel, nz, cap, blk), 0,
        [shape((nr, NX * tok, sub), BF), shape((nr, steps, sub, NX * lanes), BF), shape((nz, block, wide // nr), BF)],
        buffers + [dma(*b) for b in sems],
        parts.reshape(3, NX, sub, lanes), meta, tokens, teacher_in[0], teacher_out[0],
        specs=[whole, whole, whole, far, far],
    )

    span = wide // nr
    count = steps
    wing = span // count
    chunk = NX * lanes
    flows = []
    for f in range(count):
        one, two = (NX, ny) if f < count // 2 else (ny, NX)
        flows += [(NX, ny, block, wing)] * 2
        flows += [(2, one // 2, two, block, wing), (2, one // 2 - 1, two, block, wing), (two, block, wing)]
        flows += [(2, two // 2, block, wing), (2, two // 2 - 1, block, wing)]
    buffers = [(nr, steps, sub, chunk), (2, steps, block, span), (2, steps - 1, block, span), (nz, sub, chunk), (steps, sub, chunk)]
    buffers += [(2, steps, sub, chunk), (2, steps - 1, sub, chunk), (sub, chunk)]
    grad, losses = kernel_call(
        functools.partial(tail_kernel, nz, count, tok), 4,
        [shape((NX, sub, lanes), BF), shape((nr * ny, block, 128), F32)],
        [pltpu.VMEM(b, BF) for b in buffers] + [pltpu.VMEM((block, 128), F32)]
        + [dma(4 * count + 1, 2, steps, 1)] * 2 + [dma(2, steps, 6)] * 2 + [dma(steps)] * 2 + [dma(3, 6)] * 2
        + [dma(2 * ny - 1)] * 2 + [dma(9)]
        + [pltpu.VMEM(b, BF) for b in flows],
        hidden, student_down, teacher,
        specs=[whole, far, whole],
    )
    token_loss = jnp.sum(losses.reshape(nr, ny * block, 128), axis=(0, 2)) / width
    grad = grad.reshape(ff, lanes)[:, :blk].astype(F32)
    return token_loss, grad


def solution(mesh):
    dp = ("z", "x")
    in_specs = (
        P(dp, None),
        P(dp + ("col",), None),
        P(dp + ("col",), None),
        P(dp + ("col",), None, None, "row"),
        P(dp + ("col",), "row", None),
        P(None, dp, ("row", "col")),
        P(("row", "col"), dp),
    )
    out_specs = (P(dp), P(("row", "col"), dp))
    return jax.shard_map(
        on_device, mesh=split_mesh(mesh), in_specs=in_specs, out_specs=out_specs, check_vma=False
    )
```
